32 devices in a mesh: batch: 8 (over z, x), mp: 4 (over y, core).
Axes of the slice: x: 2, y: 2, z: 4, core: 2. Of those that a mesh axis runs over, the one named last changes fastest.
Arguments:
- block_input: bfloat16 [16384, 768], P('batch'), may hold values from -6 to 6
- first_values: bfloat16 [16384, 384], P('batch'), may hold values from -6 to 6
- norm1_gain: float32 [768], replicated, may hold values from 0.5 to 1.5
- norm1_bias: float32 [768], replicated, may hold values from -1 to 1
- query_weight: bfloat16 [768, 768], P(None, 'mp'), may hold values from -0.21875 to 0.21875
- key_weight: bfloat16 [768, 768], P(None, 'mp'), may hold values from -0.21875 to 0.21875
- value_weight: bfloat16 [768, 384], replicated, may hold values from -0.21875 to 0.21875
- out_weight: bfloat16 [768, 768], P('mp'), may hold values from -0.875 to 0.875
- norm2_gain: float32 [768], replicated, may hold values from 0.5 to 1.5
- norm2_bias: float32 [768], replicated, may hold values from -1 to 1
- up_weight: bfloat16 [768, 3072], P(None, 'mp'), may hold values from -0.21875 to 0.21875
- down_weight: bfloat16 [3072, 768], P('mp'), may hold values from -0.109375 to 0.109375
- out_grad: bfloat16 [16384, 768], P('batch'), may hold values from -6 to 6
- doc_lengths: int32 [8, 8], P('batch'), may hold values from 0 to 1024, as said below
Outputs:
- block_out: float32 [16384, 768], P('batch')
- input_grad: float32 [16384, 768], P('batch')
- first_values_grad: float32 [16384, 384], P('batch')
- norm1_gain_grad: float32 [768], replicated
- norm1_bias_grad: float32 [768], replicated
- query_weight_grad: float32 [768, 768], P(None, 'mp')
- key_weight_grad: float32 [768, 768], P(None, 'mp')
- value_weight_grad: float32 [768, 384], replicated
- out_weight_grad: float32 [768, 768], P('mp')
- norm2_gain_grad: float32 [768], replicated
- norm2_bias_grad: float32 [768], replicated
- up_weight_grad: float32 [768, 3072], P(None, 'mp')
- down_weight_grad: float32 [3072, 768], P('mp')
The draws below stay inside these ranges and needn't reach their ends.
Inputs may be any that keep to these rules, and one draw needn't show every extreme that they name: `doc_lengths`: each row lists the lengths of the documents packed into one row of 2048 token slots, in order; a row's lengths sum to 2048, slots of length 0 hold no document and may stand anywhere in the row, and no document crosses a multiple of min(2048, 1024) slots. Some row holds documents of exactly min(2048, 1024) tokens.
All inputs are finite; a program needn't handle non-finite values.
Results may differ from the reference program's by a relative error of at most 0.019.
Values may be sent and summed in bfloat16 or wider, within the bound.
A program may use at most 192 MiB of HBM per device.

```python
import jax
import jax.numpy as jnp
from jax import lax

D = 768
FF = 3072
HEADS = 12
HEAD = 64
TOK_DEV = 2048
CONTEXT = 1024
DOCS = 8
TOKENS = 16384
N_BATCH = 8
N_MP = 4


def draw_doc_lengths(key, part):
    key = jax.random.fold_in(key, 11)
    span = min(TOK_DEV, CONTEXT)
    segments = TOK_DEV // span
    per_segment = DOCS // segments
    source_key, weight_key, forced_key = jax.random.split(key, 3)
    source = jax.random.randint(source_key, (N_BATCH,), 0, 3)
    forced = jax.random.randint(forced_key, (), 0, N_BATCH)
    source = jnp.where(jnp.arange(N_BATCH) == forced, 2, source)
    counts = jnp.where(source == 0, per_segment, jnp.where(source == 1, max(per_segment // 2, 1), 1))
    weights = jax.random.randint(weight_key, (N_BATCH, segments, per_segment), 1, 9)
    slots = jnp.arange(per_segment)[None, None, :]
    weights = jnp.where(slots < counts[:, None, None], weights, 0)
    doc_ends = span * jnp.cumsum(weights, axis=2) // jnp.sum(weights, axis=2, keepdims=True)
    starts = jnp.concatenate([jnp.zeros((N_BATCH, segments, 1), doc_ends.dtype), doc_ends[:, :, :-1]], axis=2)
    lengths = (doc_ends - starts).reshape(N_BATCH, segments * per_segment)
    padding = jnp.zeros((N_BATCH, DOCS - segments * per_segment), lengths.dtype)
    return jnp.concatenate([lengths, padding], axis=1).astype(jnp.int32)


def levels(rng, extent, shards, smallest, high):
    factor_of = 1.0
    for dim, parts in shards:
        steps = jax.random.uniform(jax.random.fold_in(jax.random.fold_in(rng, 6), dim), (parts,), jnp.float32, smallest / len(shards), high / len(shards))
        factor_of = factor_of * jnp.repeat(jnp.exp(steps), extent[dim] // parts).reshape((-1,) + (1,) * (len(extent) - 1 - dim))
    return factor_of


def gaussian(rng, shape, scale, bound, shards=(), kind=jnp.bfloat16):
    result = scale * jax.random.normal(rng, shape, jnp.float32)
    if shards:
        result = result * levels(rng, shape, shards, -0.22, 0.18)
    return jnp.clip(result, -bound, bound).astype(kind)


def setup_inputs(seed: int = 0) -> dict:
    keys = jax.random.split(jax.random.key(seed), 15)
    block_input = gaussian(keys[0], (TOKENS, D), 1.0, 6.0, ((0, 8),))
    first_values = gaussian(keys[1], (TOKENS, D // 2), 1.0, 6.0, ((0, 8),))
    norm1_gain = jnp.clip(1.0 + 0.1 * jax.random.normal(keys[2], (D,), jnp.float32), 0.5, 1.5)
    norm1_bias = gaussian(keys[3], (D,), 0.2, 1.0, (), jnp.float32)
    query_weight = gaussian(keys[4], (D, D), D ** -0.5, 0.21875, ((1, 4),))
    key_weight = gaussian(keys[5], (D, D), D ** -0.5, 0.21875, ((1, 4),))
    value_weight = gaussian(keys[6], (D, D // 2), D ** -0.5, 0.21875)
    out_weight = gaussian(keys[7], (D, D), (D // 16) ** -0.5, 0.875, ((0, 4),))
    norm2_gain = jnp.clip(1.0 + 0.1 * jax.random.normal(keys[8], (D,), jnp.float32), 0.5, 1.5)
    norm2_bias = gaussian(keys[9], (D,), 0.2, 1.0, (), jnp.float32)
    up_weight = gaussian(keys[10], (D, FF), D ** -0.5, 0.21875, ((1, 4),))
    down_weight = gaussian(keys[11], (FF, D), FF ** -0.5, 0.109375, ((0, 4),))
    out_grad = gaussian(keys[12], (TOKENS, D), 1.0, 6.0, ((0, 8),))
    doc_lengths = draw_doc_lengths(jax.random.fold_in(keys[14], 71), 0)
    return {"block_input": block_input, "first_values": first_values, "norm1_gain": norm1_gain, "norm1_bias": norm1_bias, "query_weight": query_weight, "key_weight": key_weight, "value_weight": value_weight, "out_weight": out_weight, "norm2_gain": norm2_gain, "norm2_bias": norm2_bias, "up_weight": up_weight, "down_weight": down_weight, "out_grad": out_grad, "doc_lengths": doc_lengths}


@jax.custom_vjp
def low(v):
    return lax.optimization_barrier(v.astype(jnp.bfloat16)).astype(jnp.float32)

@jax.custom_vjp
def low_back(v):
    return v

def low_keep(v):
    return (low(v), None)

def low_pass(kept, grad):
    return (grad,)

def back_keep(v):
    return (v, None)

def back_low(kept, grad):
    return (low(grad),)
low.defvjp(low_keep, low_pass)
low_back.defvjp(back_keep, back_low)
EPS = 1e-05
MASKED = -1e+30
HIGH = lax.Precision.HIGHEST

def layer_norm(values, gain, bias):
    average = lax.optimization_barrier(jnp.mean(values, axis=-1, keepdims=True))
    centred = values - average
    variance = lax.optimization_barrier(jnp.mean(centred * centred, axis=-1, keepdims=True))
    return centred * lax.rsqrt(variance + EPS) * gain + bias

def matmul(left, right):
    return jnp.dot(left, right, precision=HIGH, preferred_element_type=jnp.float32)

def doc_numbers(lengths):
    doc_ends = jnp.cumsum(lengths)
    position = jnp.arange(TOK_DEV, dtype=jnp.int32)
    return lax.optimization_barrier(jnp.sum((position[:, None] >= doc_ends[None, :]).astype(jnp.int32), axis=1))

def attend(packed):
    queries, keys_in, values, numbers = packed
    query_heads = queries.reshape(TOK_DEV, HEADS, HEAD)
    key_heads = keys_in.reshape(TOK_DEV, HEADS, HEAD)
    value_heads = values.reshape(TOK_DEV, HEADS, HEAD)
    scores = jnp.einsum('qhd,khd->hqk', query_heads, key_heads, precision=HIGH) * HEAD ** (-0.5)
    scores = low_back(scores)
    position = jnp.arange(TOK_DEV, dtype=jnp.int32)
    visible = (numbers[:, None] == numbers[None, :]) & (position[:, None] >= position[None, :])
    scores = jnp.where(visible[None], scores, MASKED)
    highest = lax.optimization_barrier(jnp.max(scores, axis=-1, keepdims=True))
    weights = jnp.exp(scores - highest)
    weights = low(weights / lax.optimization_barrier(jnp.sum(weights, axis=-1, keepdims=True)))
    mixed = jnp.einsum('hqk,khd->qhd', weights, value_heads, precision=HIGH)
    return mixed.reshape(TOK_DEV, D)

def make_forward(numbers):

    def forward(inputs, first_in, gain1, bias1, query_w, key_w, value_w, out_w, gain2, bias2, up_w, down_w):
        normed1 = low(layer_norm(inputs, gain1, bias1))
        queries = low_back(low(matmul(normed1, query_w)))
        keys_in = low_back(low(matmul(normed1, key_w)))
        fresh = low_back(low(matmul(normed1, value_w)))
        values = jnp.concatenate([fresh, first_in], axis=1)
        shaped = (queries.reshape(N_BATCH, TOK_DEV, D), keys_in.reshape(N_BATCH, TOK_DEV, D), values.reshape(N_BATCH, TOK_DEV, D), numbers)
        mixed = lax.map(jax.checkpoint(attend), shaped).reshape(N_BATCH * TOK_DEV, D)
        mixed = low_back(low(mixed))
        group_width = D // N_MP
        attention = jnp.zeros((N_BATCH * TOK_DEV, D), jnp.float32)
        for member in range(N_MP):
            lower = member * group_width
            attention = attention + low(matmul(mixed[:, lower:lower + group_width], out_w[lower:lower + group_width]))
        attention = low_back(attention)
        hidden = inputs + attention
        normed2 = low(layer_norm(hidden, gain2, bias2))
        up_proj = low_back(matmul(normed2, up_w))
        activated = low(jax.nn.gelu(up_proj, approximate=True))
        unit_width = FF // N_MP
        feed = jnp.zeros((N_BATCH * TOK_DEV, D), jnp.float32)
        for member in range(N_MP):
            lower = member * unit_width
            feed = feed + low(matmul(activated[:, lower:lower + unit_width], down_w[lower:lower + unit_width]))
        feed = low_back(feed)
        return hidden + feed
    return forward

def reference(block_input, first_values, norm1_gain, norm1_bias, query_weight, key_weight, value_weight, out_weight, norm2_gain, norm2_bias, up_weight, down_weight, out_grad, doc_lengths):
    numbers = jax.vmap(doc_numbers)(doc_lengths)
    forward = make_forward(numbers)
    primals = (block_input.astype(jnp.float32), first_values.astype(jnp.float32), norm1_gain, norm1_bias, query_weight.astype(jnp.float32), key_weight.astype(jnp.float32), value_weight.astype(jnp.float32), out_weight.astype(jnp.float32), norm2_gain, norm2_bias, up_weight.astype(jnp.float32), down_weight.astype(jnp.float32))
    block_out, pullback = jax.vjp(forward, *primals)
    grads = pullback(out_grad.astype(jnp.float32))
    return (block_out, grads[0], grads[1], grads[2], grads[3], grads[4], grads[5], grads[6], grads[7], grads[8], grads[9], grads[10], grads[11])
```

```python
import functools

import jax
import jax.numpy as jnp
from jax import lax
from jax.experimental import pallas as pl
from jax.experimental.pallas import tpu as pltpu
from jax.sharding import PartitionSpec as P

HEAD = 64
CONTEXT = 1024
EPS = 1e-05
MASKED = -1e30
QROWS = 256
SCALE = HEAD ** (-0.5)
GELU_C = 0.7978845608028654
GELU_A = 0.044715

F32 = jnp.float32
BF16 = jnp.bfloat16
VMEM_LIMIT = 56 * 1024 * 1024

NN = (((1,), (0,)), ((), ()))
NT = (((1,), (1,)), ((), ()))
TN = (((0,), (0,)), ((), ()))


def mm(left, right, dims=NN):
    return lax.dot_general(left, right, dims, preferred_element_type=F32)


def normalise(values):
    average = jnp.mean(values, axis=-1, keepdims=True)
    centred = values - average
    variance = jnp.mean(centred * centred, axis=-1, keepdims=True)
    inverse = lax.rsqrt(variance + EPS)
    return centred * inverse, inverse


def call(body, name, out_shape, in_specs, out_specs, args, scalars, flops, scratch=()):
    grid_spec = pltpu.PrefetchScalarGridSpec(
        num_scalar_prefetch=1,
        grid=(1,),
        in_specs=in_specs,
        out_specs=out_specs,
        scratch_shapes=list(scratch),
    )
    nbytes = sum(a.size * a.dtype.itemsize for a in args)
    nbytes += sum(o.size * o.dtype.itemsize for o in out_shape)
    return pl.pallas_call(
        body,
        grid_spec=grid_spec,
        out_shape=out_shape,
        name=name,
        cost_estimate=pl.CostEstimate(flops=flops, bytes_accessed=nbytes, transcendentals=0),
        compiler_params=pltpu.CompilerParams(vmem_limit_bytes=VMEM_LIMIT),
    )(scalars, *args)


def whole(shape):
    return pl.BlockSpec(shape, lambda i, s: (0,) * len(shape))


def sds(shape, dtype):
    return jax.ShapeDtypeStruct(shape, dtype)


def fill_bias(s_ref, bias_ref, seg, docs):
    base = s_ref[0] * seg
    for block in range(seg // QROWS):
        low, keys = block * QROWS, (block + 1) * QROWS
        row = lax.broadcasted_iota(jnp.int32, (QROWS, 1), 0) + low
        start = jnp.zeros((QROWS, 1), jnp.int32)
        end = jnp.int32(0)
        for doc in range(docs):
            end = end + s_ref[2 + doc]
            rel = end - base
            start = jnp.maximum(start, jnp.where(rel <= row, rel, 0))
        col = lax.broadcasted_iota(jnp.int32, (QROWS, keys), 1)
        seen = (col >= start) & (col <= row)
        bias_ref[low:keys, :keys] = jnp.where(seen, 0.0, MASKED)


def head_parts(width):
    parts = []
    for head in range(width // HEAD):
        pair = head // 2 * 2 * HEAD
        if pair + 2 * HEAD <= width:
            parts.append((pair, pair + 2 * HEAD, head % 2))
        else:
            parts.append((pair, pair + HEAD, None))
    return parts


def pick(values, half):
    if half is None:
        return values
    lane = lax.broadcasted_iota(jnp.int32, values.shape, 1)
    keep = (lane < HEAD) if half == 0 else (lane >= HEAD)
    return jnp.where(keep, values, jnp.zeros_like(values))


def attention_forward(bias_ref, q_ref, k_ref, v_ref, mixed_ref, lse_ref, seg, width):
    lane = lax.broadcasted_iota(jnp.int32, (QROWS, 2 * HEAD), 1)
    for block in range(seg // QROWS):
        low, keys = block * QROWS, (block + 1) * QROWS
        held = None
        stats = []
        for first, last, half in head_parts(width):
            query = pick(q_ref[low:keys, first:last], half) * jnp.asarray(SCALE, BF16)
            scores = mm(query, k_ref[:keys, first:last], NT) + bias_ref[low:keys, :keys]
            highest = jnp.max(scores, axis=-1, keepdims=True)
            weights = jnp.exp(scores - highest)
            total = jnp.sum(weights, axis=-1, keepdims=True)
            mixed = mm(weights.astype(BF16), v_ref[:keys, first:last]) / total
            stats.append(highest + jnp.log(total))
            if half == 0:
                held = mixed
            elif half == 1:
                both = jnp.where(lane < HEAD, held, mixed)
                mixed_ref[low:keys, first:last] = both.astype(BF16)
            else:
                mixed_ref[low:keys, first:last] = mixed.astype(BF16)
        for head, stat in enumerate(stats):
            lse_ref[low:keys, head : head + 1] = stat


def solution(mesh):
    batch_size = mesh.shape["batch"]
    assert mesh.shape["mp"] == 4

    def swap(values, bit):
        return lax.ppermute(values, "mp", [(i, i ^ bit) for i in range(4)])

    def shards(
        block_input,
        first_values,
        norm1_gain,
        norm1_bias,
        query_weight,
        key_weight,
        value_weight,
        out_weight,
        norm2_gain,
        norm2_bias,
        up_weight,
        down_weight,
        out_grad,
        doc_lengths,
    ):
        rows, width = block_input.shape
        cols = query_weight.shape[1]
        hid = up_weight.shape[1]
        half_width = value_weight.shape[1]
        docs = doc_lengths.shape[1]
        seg = rows // 2
        own = rows // 4
        assert seg == min(rows, CONTEXT)
        member = lax.axis_index("mp")
        y, c = member // 2, member % 2
        scalars = jnp.concatenate([jnp.stack([y, c]), doc_lengths[0]]).astype(jnp.int32)
        is_low = y == 0
        gain1, bias1 = norm1_gain.reshape(1, -1), norm1_bias.reshape(1, -1)
        gain2, bias2 = norm2_gain.reshape(1, -1), norm2_bias.reshape(1, -1)

        seg_rows = pl.BlockSpec((seg, width), lambda i, s: (s[0], 0))
        own_rows = pl.BlockSpec((own, width), lambda i, s: (2 * s[0] + s[1], 0))
        far_rows = pl.BlockSpec((own, width), lambda i, s: (2 * (1 - s[0]) + s[1], 0))

        pack = jnp.concatenate([query_weight, key_weight], axis=1)
        pack_far = swap(pack, 2)
        out_far = swap(out_weight, 2)
        up_sib = swap(up_weight, 1)
        down_sib = swap(down_weight, 1)
        query_far, key_far = pack_far[:, :cols], pack_far[:, cols:]

        def first_kernel(s, x, g, b, wq, wk, wv, fv, n1, q, k, vo, vf, mixed, lse, bias):
            fill_bias(s, bias, seg, docs)
            hat, _ = normalise(x[...].astype(F32))
            normed = (hat * g[...] + b[...]).astype(BF16)
            n1[...] = normed
            q[...] = mm(normed, wq[...]).astype(BF16)
            k[...] = mm(normed, wk[...]).astype(BF16)
            core = s[1] == 0
            value_cols = jnp.where(core, wv[:, :cols], wv[:, cols : 2 * cols])
            fresh = mm(normed, value_cols).astype(BF16)
            reused = jnp.where(core, fv[:, :cols], fv[:, cols : 2 * cols])
            low_chip = s[0] == 0
            vo[...] = jnp.where(low_chip, fresh, reused)
            vf[...] = jnp.where(low_chip, reused, fresh)
            attention_forward(bias, q, k, vo, mixed, lse, seg, cols)

        attn_flops = 2 * 2 * seg * seg * cols * 4
        n1, q_own, k_own, v_own, v_far, mixed_own, lse_own = call(
            first_kernel,
            "attn_own",
            [
                sds((seg, width), BF16),
                *[sds((seg, cols), BF16)] * 5,
                sds((seg, 2 * HEAD), F32),
            ],
            [
                seg_rows,
                whole((1, width)),
                whole((1, width)),
                whole((width, cols)),
                whole((width, cols)),
                whole((width, half_width)),
                pl.BlockSpec((seg, half_width), lambda i, s: (s[0], 0)),
            ],
            [whole((seg, width)), *[whole((seg, cols))] * 5, whole((seg, 2 * HEAD))],
            (block_input, gain1, bias1, query_weight, key_weight, value_weight, first_values),
            scalars,
            attn_flops * 2,
            [pltpu.VMEM((seg, seg), F32)],
        )

        def second_kernel(s, n1, wq, wk, v, q, k, mixed, lse, bias):
            fill_bias(s, bias, seg, docs)
            normed = n1[...]
            q[...] = mm(normed, wq[...]).astype(BF16)
            k[...] = mm(normed, wk[...]).astype(BF16)
            attention_forward(bias, q, k, v, mixed, lse, seg, cols)

        q_far, k_far, mixed_far, lse_far = call(
            second_kernel,
            "attn_far",
            [*[sds((seg, cols), BF16)] * 3, sds((seg, 2 * HEAD), F32)],
            [
                whole((seg, width)),
                whole((width, cols)),
                whole((width, cols)),
                whole((seg, cols)),
            ],
            [*[whole((seg, cols))] * 3, whole((seg, 2 * HEAD))],
            (n1, query_far, key_far, v_far),
            scalars,
            attn_flops * 2,
            [pltpu.VMEM((seg, seg), F32)],
        )

        def out_kernel(s, mo, mf, wo, wf, send, keep):
            def part(start):
                left = mm(mo[pl.ds(start, own), :], wo[...]).astype(BF16).astype(F32)
                right = mm(mf[pl.ds(start, own), :], wf[...]).astype(BF16).astype(F32)
                return (left + right).astype(BF16)

            core = s[1]
            send[...] = part(pl.multiple_of((1 - core) * own, own))
            keep[...] = part(pl.multiple_of(core * own, own))

        att_send, att_keep = call(
            out_kernel,
            "out_proj",
            [sds((own, width), BF16)] * 2,
            [*[whole((seg, cols))] * 2, *[whole((cols, width))] * 2],
            [whole((own, width))] * 2,
            (mixed_own, mixed_far, out_weight, out_far),
            scalars,
            2 * seg * 2 * cols * width,
        )
        att_recv = swap(att_send, 1)

        def norm2_kernel(s, x, keep, recv, g, b, hid_out, n2):
            hidden = x[...].astype(F32) + (keep[...].astype(F32) + recv[...].astype(F32))
            hid_out[...] = hidden
            hat, _ = normalise(hidden)
            n2[...] = (hat * g[...] + b[...]).astype(BF16)

        hidden, n2_own = call(
            norm2_kernel,
            "norm2",
            [sds((own, width), F32), sds((own, width), BF16)],
            [own_rows, whole((own, width)), whole((own, width)), whole((1, width)), whole((1, width))],
            [whole((own, width))] * 2,
            (block_input, att_keep, att_recv, gain2, bias2),
            scalars,
            own * width * 10,
        )
        n2_far = swap(n2_own, 2)

        def mlp_kernel(s, n2, og, wu0, wd0, wu1, wd1, act0, dup0, act1, dup1, dn2):
            left, grad = n2[...], og[...]
            total = jnp.zeros((own, width), F32)
            step = min(hid, 256)
            for wu, wd, act, dup in ((wu0, wd0, act0, dup0), (wu1, wd1, act1, dup1)):
                for tile in range(hid // step):
                    span = slice(tile * step, (tile + 1) * step)
                    up = mm(left, wu[:, span])
                    back = mm(grad, wd[span, :], NT)
                    square = up * up
                    slope = jnp.tanh(GELU_C * up * (1.0 + GELU_A * square))
                    bell = 0.5 * (1.0 + slope)
                    act[:, span] = (up * bell).astype(BF16)
                    inner = GELU_C * (1.0 + 3.0 * GELU_A * square)
                    deriv = bell + 0.5 * up * (1.0 - slope * slope) * inner
                    d_up = (back * deriv).astype(BF16)
                    dup[:, span] = d_up
                    total = total + mm(d_up, wu[:, span], NT)
            dn2[...] = total.astype(BF16)

        def mlp(n2, og_spec, name):
            return call(
                mlp_kernel,
                name,
                [*[sds((own, hid), BF16)] * 4, sds((own, width), BF16)],
                [
                    whole((own, width)),
                    og_spec,
                    *[whole((width, hid)), whole((hid, width))] * 2,
                ],
                [*[whole((own, hid))] * 4, whole((own, width))],
                (n2, out_grad, up_weight, down_weight, up_sib, down_sib),
                scalars,
                2 * 3 * own * width * 2 * hid,
            )

        act_oo, dup_oo, act_os, dup_os, dn2_own = mlp(n2_own, own_rows, "mlp_own")
        act_fo, dup_fo, act_fs, dup_fs, dn2_far = mlp(n2_far, far_rows, "mlp_far")
        dn2_recv = swap(dn2_far, 2)
        feed_far = (mm(act_fo, down_weight) + mm(act_fs, down_sib)).astype(BF16)
        feed_recv = swap(feed_far, 2)
        feed_own = mm(act_oo, down_weight) + mm(act_os, down_sib)

        def own_block(values):
            return lax.dynamic_slice_in_dim(values, (2 * y + c) * own, own, 0)

        def far_block(values):
            return lax.dynamic_slice_in_dim(values, (2 * (1 - y) + c) * own, own, 0)

        og_own, og_far = own_block(out_grad), far_block(out_grad)
        down_s = (mm(act_os, og_own, TN) + mm(act_fs, og_far, TN)).astype(BF16)
        up_s = (mm(n2_own, dup_os, TN) + mm(n2_far, dup_fs, TN)).astype(BF16)
        down_o = mm(act_oo, og_own, TN) + mm(act_fo, og_far, TN)
        up_o = mm(n2_own, dup_oo, TN) + mm(n2_far, dup_fo, TN)
        down_part = (down_o + swap(down_s, 1).astype(F32)).astype(BF16)
        up_part = (up_o + swap(up_s, 1).astype(F32)).astype(BF16)
        down_grad, up_grad = lax.psum((down_part, up_part), "batch")

        def norm2_back(s, h, keep, recv, og, g, dh_out, da, gg, gb):
            d_norm = keep[...].astype(F32) + recv[...].astype(F32)
            hat, inverse = normalise(h[...])
            gg[...] = jnp.sum(d_norm * hat, axis=0, keepdims=True)
            gb[...] = jnp.sum(d_norm, axis=0, keepdims=True)
            scaled = d_norm * g[...]
            mean1 = jnp.mean(scaled, axis=-1, keepdims=True)
            mean2 = jnp.mean(scaled * hat, axis=-1, keepdims=True)
            through = (scaled - mean1 - hat * mean2) * inverse
            dh_out[...] = through
            da[...] = (og[...].astype(F32) + through).astype(BF16)

        d_hidden, d_att_own, gain2_part, bias2_part = call(
            norm2_back,
            "norm2_back",
            [sds((own, width), F32), sds((own, width), BF16), *[sds((1, width), F32)] * 2],
            [
                whole((own, width)),
                whole((own, width)),
                whole((own, width)),
                own_rows,
                whole((1, width)),
            ],
            [whole((own, width)), whole((own, width)), whole((1, width)), whole((1, width))],
            (hidden, dn2_own, dn2_recv, out_grad, gain2),
            scalars,
            own * width * 20,
        )
        d_att_sib = swap(d_att_own, 1)
        d_att = jnp.where(
            c == 0,
            jnp.concatenate([d_att_own, d_att_sib], 0),
            jnp.concatenate([d_att_sib, d_att_own], 0),
        )
        out_o = mm(mixed_own, d_att, TN)
        out_f = mm(mixed_far, d_att, TN).astype(BF16)

        def back_kernel(s, da, wo, mixed, lse, q, k, v, dq, dk, dv, bias, dm, dkt, dvt):
            fill_bias(s, bias, seg, docs)
            dm[...] = mm(da[...], wo[...], NT).astype(BF16)
            dkt[...] = jnp.zeros_like(dkt)
            dvt[...] = jnp.zeros_like(dvt)
            lane = lax.broadcasted_iota(jnp.int32, (QROWS, 2 * HEAD), 1)
            for block in range(seg // QROWS):
                low, keys = block * QROWS, (block + 1) * QROWS
                held = None
                for head, (first, last, half) in enumerate(head_parts(cols)):
                    query = pick(q[low:keys, first:last], half) * jnp.asarray(SCALE, BF16)
                    grad = pick(dm[low:keys, first:last], half)
                    scores = mm(query, k[:keys, first:last], NT) + bias[low:keys, :keys]
                    weights = jnp.exp(scores - lse[low:keys, head : head + 1])
                    d_weights = mm(grad, v[:keys, first:last], NT)
                    inner = jnp.sum(
                        grad.astype(F32) * mixed[low:keys, first:last].astype(F32),
                        axis=-1,
                        keepdims=True,
                    )
                    d_scores = (weights * (d_weights - inner)).astype(BF16)
                    dvt[:keys, first:last] += mm(weights.astype(BF16), grad, TN)
                    dkt[:keys, first:last] += mm(d_scores, query, TN)
                    d_query = mm(d_scores, k[:keys, first:last]) * SCALE
                    if half == 0:
                        held = d_query
                    elif half == 1:
                        both = jnp.where(lane < HEAD, held, d_query)
                        dq[low:keys, first:last] = both.astype(BF16)
                    else:
                        dq[low:keys, first:last] = d_query.astype(BF16)
            dk[...] = dkt[...].astype(BF16)
            dv[...] = dvt[...].astype(BF16)

        def attention_back(weight, mixed, lse, q, k, v, name):
            return call(
                back_kernel,
                name,
                [sds((seg, cols), BF16)] * 3,
                [
                    whole((seg, width)),
                    whole((cols, width)),
                    whole((seg, cols)),
                    whole((seg, 2 * HEAD)),
                    *[whole((seg, cols))] * 3,
                ],
                [whole((seg, cols))] * 3,
                (d_att, weight, mixed, lse, q, k, v),
                scalars,
                attn_flops * 3,
                [
                    pltpu.VMEM((seg, seg), F32),
                    pltpu.VMEM((seg, cols), BF16),
                    pltpu.VMEM((seg, cols), F32),
                    pltpu.VMEM((seg, cols), F32),
                ],
            )

        dq_far, dk_far, dv_far = attention_back(
            out_far, mixed_far, lse_far, q_far, k_far, v_far, "back_far"
        )
        q_f = mm(n1, dq_far, TN)
        k_f = mm(n1, dk_far, TN)
        dq_own, dk_own, dv_own = attention_back(
            out_weight, mixed_own, lse_own, q_own, k_own, v_own, "back_own"
        )
        q_o = mm(n1, dq_own, TN)
        k_o = mm(n1, dk_own, TN)
        d_fresh = jnp.where(is_low, dv_own, dv_far)
        d_reused = jnp.where(is_low, dv_far, dv_own)
        v_part = mm(n1, d_fresh, TN)
        attn_far = jnp.concatenate([q_f.astype(BF16), k_f.astype(BF16), v_part.astype(BF16)], axis=1)
        attn_recv = swap(attn_far, 2).astype(F32)
        out_recv = swap(out_f, 2).astype(F32)
        q_sum = q_o + attn_recv[:, :cols]
        k_sum = k_o + attn_recv[:, cols : 2 * cols]
        v_sum = v_part.astype(BF16).astype(F32) + attn_recv[:, 2 * cols :]
        out_sum = out_o + out_recv
        attn_sum = jnp.concatenate([q_sum, k_sum, v_sum], axis=1).astype(BF16)

        def dn1_kernel(s, dqo, dko, dqf, dkf, df, wqo, wko, wqf, wkf, wv, send, keep):
            value_cols = jnp.where(s[1] == 0, wv[:, :cols], wv[:, cols : 2 * cols])

            def part(start):
                span = pl.ds(start, own)
                total = mm(dqo[span, :], wqo[...], NT) + mm(dko[span, :], wko[...], NT)
                total = total + mm(dqf[span, :], wqf[...], NT) + mm(dkf[span, :], wkf[...], NT)
                return (total + mm(df[span, :], value_cols, NT)).astype(BF16)

            core = s[1]
            send[...] = part(pl.multiple_of((1 - core) * own, own))
            keep[...] = part(pl.multiple_of(core * own, own))

        dn1_send, dn1_keep = call(
            dn1_kernel,
            "dn1",
            [sds((own, width), BF16)] * 2,
            [*[whole((seg, cols))] * 5, *[whole((width, cols))] * 4, whole((width, half_width))],
            [whole((own, width))] * 2,
            (
                dq_own,
                dk_own,
                dq_far,
                dk_far,
                d_fresh,
                query_weight,
                key_weight,
                query_far,
                key_far,
                value_weight,
            ),
            scalars,
            2 * seg * 5 * cols * width,
        )
        dn1_recv = swap(dn1_send, 1)

        def norm1_back(s, x, keep, recv, dh, g, out, gg, gb):
            d_norm = keep[...].astype(F32) + recv[...].astype(F32)
            hat, inverse = normalise(x[...].astype(F32))
            gg[...] = jnp.sum(d_norm * hat, axis=0, keepdims=True)
            gb[...] = jnp.sum(d_norm, axis=0, keepdims=True)
            scaled = d_norm * g[...]
            mean1 = jnp.mean(scaled, axis=-1, keepdims=True)
            mean2 = jnp.mean(scaled * hat, axis=-1, keepdims=True)
            out[...] = ((scaled - mean1 - hat * mean2) * inverse + dh[...]).astype(BF16)

        in_delta, gain1_part, bias1_part = call(
            norm1_back,
            "norm1_back",
            [sds((own, width), BF16), *[sds((1, width), F32)] * 2],
            [
                own_rows,
                whole((own, width)),
                whole((own, width)),
                whole((own, width)),
                whole((1, width)),
            ],
            [whole((own, width)), whole((1, width)), whole((1, width))],
            (block_input, dn1_keep, dn1_recv, d_hidden, gain1),
            scalars,
            own * width * 20,
        )

        def gather(mine):
            far = swap(mine, 2)
            near = swap(mine, 1)
            diag = swap(far, 1)
            low = jnp.where(is_low, mine, far), jnp.where(is_low, near, diag)
            high = jnp.where(is_low, far, mine), jnp.where(is_low, diag, near)
            flip = c == 0
            return jnp.concatenate(
                [
                    jnp.where(flip, low[0], low[1]),
                    jnp.where(flip, low[1], low[0]),
                    jnp.where(flip, high[0], high[1]),
                    jnp.where(flip, high[1], high[0]),
                ],
                axis=0,
            ).astype(F32)

        out_delta = own_block(block_input).astype(F32)
        out_delta = (hidden - out_delta) + feed_own + feed_recv.astype(F32)
        block_out = block_input.astype(F32) + gather(out_delta.astype(BF16))
        input_grad = out_grad.astype(F32) + gather(in_delta)

        reused_far = swap(d_reused, 2)
        both = jnp.where(
            is_low,
            jnp.concatenate([d_reused, reused_far], 0),
            jnp.concatenate([reused_far, d_reused], 0),
        )
        both_sib = swap(both, 1)
        first_values_grad = jnp.where(
            c == 0,
            jnp.concatenate([both, both_sib], 1),
            jnp.concatenate([both_sib, both], 1),
        ).astype(F32)

        attn_sum, out_sum, up_grad, down_grad = lax.optimization_barrier(
            (attn_sum, out_sum.astype(BF16), up_grad, down_grad)
        )
        attn_sum, out_sum = lax.psum((attn_sum, out_sum), "batch")
        attn_sum = attn_sum.astype(F32)
        query_grad = attn_sum[:, :cols]
        key_grad = attn_sum[:, cols : 2 * cols]
        v_mine = attn_sum[:, 2 * cols :]
        v_sib = swap(attn_sum[:, 2 * cols :].astype(BF16), 1).astype(F32)
        value_grad = jnp.where(
            c == 0,
            jnp.concatenate([v_mine, v_sib], 1),
            jnp.concatenate([v_sib, v_mine], 1),
        )
        vectors = jnp.concatenate([gain1_part, bias1_part, gain2_part, bias2_part], axis=0)
        vectors = lax.psum(vectors, ("batch", "mp"))
        return (
            block_out,
            input_grad,
            first_values_grad,
            vectors[0],
            vectors[1],
            query_grad,
            key_grad,
            value_grad,
            out_sum.astype(F32),
            vectors[2],
            vectors[3],
            up_grad.astype(F32),
            down_grad.astype(F32),
        )

    return jax.shard_map(
        shards,
        mesh=mesh,
        in_specs=(
            P("batch", None),
            P("batch", None),
            P(),
            P(),
            P(None, "mp"),
            P(None, "mp"),
            P(),
            P("mp", None),
            P(),
            P(),
            P(None, "mp"),
            P("mp", None),
            P("batch", None),
            P("batch", None),
        ),
        out_specs=(
            P("batch", None),
            P("batch", None),
            P("batch", None),
            P(),
            P(),
            P(None, "mp"),
            P(None, "mp"),
            P(),
            P("mp", None),
            P(),
            P(),
            P(None, "mp"),
            P("mp", None),
        ),
        check_vma=False,
    )
```

```python
import functools

import jax
import jax.numpy as jnp
from jax import lax
from jax.experimental import pallas as pl
from jax.experimental.pallas import tpu as pltpu
from jax.sharding import PartitionSpec as P

HEAD = 64
CONTEXT = 1024
EPS = 1e-05
MASKED = -1e30
QROWS = 256
SCALE = HEAD ** (-0.5)
GELU_C = 0.7978845608028654
GELU_A = 0.044715

F32 = jnp.float32
BF16 = jnp.bfloat16
VMEM_LIMIT = 56 * 1024 * 1024

NN = (((1,), (0,)), ((), ()))
NT = (((1,), (1,)), ((), ()))
TN = (((0,), (0,)), ((), ()))


def mm(left, right, dims=NN):
    return lax.dot_general(left, right, dims, preferred_element_type=F32)


def normalise(values):
    average = jnp.mean(values, axis=-1, keepdims=True)
    centred = values - average
    variance = jnp.mean(centred * centred, axis=-1, keepdims=True)
    inverse = lax.rsqrt(variance + EPS)
    return centred * inverse, inverse


def call(body, name, out_shape, in_specs, out_specs, args, scalars, flops, scratch=()):
    grid_spec = pltpu.PrefetchScalarGridSpec(
        num_scalar_prefetch=1,
        grid=(1,),
        in_specs=in_specs,
        out_specs=out_specs,
        scratch_shapes=list(scratch),
    )
    nbytes = sum(a.size * a.dtype.itemsize for a in args)
    nbytes += sum(o.size * o.dtype.itemsize for o in out_shape)
    return pl.pallas_call(
        body,
        grid_spec=grid_spec,
        out_shape=out_shape,
        name=name,
        cost_estimate=pl.CostEstimate(flops=flops, bytes_accessed=nbytes, transcendentals=0),
        compiler_params=pltpu.CompilerParams(vmem_limit_bytes=VMEM_LIMIT),
    )(scalars, *args)


def whole(shape):
    return pl.BlockSpec(shape, lambda i, s: (0,) * len(shape))


def sds(shape, dtype):
    return jax.ShapeDtypeStruct(shape, dtype)


def fill_bias(s_ref, bias_ref, seg, docs):
    base = s_ref[0] * seg
    for block in range(seg // QROWS):
        low, keys = block * QROWS, (block + 1) * QROWS
        row = lax.broadcasted_iota(jnp.int32, (QROWS, 1), 0) + low
        start = jnp.zeros((QROWS, 1), jnp.int32)
        end = jnp.int32(0)
        for doc in range(docs):
            end = end + s_ref[2 + doc]
            rel = end - base
            start = jnp.maximum(start, jnp.where(rel <= row, rel, 0))
        col = lax.broadcasted_iota(jnp.int32, (QROWS, keys), 1)
        seen = (col >= start) & (col <= row)
        bias_ref[low:keys, :keys] = jnp.where(seen, 0.0, MASKED)


def head_parts(width):
    parts = []
    for head in range(width // HEAD):
        pair = head // 2 * 2 * HEAD
        if pair + 2 * HEAD <= width:
            parts.append((pair, pair + 2 * HEAD, head % 2))
        else:
            parts.append((pair, pair + HEAD, None))
    return parts


def pick(values, half):
    if half is None:
        return values
    lane = lax.broadcasted_iota(jnp.int32, values.shape, 1)
    keep = (lane < HEAD) if half == 0 else (lane >= HEAD)
    return jnp.where(keep, values, jnp.zeros_like(values))


def attention_forward(bias_ref, q_ref, k_ref, v_ref, mixed_ref, lse_ref, seg, width):
    lane = lax.broadcasted_iota(jnp.int32, (QROWS, 2 * HEAD), 1)
    for block in range(seg // QROWS):
        low, keys = block * QROWS, (block + 1) * QROWS
        held = None
        stats = []
        for first, last, half in head_parts(width):
            query = pick(q_ref[low:keys, first:last], half) * jnp.asarray(SCALE, BF16)
            scores = mm(query, k_ref[:keys, first:last], NT) + bias_ref[low:keys, :keys]
            highest = jnp.max(scores, axis=-1, keepdims=True)
            weights = jnp.exp(scores - highest)
            total = jnp.sum(weights, axis=-1, keepdims=True)
            mixed = mm(weights.astype(BF16), v_ref[:keys, first:last]) / total
            stats.append(highest + jnp.log(total))
            if half == 0:
                held = mixed
            elif half == 1:
                both = jnp.where(lane < HEAD, held, mixed)
                mixed_ref[low:keys, first:last] = both.astype(BF16)
            else:
                mixed_ref[low:keys, first:last] = mixed.astype(BF16)
        for head, stat in enumerate(stats):
            lse_ref[low:keys, head : head + 1] = stat


def solution(mesh):
    batch_size = mesh.shape["batch"]
    assert mesh.shape["mp"] == 4

    def swap(values, bit):
        return lax.ppermute(values, "mp", [(i, i ^ bit) for i in range(4)])

    def shards(
        block_input,
        first_values,
        norm1_gain,
        norm1_bias,
        query_weight,
        key_weight,
        value_weight,
        out_weight,
        norm2_gain,
        norm2_bias,
        up_weight,
        down_weight,
        out_grad,
        doc_lengths,
    ):
        rows, width = block_input.shape
        cols = query_weight.shape[1]
        hid = up_weight.shape[1]
        half_width = value_weight.shape[1]
        docs = doc_lengths.shape[1]
        seg = rows // 2
        own = rows // 4
        assert seg == min(rows, CONTEXT)
        member = lax.axis_index("mp")
        y, c = member // 2, member % 2
        scalars = jnp.concatenate([jnp.stack([y, c]), doc_lengths[0]]).astype(jnp.int32)
        is_low = y == 0
        gain1, bias1 = norm1_gain.reshape(1, -1), norm1_bias.reshape(1, -1)
        gain2, bias2 = norm2_gain.reshape(1, -1), norm2_bias.reshape(1, -1)

        seg_rows = pl.BlockSpec((seg, width), lambda i, s: (s[0], 0))
        own_rows = pl.BlockSpec((own, width), lambda i, s: (2 * s[0] + s[1], 0))
        far_rows = pl.BlockSpec((own, width), lambda i, s: (2 * (1 - s[0]) + s[1], 0))

        pack = jnp.concatenate([query_weight.T, key_weight.T, out_weight], axis=0)
        pack_far = swap(pack, 2)
        up_sib = swap(up_weight, 1)
        down_sib = swap(down_weight, 1)

        def project(normed, w, q, k):
            q[...] = mm(normed, w[:cols, :], NT).astype(BF16)
            k[...] = mm(normed, w[cols : 2 * cols, :], NT).astype(BF16)

        def first_kernel(s, x, g, b, w, wv, fv, n1, q, k, vo, vf, mixed, lse, bias):
            fill_bias(s, bias, seg, docs)
            hat, _ = normalise(x[...].astype(F32))
            normed = (hat * g[...] + b[...]).astype(BF16)
            n1[...] = normed
            project(normed, w, q, k)
            core = s[1] == 0
            value_cols = jnp.where(core, wv[:, :cols], wv[:, cols : 2 * cols])
            fresh = mm(normed, value_cols).astype(BF16)
            reused = jnp.where(core, fv[:, :cols], fv[:, cols : 2 * cols])
            low_chip = s[0] == 0
            vo[...] = jnp.where(low_chip, fresh, reused)
            vf[...] = jnp.where(low_chip, reused, fresh)
            attention_forward(bias, q, k, vo, mixed, lse, seg, cols)

        attn_flops = 2 * 2 * seg * seg * cols * 4
        n1, q_own, k_own, v_own, v_far, mixed_own, lse_own = call(
            first_kernel,
            "attn_own",
            [
                sds((seg, width), BF16),
                *[sds((seg, cols), BF16)] * 5,
                sds((seg, 2 * HEAD), F32),
            ],
            [
                seg_rows,
                whole((1, width)),
                whole((1, width)),
                whole((3 * cols, width)),
                whole((width, half_width)),
                pl.BlockSpec((seg, half_width), lambda i, s: (s[0], 0)),
            ],
            [whole((seg, width)), *[whole((seg, cols))] * 5, whole((seg, 2 * HEAD))],
            (block_input, gain1, bias1, pack, value_weight, first_values),
            scalars,
            attn_flops * 2,
            [pltpu.VMEM((seg, seg), F32)],
        )

        def second_kernel(s, n1, w, v, q, k, mixed, lse, bias):
            fill_bias(s, bias, seg, docs)
            project(n1[...], w, q, k)
            attention_forward(bias, q, k, v, mixed, lse, seg, cols)

        q_far, k_far, mixed_far, lse_far = call(
            second_kernel,
            "attn_far",
            [*[sds((seg, cols), BF16)] * 3, sds((seg, 2 * HEAD), F32)],
            [
                whole((seg, width)),
                whole((3 * cols, width)),
                whole((seg, cols)),
            ],
            [*[whole((seg, cols))] * 3, whole((seg, 2 * HEAD))],
            (n1, pack_far, v_far),
            scalars,
            attn_flops * 2,
            [pltpu.VMEM((seg, seg), F32)],
        )

        def out_kernel(s, mo, mf, wo, wf, send, keep):
            def part(start):
                left = mm(mo[pl.ds(start, own), :], wo[2 * cols :, :]).astype(BF16).astype(F32)
                right = mm(mf[pl.ds(start, own), :], wf[2 * cols :, :]).astype(BF16).astype(F32)
                return (left + right).astype(BF16)

            core = s[1]
            send[...] = part(pl.multiple_of((1 - core) * own, own))
            keep[...] = part(pl.multiple_of(core * own, own))

        att_send, att_keep = call(
            out_kernel,
            "out_proj",
            [sds((own, width), BF16)] * 2,
            [*[whole((seg, cols))] * 2, *[whole((3 * cols, width))] * 2],
            [whole((own, width))] * 2,
            (mixed_own, mixed_far, pack, pack_far),
            scalars,
            2 * seg * 2 * cols * width,
        )
        att_recv = swap(att_send, 1)

        def norm2_kernel(s, x, keep, recv, g, b, hid_out, n2):
            hidden = x[...].astype(F32) + (keep[...].astype(F32) + recv[...].astype(F32))
            hid_out[...] = hidden
            hat, _ = normalise(hidden)
            n2[...] = (hat * g[...] + b[...]).astype(BF16)

        hidden, n2_own = call(
            norm2_kernel,
            "norm2",
            [sds((own, width), F32), sds((own, width), BF16)],
            [own_rows, whole((own, width)), whole((own, width)), whole((1, width)), whole((1, width))],
            [whole((own, width))] * 2,
            (block_input, att_keep, att_recv, gain2, bias2),
            scalars,
            own * width * 10,
        )
        n2_far = swap(n2_own, 2)

        def mlp_kernel(s, n2, og, wu0, wd0, wu1, wd1, act0, dup0, act1, dup1, dn2):
            left, grad = n2[...], og[...]
            total = jnp.zeros((own, width), F32)
            step = min(hid, 256)
            for wu, wd, act, dup in ((wu0, wd0, act0, dup0), (wu1, wd1, act1, dup1)):
                for tile in range(hid // step):
                    span = slice(tile * step, (tile + 1) * step)
                    up = mm(left, wu[:, span])
                    back = mm(grad, wd[span, :], NT)
                    square = up * up
                    slope = jnp.tanh(GELU_C * up * (1.0 + GELU_A * square))
                    bell = 0.5 * (1.0 + slope)
                    act[:, span] = (up * bell).astype(BF16)
                    inner = GELU_C * (1.0 + 3.0 * GELU_A * square)
                    deriv = bell + 0.5 * up * (1.0 - slope * slope) * inner
                    d_up = (back * deriv).astype(BF16)
                    dup[:, span] = d_up
                    total = total + mm(d_up, wu[:, span], NT)
            dn2[...] = total.astype(BF16)

        def mlp(n2, og_spec, name):
            return call(
                mlp_kernel,
                name,
                [*[sds((own, hid), BF16)] * 4, sds((own, width), BF16)],
                [
                    whole((own, width)),
                    og_spec,
                    *[whole((width, hid)), whole((hid, width))] * 2,
                ],
                [*[whole((own, hid))] * 4, whole((own, width))],
                (n2, out_grad, up_weight, down_weight, up_sib, down_sib),
                scalars,
                2 * 3 * own * width * 2 * hid,
            )

        act_oo, dup_oo, act_os, dup_os, dn2_own = mlp(n2_own, own_rows, "mlp_own")
        act_fo, dup_fo, act_fs, dup_fs, dn2_far = mlp(n2_far, far_rows, "mlp_far")
        dn2_recv = swap(dn2_far, 2)
        feed_far = (mm(act_fo, down_weight) + mm(act_fs, down_sib)).astype(BF16)
        feed_recv = swap(feed_far, 2)
        feed_own = mm(act_oo, down_weight) + mm(act_os, down_sib)

        def own_block(values):
            return lax.dynamic_slice_in_dim(values, (2 * y + c) * own, own, 0)

        def far_block(values):
            return lax.dynamic_slice_in_dim(values, (2 * (1 - y) + c) * own, own, 0)

        og_own, og_far = own_block(out_grad), far_block(out_grad)
        down_s = (mm(act_os, og_own, TN) + mm(act_fs, og_far, TN)).astype(BF16)
        up_s = (mm(n2_own, dup_os, TN) + mm(n2_far, dup_fs, TN)).astype(BF16)
        down_o = mm(act_oo, og_own, TN) + mm(act_fo, og_far, TN)
        up_o = mm(n2_own, dup_oo, TN) + mm(n2_far, dup_fo, TN)
        down_part = (down_o + swap(down_s, 1).astype(F32)).astype(BF16)
        up_part = (up_o + swap(up_s, 1).astype(F32)).astype(BF16)
        down_grad, up_grad = lax.psum((down_part, up_part), "batch")

        def norm2_back(s, h, keep, recv, og, g, dh_out, da, gg, gb):
            d_norm = keep[...].astype(F32) + recv[...].astype(F32)
            hat, inverse = normalise(h[...])
            gg[...] = jnp.sum(d_norm * hat, axis=0, keepdims=True)
            gb[...] = jnp.sum(d_norm, axis=0, keepdims=True)
            scaled = d_norm * g[...]
            mean1 = jnp.mean(scaled, axis=-1, keepdims=True)
            mean2 = jnp.mean(scaled * hat, axis=-1, keepdims=True)
            through = (scaled - mean1 - hat * mean2) * inverse
            dh_out[...] = through
            da[...] = (og[...].astype(F32) + through).astype(BF16)

        d_hidden, d_att_own, gain2_part, bias2_part = call(
            norm2_back,
            "norm2_back",
            [sds((own, width), F32), sds((own, width), BF16), *[sds((1, width), F32)] * 2],
            [
                whole((own, width)),
                whole((own, width)),
                whole((own, width)),
                own_rows,
                whole((1, width)),
            ],
            [whole((own, width)), whole((own, width)), whole((1, width)), whole((1, width))],
            (hidden, dn2_own, dn2_recv, out_grad, gain2),
            scalars,
            own * width * 20,
        )
        d_att_sib = swap(d_att_own, 1)
        def back_kernel(
            s, mine, theirs, w, n1, mixed, lse, q, k, v, dq, dk, dv, grads, bias, da, dm, dkt, dvt
        ):
            da[pl.ds(pl.multiple_of(s[1] * own, own), own), :] = mine[...]
            da[pl.ds(pl.multiple_of((1 - s[1]) * own, own), own), :] = theirs[...]
            fill_bias(s, bias, seg, docs)
            dm[...] = mm(da[...], w[2 * cols :, :], NT).astype(BF16)
            grads[2 * cols : 3 * cols, :] = mm(mixed[...], da[...], TN).astype(BF16)
            dkt[...] = jnp.zeros_like(dkt)
            dvt[...] = jnp.zeros_like(dvt)
            lane = lax.broadcasted_iota(jnp.int32, (QROWS, 2 * HEAD), 1)
            for block in range(seg // QROWS):
                low, keys = block * QROWS, (block + 1) * QROWS
                held = None
                for head, (first, last, half) in enumerate(head_parts(cols)):
                    query = pick(q[low:keys, first:last], half) * jnp.asarray(SCALE, BF16)
                    grad = pick(dm[low:keys, first:last], half)
                    scores = mm(query, k[:keys, first:last], NT) + bias[low:keys, :keys]
                    weights = jnp.exp(scores - lse[low:keys, head : head + 1])
                    d_weights = mm(grad, v[:keys, first:last], NT)
                    inner = jnp.sum(
                        grad.astype(F32) * mixed[low:keys, first:last].astype(F32),
                        axis=-1,
                        keepdims=True,
                    )
                    d_scores = (weights * (d_weights - inner)).astype(BF16)
                    dvt[:keys, first:last] += mm(weights.astype(BF16), grad, TN)
                    dkt[:keys, first:last] += mm(d_scores, query, TN)
                    d_query = mm(d_scores, k[:keys, first:last]) * SCALE
                    if half == 0:
                        held = d_query
                    elif half == 1:
                        both = jnp.where(lane < HEAD, held, d_query)
                        dq[low:keys, first:last] = both.astype(BF16)
                    else:
                        dq[low:keys, first:last] = d_query.astype(BF16)
            dk[...] = dkt[...].astype(BF16)
            dv[...] = dvt[...].astype(BF16)
            grads[:cols, :] = mm(dq[...], n1[...], TN).astype(BF16)
            grads[cols : 2 * cols, :] = mm(dk[...], n1[...], TN).astype(BF16)
            grads[3 * cols :, :] = mm(dv[...], n1[...], TN).astype(BF16)

        def attention_back(weight, mixed, lse, q, k, v, name):
            return call(
                back_kernel,
                name,
                [*[sds((seg, cols), BF16)] * 3, sds((4 * cols, width), BF16)],
                [
                    *[whole((own, width))] * 2,
                    whole((3 * cols, width)),
                    whole((seg, width)),
                    whole((seg, cols)),
                    whole((seg, 2 * HEAD)),
                    *[whole((seg, cols))] * 3,
                ],
                [*[whole((seg, cols))] * 3, whole((4 * cols, width))],
                (d_att_own, d_att_sib, weight, n1, mixed, lse, q, k, v),
                scalars,
                attn_flops * 3,
                [
                    pltpu.VMEM((seg, seg), F32),
                    pltpu.VMEM((seg, width), BF16),
                    pltpu.VMEM((seg, cols), BF16),
                    pltpu.VMEM((seg, cols), F32),
                    pltpu.VMEM((seg, cols), F32),
                ],
            )

        dq_far, dk_far, dv_far, grads_far = attention_back(
            pack_far, mixed_far, lse_far, q_far, k_far, v_far, "back_far"
        )
        dq_own, dk_own, dv_own, grads_own = attention_back(
            pack, mixed_own, lse_own, q_own, k_own, v_own, "back_own"
        )
        d_fresh = jnp.where(is_low, dv_own, dv_far)
        d_reused = jnp.where(is_low, dv_far, dv_own)
        v_part = jnp.where(is_low, grads_own[3 * cols :], grads_far[3 * cols :])
        grads_recv = swap(grads_far[: 3 * cols], 2)
        v_recv = swap(v_part, 2)

        def dn1_kernel(s, dqo, dko, dqf, dkf, df, wo, wf, wv, send, keep):
            value_cols = jnp.where(s[1] == 0, wv[:, :cols], wv[:, cols : 2 * cols])

            def part(start):
                span = pl.ds(start, own)
                total = mm(dqo[span, :], wo[:cols, :]) + mm(dko[span, :], wo[cols : 2 * cols, :])
                total = total + mm(dqf[span, :], wf[:cols, :])
                total = total + mm(dkf[span, :], wf[cols : 2 * cols, :])
                return (total + mm(df[span, :], value_cols, NT)).astype(BF16)

            core = s[1]
            send[...] = part(pl.multiple_of((1 - core) * own, own))
            keep[...] = part(pl.multiple_of(core * own, own))

        dn1_send, dn1_keep = call(
            dn1_kernel,
            "dn1",
            [sds((own, width), BF16)] * 2,
            [*[whole((seg, cols))] * 5, *[whole((3 * cols, width))] * 2, whole((width, half_width))],
            [whole((own, width))] * 2,
            (
                dq_own,
                dk_own,
                dq_far,
                dk_far,
                d_fresh,
                pack,
                pack_far,
                value_weight,
            ),
            scalars,
            2 * seg * 5 * cols * width,
        )
        dn1_recv = swap(dn1_send, 1)

        def norm1_back(s, x, keep, recv, dh, g, out, gg, gb):
            d_norm = keep[...].astype(F32) + recv[...].astype(F32)
            hat, inverse = normalise(x[...].astype(F32))
            gg[...] = jnp.sum(d_norm * hat, axis=0, keepdims=True)
            gb[...] = jnp.sum(d_norm, axis=0, keepdims=True)
            scaled = d_norm * g[...]
            mean1 = jnp.mean(scaled, axis=-1, keepdims=True)
            mean2 = jnp.mean(scaled * hat, axis=-1, keepdims=True)
            out[...] = ((scaled - mean1 - hat * mean2) * inverse + dh[...]).astype(BF16)

        in_delta, gain1_part, bias1_part = call(
            norm1_back,
            "norm1_back",
            [sds((own, width), BF16), *[sds((1, width), F32)] * 2],
            [
                own_rows,
                whole((own, width)),
                whole((own, width)),
                whole((own, width)),
                whole((1, width)),
            ],
            [whole((own, width)), whole((1, width)), whole((1, width))],
            (block_input, dn1_keep, dn1_recv, d_hidden, gain1),
            scalars,
            own * width * 20,
        )

        def gather(mine):
            far = swap(mine, 2)
            near = swap(mine, 1)
            diag = swap(far, 1)
            low = jnp.where(is_low, mine, far), jnp.where(is_low, near, diag)
            high = jnp.where(is_low, far, mine), jnp.where(is_low, diag, near)
            flip = c == 0
            return jnp.concatenate(
                [
                    jnp.where(flip, low[0], low[1]),
                    jnp.where(flip, low[1], low[0]),
                    jnp.where(flip, high[0], high[1]),
                    jnp.where(flip, high[1], high[0]),
                ],
                axis=0,
            ).astype(F32)

        out_delta = own_block(block_input).astype(F32)
        out_delta = (hidden - out_delta) + feed_own + feed_recv.astype(F32)
        block_out = block_input.astype(F32) + gather(out_delta.astype(BF16))
        input_grad = out_grad.astype(F32) + gather(in_delta)

        reused_far = swap(d_reused, 2)
        both = jnp.where(
            is_low,
            jnp.concatenate([d_reused, reused_far], 0),
            jnp.concatenate([reused_far, d_reused], 0),
        )
        both_sib = swap(both, 1)
        first_values_grad = jnp.where(
            c == 0,
            jnp.concatenate([both, both_sib], 1),
            jnp.concatenate([both_sib, both], 1),
        ).astype(F32)

        vectors = jnp.concatenate([gain1_part, bias1_part, gain2_part, bias2_part], axis=0)
        vectors = vectors + swap(vectors, 1)
        vectors = vectors + swap(vectors, 2)
        attn_part = grads_own[: 3 * cols].astype(F32) + grads_recv.astype(F32)
        attn_sum = jnp.concatenate(
            [
                attn_part,
                v_part.astype(F32) + v_recv.astype(F32),
                jnp.pad(vectors, ((0, 12), (0, 0))),
            ],
            axis=0,
        ).astype(BF16)
        attn_sum, up_grad, down_grad = lax.optimization_barrier((attn_sum, up_grad, down_grad))
        attn_sum = lax.psum(attn_sum, "batch")
        v_mine = attn_sum[3 * cols : 4 * cols]
        v_sib = swap(v_mine, 1)
        value_grad = jnp.where(
            c == 0,
            jnp.concatenate([v_mine, v_sib], 0),
            jnp.concatenate([v_sib, v_mine], 0),
        ).astype(F32).T
        attn_sum = attn_sum.astype(F32)
        query_grad = attn_sum[:cols].T
        key_grad = attn_sum[cols : 2 * cols].T
        out_sum = attn_sum[2 * cols : 3 * cols]
        vectors = attn_sum[4 * cols : 4 * cols + 4]
        return (
            block_out,
            input_grad,
            first_values_grad,
            vectors[0],
            vectors[1],
            query_grad,
            key_grad,
            value_grad,
            out_sum,
            vectors[2],
            vectors[3],
            up_grad.astype(F32),
            down_grad.astype(F32),
        )

    return jax.shard_map(
        shards,
        mesh=mesh,
        in_specs=(
            P("batch", None),
            P("batch", None),
            P(),
            P(),
            P(None, "mp"),
            P(None, "mp"),
            P(),
            P("mp", None),
            P(),
            P(),
            P(None, "mp"),
            P("mp", None),
            P("batch", None),
            P("batch", None),
        ),
        out_specs=(
            P("batch", None),
            P("batch", None),
            P("batch", None),
            P(),
            P(),
            P(None, "mp"),
            P(None, "mp"),
            P(),
            P("mp", None),
            P(),
            P(),
            P(None, "mp"),
            P("mp", None),
        ),
        check_vma=False,
    )
```

```python
import functools

import jax
import jax.numpy as jnp
from jax import lax
from jax.experimental import pallas as pl
from jax.experimental.pallas import tpu as pltpu
from jax.sharding import PartitionSpec as P

HEAD = 64
CONTEXT = 1024
EPS = 1e-05
MASKED = -1e30
QROWS = 256
SCALE = HEAD ** (-0.5)
GELU_C = 0.7978845608028654
GELU_A = 0.044715

F32 = jnp.float32
BF16 = jnp.bfloat16
VMEM_LIMIT = 56 * 1024 * 1024

NN = (((1,), (0,)), ((), ()))
NT = (((1,), (1,)), ((), ()))
TN = (((0,), (0,)), ((), ()))


def mm(left, right, dims=NN):
    return lax.dot_general(left, right, dims, preferred_element_type=F32)


def normalise(values):
    average = jnp.mean(values, axis=-1, keepdims=True)
    centred = values - average
    variance = jnp.mean(centred * centred, axis=-1, keepdims=True)
    inverse = lax.rsqrt(variance + EPS)
    return centred * inverse, inverse


def call(body, name, out_shape, in_specs, out_specs, args, scalars, flops, scratch=()):
    grid_spec = pltpu.PrefetchScalarGridSpec(
        num_scalar_prefetch=1,
        grid=(1,),
        in_specs=in_specs,
        out_specs=out_specs,
        scratch_shapes=list(scratch),
    )
    nbytes = sum(a.size * a.dtype.itemsize for a in args)
    nbytes += sum(o.size * o.dtype.itemsize for o in out_shape)
    return pl.pallas_call(
        body,
        grid_spec=grid_spec,
        out_shape=out_shape,
        name=name,
        cost_estimate=pl.CostEstimate(flops=flops, bytes_accessed=nbytes, transcendentals=0),
        compiler_params=pltpu.CompilerParams(vmem_limit_bytes=VMEM_LIMIT),
    )(scalars, *args)


def whole(shape):
    return pl.BlockSpec(shape, lambda i, s: (0,) * len(shape))


def sds(shape, dtype):
    return jax.ShapeDtypeStruct(shape, dtype)


def fill_bias(s_ref, bias_ref, seg, docs):
    base = s_ref[0] * seg
    for block in range(seg // QROWS):
        low, keys = block * QROWS, (block + 1) * QROWS
        row = lax.broadcasted_iota(jnp.int32, (QROWS, 1), 0) + low
        start = jnp.zeros((QROWS, 1), jnp.int32)
        end = jnp.int32(0)
        for doc in range(docs):
            end = end + s_ref[2 + doc]
            rel = end - base
            start = jnp.maximum(start, jnp.where(rel <= row, rel, 0))
        col = lax.broadcasted_iota(jnp.int32, (QROWS, keys), 1)
        seen = (col >= start) & (col <= row)
        bias_ref[low:keys, :keys] = jnp.where(seen, 0.0, MASKED)


def head_parts(width):
    parts = []
    for head in range(width // HEAD):
        pair = head // 2 * 2 * HEAD
        if pair + 2 * HEAD <= width:
            parts.append((pair, pair + 2 * HEAD, head % 2))
        else:
            parts.append((pair, pair + HEAD, None))
    return parts


def pick(values, half):
    if half is None:
        return values
    lane = lax.broadcasted_iota(jnp.int32, values.shape, 1)
    keep = (lane < HEAD) if half == 0 else (lane >= HEAD)
    return jnp.where(keep, values, jnp.zeros_like(values))


def attention_forward(bias_ref, q_ref, k_ref, v_ref, mixed_ref, lse_ref, seg, width):
    lane = lax.broadcasted_iota(jnp.int32, (QROWS, 2 * HEAD), 1)
    for block in range(seg // QROWS):
        low, keys = block * QROWS, (block + 1) * QROWS
        held = None
        stats = []
        for first, last, half in head_parts(width):
            query = pick(q_ref[low:keys, first:last], half) * jnp.asarray(SCALE, BF16)
            scores = mm(query, k_ref[:keys, first:last], NT) + bias_ref[low:keys, :keys]
            highest = jnp.max(scores, axis=-1, keepdims=True)
            weights = jnp.exp(scores - highest)
            total = jnp.sum(weights, axis=-1, keepdims=True)
            mixed = mm(weights.astype(BF16), v_ref[:keys, first:last]) / total
            stats.append(highest + jnp.log(total))
            if half == 0:
                held = mixed
            elif half == 1:
                both = jnp.where(lane < HEAD, held, mixed)
                mixed_ref[low:keys, first:last] = both.astype(BF16)
            else:
                mixed_ref[low:keys, first:last] = mixed.astype(BF16)
        for head, stat in enumerate(stats):
            lse_ref[low:keys, head : head + 1] = stat


MESH = pl.DeviceIdType.MESH


def flipped(index, bit):
    digit = lax.rem(lax.div(index, jnp.int32(bit)), jnp.int32(2))
    return index + bit - 2 * bit * digit, digit


class Wire:
    def __init__(self, send, recv):
        self.send, self.recv, self.used, self.sent = send, recv, 0, []

    def copy(self, src, dst, device):
        at = self.used
        self.used += 1
        return pltpu.make_async_remote_copy(
            src_ref=src,
            dst_ref=dst,
            send_sem=self.send.at[at],
            recv_sem=self.recv.at[at],
            device_id=device,
            device_id_type=MESH,
        )

    def start(self, src, dst, device):
        moving = self.copy(src, dst, device)
        moving.start()
        self.sent.append(moving)
        return moving

    def drain(self):
        for moving in self.sent:
            moving.wait_send()


def rows_at(start, count):
    return pl.ds(pl.multiple_of(start, 16), count)


def greet(devices):
    barrier = pltpu.get_barrier_semaphore()
    for device in devices:
        pl.semaphore_signal(barrier, inc=1, device_id=device, device_id_type=MESH)
    pl.semaphore_wait(barrier, len(devices))


class Reduction:
    def __init__(self, wire, index, bits, acc, out, recv, base, count):
        self.wire, self.acc, self.out, self.recv = wire, acc, out, recv
        self.base, self.count = base, count
        self.start, self.size = jnp.int32(base), count
        self.fills = base
        self.index, self.bits = index, bits
        self.trail = []

    def send_half(self, step):
        other, digit = flipped(self.index, self.bits[step])
        half = self.size // 2
        keep = self.start + digit * half
        give = self.start + (1 - digit) * half
        land = self.recv.at[pl.ds(self.fills, half), :]
        self.moving = self.wire.start(self.acc.at[rows_at(give, half), :], land, {"batch": other})
        self.trail.append((self.start, self.size, other))
        self.start, self.size = keep, half

    def add_half(self):
        self.moving.wait_recv()
        span = rows_at(self.start, self.size)
        landed = self.recv[self.fills : self.fills + self.size, :]
        total = self.acc[span, :].astype(F32) + landed.astype(F32)
        self.acc[span, :] = total.astype(BF16)
        self.fills += self.size

    def turn(self):
        span = rows_at(self.start, self.size)
        self.out[span, :] = self.acc[span, :]

    def send_whole(self):
        start, size, other = self.trail.pop()
        here = self.out.at[rows_at(self.start, self.size), :]
        self.moving = self.wire.start(here, here, {"batch": other})
        self.start, self.size = start, size

    def take_whole(self):
        self.moving.wait_recv()


def solution(mesh):
    batch_size = mesh.shape["batch"]
    assert mesh.shape["mp"] == 4

    def swap(values, bit):
        return lax.ppermute(values, "mp", [(i, i ^ bit) for i in range(4)])

    def shards(
        block_input,
        first_values,
        norm1_gain,
        norm1_bias,
        query_weight,
        key_weight,
        value_weight,
        out_weight,
        norm2_gain,
        norm2_bias,
        up_weight,
        down_weight,
        out_grad,
        doc_lengths,
    ):
        rows, width = block_input.shape
        cols = query_weight.shape[1]
        hid = up_weight.shape[1]
        half_width = value_weight.shape[1]
        docs = doc_lengths.shape[1]
        seg = rows // 2
        own = rows // 4
        assert seg == min(rows, CONTEXT)
        member = lax.axis_index("mp")
        y, c = member // 2, member % 2
        scalars = jnp.concatenate([jnp.stack([y, c]), doc_lengths[0]]).astype(jnp.int32)
        is_low = y == 0
        gain1, bias1 = norm1_gain.reshape(1, -1), norm1_bias.reshape(1, -1)
        gain2, bias2 = norm2_gain.reshape(1, -1), norm2_bias.reshape(1, -1)

        seg_rows = pl.BlockSpec((seg, width), lambda i, s: (s[0], 0))
        own_rows = pl.BlockSpec((own, width), lambda i, s: (2 * s[0] + s[1], 0))
        far_rows = pl.BlockSpec((own, width), lambda i, s: (2 * (1 - s[0]) + s[1], 0))

        pack = jnp.concatenate([query_weight.T, key_weight.T, out_weight], axis=0)
        pack_far = swap(pack, 2)
        up_sib = swap(up_weight, 1)
        down_sib = swap(down_weight, 1)

        def project(normed, w, q, k):
            q[...] = mm(normed, w[:cols, :], NT).astype(BF16)
            k[...] = mm(normed, w[cols : 2 * cols, :], NT).astype(BF16)

        def first_kernel(s, x, g, b, w, wv, fv, n1, q, k, vo, vf, mixed, lse, bias):
            fill_bias(s, bias, seg, docs)
            hat, _ = normalise(x[...].astype(F32))
            normed = (hat * g[...] + b[...]).astype(BF16)
            n1[...] = normed
            project(normed, w, q, k)
            core = s[1] == 0
            value_cols = jnp.where(core, wv[:, :cols], wv[:, cols : 2 * cols])
            fresh = mm(normed, value_cols).astype(BF16)
            reused = jnp.where(core, fv[:, :cols], fv[:, cols : 2 * cols])
            low_chip = s[0] == 0
            vo[...] = jnp.where(low_chip, fresh, reused)
            vf[...] = jnp.where(low_chip, reused, fresh)
            attention_forward(bias, q, k, vo, mixed, lse, seg, cols)

        attn_flops = 2 * 2 * seg * seg * cols * 4
        n1, q_own, k_own, v_own, v_far, mixed_own, lse_own = call(
            first_kernel,
            "attn_own",
            [
                sds((seg, width), BF16),
                *[sds((seg, cols), BF16)] * 5,
                sds((seg, 2 * HEAD), F32),
            ],
            [
                seg_rows,
                whole((1, width)),
                whole((1, width)),
                whole((3 * cols, width)),
                whole((width, half_width)),
                pl.BlockSpec((seg, half_width), lambda i, s: (s[0], 0)),
            ],
            [whole((seg, width)), *[whole((seg, cols))] * 5, whole((seg, 2 * HEAD))],
            (block_input, gain1, bias1, pack, value_weight, first_values),
            scalars,
            attn_flops * 2,
            [pltpu.VMEM((seg, seg), F32)],
        )

        def second_kernel(s, n1, w, v, q, k, mixed, lse, bias):
            fill_bias(s, bias, seg, docs)
            project(n1[...], w, q, k)
            attention_forward(bias, q, k, v, mixed, lse, seg, cols)

        q_far, k_far, mixed_far, lse_far = call(
            second_kernel,
            "attn_far",
            [*[sds((seg, cols), BF16)] * 3, sds((seg, 2 * HEAD), F32)],
            [
                whole((seg, width)),
                whole((3 * cols, width)),
                whole((seg, cols)),
            ],
            [*[whole((seg, cols))] * 3, whole((seg, 2 * HEAD))],
            (n1, pack_far, v_far),
            scalars,
            attn_flops * 2,
            [pltpu.VMEM((seg, seg), F32)],
        )

        def out_kernel(s, mo, mf, wo, wf, send, keep):
            def part(start):
                left = mm(mo[pl.ds(start, own), :], wo[2 * cols :, :]).astype(BF16).astype(F32)
                right = mm(mf[pl.ds(start, own), :], wf[2 * cols :, :]).astype(BF16).astype(F32)
                return (left + right).astype(BF16)

            core = s[1]
            send[...] = part(pl.multiple_of((1 - core) * own, own))
            keep[...] = part(pl.multiple_of(core * own, own))

        att_send, att_keep = call(
            out_kernel,
            "out_proj",
            [sds((own, width), BF16)] * 2,
            [*[whole((seg, cols))] * 2, *[whole((3 * cols, width))] * 2],
            [whole((own, width))] * 2,
            (mixed_own, mixed_far, pack, pack_far),
            scalars,
            2 * seg * 2 * cols * width,
        )
        att_recv = swap(att_send, 1)

        def norm2_kernel(s, x, keep, recv, g, b, hid_out, n2):
            hidden = x[...].astype(F32) + (keep[...].astype(F32) + recv[...].astype(F32))
            hid_out[...] = hidden
            hat, _ = normalise(hidden)
            n2[...] = (hat * g[...] + b[...]).astype(BF16)

        hidden, n2_own = call(
            norm2_kernel,
            "norm2",
            [sds((own, width), F32), sds((own, width), BF16)],
            [own_rows, whole((own, width)), whole((own, width)), whole((1, width)), whole((1, width))],
            [whole((own, width))] * 2,
            (block_input, att_keep, att_recv, gain2, bias2),
            scalars,
            own * width * 10,
        )
        n2_far = swap(n2_own, 2)

        def mlp_kernel(s, n2, og, wu0, wd0, wu1, wd1, act0, dup0, act1, dup1, dn2):
            left, grad = n2[...], og[...]
            total = jnp.zeros((own, width), F32)
            step = min(hid, 256)
            for wu, wd, act, dup in ((wu0, wd0, act0, dup0), (wu1, wd1, act1, dup1)):
                for tile in range(hid // step):
                    span = slice(tile * step, (tile + 1) * step)
                    up = mm(left, wu[:, span])
                    back = mm(grad, wd[span, :], NT)
                    square = up * up
                    slope = jnp.tanh(GELU_C * up * (1.0 + GELU_A * square))
                    bell = 0.5 * (1.0 + slope)
                    act[:, span] = (up * bell).astype(BF16)
                    inner = GELU_C * (1.0 + 3.0 * GELU_A * square)
                    deriv = bell + 0.5 * up * (1.0 - slope * slope) * inner
                    d_up = (back * deriv).astype(BF16)
                    dup[:, span] = d_up
                    total = total + mm(d_up, wu[:, span], NT)
            dn2[...] = total.astype(BF16)

        def mlp(n2, og_spec, name):
            return call(
                mlp_kernel,
                name,
                [*[sds((own, hid), BF16)] * 4, sds((own, width), BF16)],
                [
                    whole((own, width)),
                    og_spec,
                    *[whole((width, hid)), whole((hid, width))] * 2,
                ],
                [*[whole((own, hid))] * 4, whole((own, width))],
                (n2, out_grad, up_weight, down_weight, up_sib, down_sib),
                scalars,
                2 * 3 * own * width * 2 * hid,
            )

        act_oo, dup_oo, act_os, dup_os, dn2_own = mlp(n2_own, own_rows, "mlp_own")
        act_fo, dup_fo, act_fs, dup_fs, dn2_far = mlp(n2_far, far_rows, "mlp_far")
        dn2_recv = swap(dn2_far, 2)
        feed_far = (mm(act_fo, down_weight) + mm(act_fs, down_sib)).astype(BF16)
        feed_recv = swap(feed_far, 2)
        feed_own = mm(act_oo, down_weight) + mm(act_os, down_sib)

        def own_block(values):
            return lax.dynamic_slice_in_dim(values, (2 * y + c) * own, own, 0)

        def far_block(values):
            return lax.dynamic_slice_in_dim(values, (2 * (1 - y) + c) * own, own, 0)

        og_own, og_far = own_block(out_grad), far_block(out_grad)
        down_s = (mm(act_os, og_own, TN) + mm(act_fs, og_far, TN)).astype(BF16)
        up_s = (mm(n2_own, dup_os, TN) + mm(n2_far, dup_fs, TN)).astype(BF16)
        down_o = mm(act_oo, og_own, TN) + mm(act_fo, og_far, TN)
        up_o = mm(n2_own, dup_oo, TN) + mm(n2_far, dup_fo, TN)
        down_part = (down_o + swap(down_s, 1).astype(F32)).astype(BF16)
        up_part = (up_o + swap(up_s, 1).astype(F32)).astype(BF16)

        bits = [1 << i for i in range(batch_size.bit_length() - 1)]
        assert 1 << len(bits) == batch_size
        granule = 16 * batch_size
        stream = -(-2 * cols // granule) * granule
        orders = (bits, bits[1:] + bits[:1])
        n_copies = 10 + 6 * len(bits) + 2

        def attention_backward(bias, w, mixed, lse, q, k, v, da, dm, dkt, dvt, dq, dk, dv):
            dm[...] = mm(da[...], w[2 * cols :, :], NT).astype(BF16)
            dkt[...] = jnp.zeros_like(dkt)
            dvt[...] = jnp.zeros_like(dvt)
            lane = lax.broadcasted_iota(jnp.int32, (QROWS, 2 * HEAD), 1)
            for block in range(seg // QROWS):
                low, keys = block * QROWS, (block + 1) * QROWS
                held = None
                for head, (first, last, half) in enumerate(head_parts(cols)):
                    query = pick(q[low:keys, first:last], half) * jnp.asarray(SCALE, BF16)
                    grad = pick(dm[low:keys, first:last], half)
                    scores = mm(query, k[:keys, first:last], NT) + bias[low:keys, :keys]
                    weights = jnp.exp(scores - lse[low:keys, head : head + 1])
                    d_weights = mm(grad, v[:keys, first:last], NT)
                    inner = jnp.sum(
                        grad.astype(F32) * mixed[low:keys, first:last].astype(F32),
                        axis=-1,
                        keepdims=True,
                    )
                    d_scores = (weights * (d_weights - inner)).astype(BF16)
                    dvt[:keys, first:last] += mm(weights.astype(BF16), grad, TN)
                    dkt[:keys, first:last] += mm(d_scores, query, TN)
                    d_query = mm(d_scores, k[:keys, first:last]) * SCALE
                    if half == 0:
                        held = d_query
                    elif half == 1:
                        both = jnp.where(lane < HEAD, held, d_query)
                        dq[low:keys, first:last] = both.astype(BF16)
                    else:
                        dq[low:keys, first:last] = d_query.astype(BF16)
            dk[...] = dkt[...].astype(BF16)
            dv[...] = dvt[...].astype(BF16)

        def norm_backward(d_norm, values, gain):
            hat, inverse = normalise(values)
            d_gain = jnp.sum(d_norm * hat, axis=0, keepdims=True)
            d_bias = jnp.sum(d_norm, axis=0, keepdims=True)
            scaled = d_norm * gain
            mean1 = jnp.mean(scaled, axis=-1, keepdims=True)
            mean2 = jnp.mean(scaled * hat, axis=-1, keepdims=True)
            return (scaled - mean1 - hat * mean2) * inverse, d_gain, d_bias

        def tail_kernel(
            lengths,
            x,
            og,
            hidden,
            dn2_keep,
            dn2_recv,
            bo_own,
            g1,
            g2,
            w_own,
            w_far,
            wv,
            n1,
            mo,
            lo,
            qo,
            ko,
            vo,
            mf,
            lf,
            qf,
            kf,
            vf,
            bo_all,
            ig_all,
            fv_all,
            total,
            vec,
            bias,
            x_here,
            og_here,
            through,
            da,
            dm,
            dkt,
            dvt,
            dqo,
            dko,
            dvo,
            dqf,
            dkf,
            dvf,
            fresh,
            g_send,
            g_recv,
            v_recv,
            dn_send,
            dn_recv,
            acc,
            landing,
            vec_send,
            vec_recv,
            send_sems,
            recv_sems,
            local_sems,
        ):
            me = lax.axis_index("mp")
            row = lax.axis_index("batch")
            sibling, core = flipped(me, 1)
            across, chip = flipped(me, 2)
            to_sib, to_far = {"mp": sibling}, {"mp": across}
            wire = Wire(send_sems, recv_sems)
            here = rows_at(me * own, own)
            loads = [
                pltpu.make_async_copy(x.at[here, :], x_here, local_sems.at[0]),
                pltpu.make_async_copy(og.at[here, :], og_here, local_sems.at[1]),
            ]
            for load in loads:
                load.start()
            greet([to_sib, to_far, *[{"batch": flipped(row, bit)[0]} for bit in bits]])
            bo_all[here, :] = bo_own[...]
            bo_far = wire.start(bo_all.at[here, :], bo_all.at[here, :], to_far)
            bo_near = wire.start(bo_all.at[here, :], bo_all.at[here, :], to_sib)
            for load in loads:
                load.wait()

            d_norm = dn2_keep[...].astype(F32) + dn2_recv[...].astype(F32)
            back, d_gain2, d_bias2 = norm_backward(d_norm, hidden[...], g2[...])
            through[...] = back
            mine = rows_at(core * own, own)
            da[mine, :] = (og_here[...].astype(F32) + back).astype(BF16)
            da_swap = wire.start(da.at[mine, :], da.at[mine, :], to_sib)
            fill_bias((chip, core, *[lengths[i] for i in range(docs)]), bias, seg, docs)
            da_swap.wait_recv()

            attention_backward(bias, w_far, mf, lf, qf, kf, vf, da, dm, dkt, dvt, dqf, dkf, dvf)
            g_send[:cols, :] = mm(dqf[...], n1[...], TN).astype(BF16)
            g_send[cols : 2 * cols, :] = mm(dkf[...], n1[...], TN).astype(BF16)
            g_send[2 * cols : 3 * cols, :] = mm(mf[...], da[...], TN).astype(BF16)
            g_swap = wire.start(g_send.at[pl.ds(0, 3 * cols), :], g_recv, to_far)
            attention_backward(bias, w_own, mo, lo, qo, ko, vo, da, dm, dkt, dvt, dqo, dko, dvo)
            bo_far.wait_recv()
            there = rows_at(across * own, own)
            bo_diag = wire.start(bo_all.at[there, :], bo_all.at[there, :], to_sib)

            low_chip = chip == 0
            fresh[...] = jnp.where(low_chip, dvo[...], dvf[...])
            fv_all[pl.ds(me, 1)] = jnp.where(low_chip, dvf[...], dvo[...])[None]
            value_cols = jnp.where(core == 0, wv[:, :cols], wv[:, cols : 2 * cols])

            def dn1_part(start):
                span = rows_at(start, own)
                part = mm(dqo[span, :], w_own[:cols, :])
                part = part + mm(dko[span, :], w_own[cols : 2 * cols, :])
                part = part + mm(dqf[span, :], w_far[:cols, :])
                part = part + mm(dkf[span, :], w_far[cols : 2 * cols, :])
                return (part + mm(fresh[span, :], value_cols, NT)).astype(BF16)

            dn_send[...] = dn1_part((1 - core) * own)
            dn_swap = wire.start(dn_send, dn_recv, to_sib)
            v_grad = mm(fresh[...], n1[...], TN).astype(BF16)
            g_send[3 * cols :, :] = v_grad
            v_swap = wire.start(g_send.at[pl.ds(3 * cols, cols), :], v_recv, to_far)
            kept = dn1_part(core * own).astype(F32)
            dn_swap.wait_recv()
            d_norm = kept + dn_recv[...].astype(F32)
            back, d_gain1, d_bias1 = norm_backward(d_norm, x_here[...].astype(F32), g1[...])
            ig_all[here, :] = (back + through[...]).astype(BF16)
            ig_far = wire.start(ig_all.at[here, :], ig_all.at[here, :], to_far)
            ig_near = wire.start(ig_all.at[here, :], ig_all.at[here, :], to_sib)
            fv_far = wire.start(fv_all.at[pl.ds(me, 1)], fv_all.at[pl.ds(me, 1)], to_far)
            fv_near = wire.start(fv_all.at[pl.ds(me, 1)], fv_all.at[pl.ds(me, 1)], to_sib)

            acc[:cols, :] = mm(dqo[...], n1[...], TN).astype(BF16)
            acc[cols : 2 * cols, :] = mm(dko[...], n1[...], TN).astype(BF16)
            acc[stream : stream + cols, :] = mm(mo[...], da[...], TN).astype(BF16)
            if stream > 2 * cols:
                acc[2 * cols : stream, :] = jnp.zeros((stream - 2 * cols, width), BF16)
                acc[stream + 2 * cols :, :] = jnp.zeros((stream - 2 * cols, width), BF16)
            g_swap.wait_recv()
            for start, source in ((0, 0), (cols, cols), (stream, 2 * cols)):
                part = acc[start : start + cols, :].astype(F32)
                part = part + g_recv[source : source + cols, :].astype(F32)
                acc[start : start + cols, :] = part.astype(BF16)
            v_swap.wait_recv()
            acc[stream + cols : stream + 2 * cols, :] = (
                g_send[3 * cols :, :].astype(F32) + v_recv[...].astype(F32)
            ).astype(BF16)

            ranks = [to_sib, to_far, *[{"batch": flipped(row, bit)[0]} for bit in bits]]
            vec_send[0] = jnp.concatenate(
                [d_gain1, d_bias1, d_gain2, d_bias2, jnp.zeros((4, width), F32)], axis=0
            )
            streams = [
                Reduction(wire, row, orders[i], acc, total, landing, i * stream, stream)
                for i in range(2)
            ]

            def vector_step(at):
                if at < len(ranks):
                    return wire.start(vec_send.at[at], vec_recv.at[at], ranks[at])
                return None

            def vector_add(at, moving):
                if moving is not None:
                    moving.wait_recv()
                    vec_send[at + 1] = vec_send[at] + vec_recv[at]

            for step in range(len(bits)):
                for one in streams:
                    one.send_half(step)
                moving = vector_step(step)
                for one in streams:
                    one.add_half()
                vector_add(step, moving)
            for one in streams:
                one.turn()
            for step in range(len(bits)):
                for one in streams:
                    one.send_whole()
                moving = vector_step(len(bits) + step)
                if step == 0:
                    ig_far.wait_recv()
                    ig_diag = wire.start(ig_all.at[there, :], ig_all.at[there, :], to_sib)
                for one in streams:
                    one.take_whole()
                vector_add(len(bits) + step, moving)
            vec[...] = vec_send[len(ranks)]
            fv_far.wait_recv()
            fv_there = fv_all.at[pl.ds(across, 1)]
            fv_diag = wire.start(fv_there, fv_there, to_sib)
            for moving in (bo_near, bo_diag, ig_near, ig_diag, fv_near, fv_diag):
                moving.wait_recv()
            wire.drain()

        vm = pl.BlockSpec(memory_space=pltpu.VMEM)
        hbm = pl.BlockSpec(memory_space=pl.ANY)
        bo_own = (hidden - own_block(block_input).astype(F32)) + feed_own + feed_recv.astype(F32)
        bo_own, down_part, up_part = lax.optimization_barrier(
            (bo_own.astype(BF16), down_part, up_part)
        )
        down_grad, up_grad = lax.psum((down_part, up_part), "batch")
        tail_args = (
            doc_lengths[0],
            block_input,
            out_grad,
            hidden,
            dn2_own,
            dn2_recv,
            bo_own,
            gain1,
            gain2,
            pack,
            pack_far,
            value_weight,
            n1,
            mixed_own,
            lse_own,
            q_own,
            k_own,
            v_own,
            mixed_far,
            lse_far,
            q_far,
            k_far,
            v_far,
        )
        bo_all, ig_all, fv_all, attn_sum, vectors = pl.pallas_call(
            tail_kernel,
            name="tail",
            out_shape=[
                sds((rows, width), BF16),
                sds((rows, width), BF16),
                sds((4, seg, cols), BF16),
                sds((2 * stream, width), BF16),
                sds((8, width), F32),
            ],
            in_specs=[pl.BlockSpec(memory_space=pltpu.SMEM), hbm, hbm, *[vm] * 20],
            out_specs=[vm] * 5,
            scratch_shapes=[
                pltpu.VMEM((seg, seg), F32),
                pltpu.VMEM((own, width), BF16),
                pltpu.VMEM((own, width), BF16),
                pltpu.VMEM((own, width), F32),
                pltpu.VMEM((seg, width), BF16),
                pltpu.VMEM((seg, cols), BF16),
                pltpu.VMEM((seg, cols), F32),
                pltpu.VMEM((seg, cols), F32),
                *[pltpu.VMEM((seg, cols), BF16)] * 7,
                pltpu.VMEM((4 * cols, width), BF16),
                pltpu.VMEM((3 * cols, width), BF16),
                pltpu.VMEM((cols, width), BF16),
                pltpu.VMEM((own, width), BF16),
                pltpu.VMEM((own, width), BF16),
                pltpu.VMEM((2 * stream, width), BF16),
                pltpu.VMEM((2 * stream, width), BF16),
                pltpu.VMEM((len(bits) + 3, 8, width), F32),
                pltpu.VMEM((len(bits) + 2, 8, width), F32),
                pltpu.SemaphoreType.DMA((n_copies,)),
                pltpu.SemaphoreType.DMA((n_copies,)),
                pltpu.SemaphoreType.DMA((2,)),
            ],
            cost_estimate=pl.CostEstimate(
                flops=attn_flops * 12, bytes_accessed=30000000, transcendentals=0
            ),
            compiler_params=pltpu.CompilerParams(
                collective_id=0, has_side_effects=True, vmem_limit_bytes=VMEM_LIMIT
            ),
        )(*tail_args)
        block_out = block_input.astype(F32) + bo_all.astype(F32)
        input_grad = out_grad.astype(F32) + ig_all.astype(F32)
        first_values_grad = jnp.concatenate(
            [
                jnp.concatenate([fv_all[0], fv_all[1]], axis=1),
                jnp.concatenate([fv_all[2], fv_all[3]], axis=1),
            ],
            axis=0,
        ).astype(F32)
        v_mine = attn_sum[stream + cols : stream + 2 * cols]
        v_sib = swap(v_mine, 1)
        value_grad = jnp.where(
            c == 0,
            jnp.concatenate([v_mine, v_sib], 0),
            jnp.concatenate([v_sib, v_mine], 0),
        ).astype(F32).T
        query_grad = attn_sum[:cols].astype(F32).T
        key_grad = attn_sum[cols : 2 * cols].astype(F32).T
        out_sum = attn_sum[stream : stream + cols].astype(F32)
        return (
            block_out,
            input_grad,
            first_values_grad,
            vectors[0],
            vectors[1],
            query_grad,
            key_grad,
            value_grad,
            out_sum,
            vectors[2],
            vectors[3],
            up_grad.astype(F32),
            down_grad.astype(F32),
        )

    return jax.shard_map(
        shards,
        mesh=mesh,
        in_specs=(
            P("batch", None),
            P("batch", None),
            P(),
            P(),
            P(None, "mp"),
            P(None, "mp"),
            P(),
            P("mp", None),
            P(),
            P(),
            P(None, "mp"),
            P("mp", None),
            P("batch", None),
            P("batch", None),
        ),
        out_specs=(
            P("batch", None),
            P("batch", None),
            P("batch", None),
            P(),
            P(),
            P(None, "mp"),
            P(None, "mp"),
            P(),
            P("mp", None),
            P(),
            P(),
            P(None, "mp"),
            P("mp", None),
        ),
        check_vma=False,
    )
```

```python
import functools

import jax
import jax.numpy as jnp
from jax import lax
from jax.experimental import pallas as pl
from jax.experimental.pallas import tpu as pltpu
from jax.sharding import PartitionSpec as P

HEAD = 64
CONTEXT = 1024
EPS = 1e-05
MASKED = -1e30
QROWS = 256
SCALE = HEAD ** (-0.5)
GELU_C = 0.7978845608028654
GELU_A = 0.044715

F32 = jnp.float32
BF16 = jnp.bfloat16
VMEM_LIMIT = 60 * 1024 * 1024

NN = (((1,), (0,)), ((), ()))
NT = (((1,), (1,)), ((), ()))
TN = (((0,), (0,)), ((), ()))


def mm(left, right, dims=NN):
    return lax.dot_general(left, right, dims, preferred_element_type=F32)


def normalise(values):
    average = jnp.mean(values, axis=-1, keepdims=True)
    centred = values - average
    variance = jnp.mean(centred * centred, axis=-1, keepdims=True)
    inverse = lax.rsqrt(variance + EPS)
    return centred * inverse, inverse


def sds(shape, dtype):
    return jax.ShapeDtypeStruct(shape, dtype)


def fill_bias(s_ref, bias_ref, seg, docs):
    base = s_ref[0] * seg
    for block in range(seg // QROWS):
        low, keys = block * QROWS, (block + 1) * QROWS
        row = lax.broadcasted_iota(jnp.int32, (QROWS, 1), 0) + low
        start = jnp.zeros((QROWS, 1), jnp.int32)
        end = jnp.int32(0)
        for doc in range(docs):
            end = end + s_ref[2 + doc]
            rel = end - base
            start = jnp.maximum(start, jnp.where(rel <= row, rel, 0))
        col = lax.broadcasted_iota(jnp.int32, (QROWS, keys), 1)
        seen = (col >= start) & (col <= row)
        bias_ref[low:keys, :keys] = jnp.where(seen, 0.0, MASKED)


def head_parts(width):
    parts = []
    for head in range(width // HEAD):
        pair = head // 2 * 2 * HEAD
        if pair + 2 * HEAD <= width:
            parts.append((pair, pair + 2 * HEAD, head % 2))
        else:
            parts.append((pair, pair + HEAD, None))
    return parts


def pick(values, half):
    if half is None:
        return values
    lane = lax.broadcasted_iota(jnp.int32, values.shape, 1)
    keep = (lane < HEAD) if half == 0 else (lane >= HEAD)
    return jnp.where(keep, values, jnp.zeros_like(values))


def attention_forward(bias_ref, q_ref, k_ref, v_ref, mixed_ref, lse_ref, seg, width):
    lane = lax.broadcasted_iota(jnp.int32, (QROWS, 2 * HEAD), 1)
    for block in range(seg // QROWS):
        low, keys = block * QROWS, (block + 1) * QROWS
        held = None
        stats = []
        for first, last, half in head_parts(width):
            query = pick(q_ref[low:keys, first:last], half) * jnp.asarray(SCALE, BF16)
            scores = mm(query, k_ref[:keys, first:last], NT) + bias_ref[low:keys, :keys]
            highest = jnp.max(scores, axis=-1, keepdims=True)
            weights = jnp.exp(scores - highest)
            total = jnp.sum(weights, axis=-1, keepdims=True)
            mixed = mm(weights.astype(BF16), v_ref[:keys, first:last]) / total
            stats.append(highest + jnp.log(total))
            if half == 0:
                held = mixed
            elif half == 1:
                both = jnp.where(lane < HEAD, held, mixed)
                mixed_ref[low:keys, first:last] = both.astype(BF16)
            else:
                mixed_ref[low:keys, first:last] = mixed.astype(BF16)
        for head, stat in enumerate(stats):
            lse_ref[low:keys, head : head + 1] = stat


MESH = pl.DeviceIdType.MESH


def flipped(index, bit):
    digit = lax.rem(lax.div(index, jnp.int32(bit)), jnp.int32(2))
    return index + bit - 2 * bit * digit, digit


class Wire:
    def __init__(self, send, recv):
        self.send, self.recv, self.used, self.sent = send, recv, 0, []

    def copy(self, src, dst, device):
        at = self.used
        self.used += 1
        return pltpu.make_async_remote_copy(
            src_ref=src,
            dst_ref=dst,
            send_sem=self.send.at[at],
            recv_sem=self.recv.at[at],
            device_id=device,
            device_id_type=MESH,
        )

    def start(self, src, dst, device):
        moving = self.copy(src, dst, device)
        moving.start()
        self.sent.append(moving)
        return moving

    def drain(self):
        for moving in self.sent:
            moving.wait_send()


def rows_at(start, count):
    return pl.ds(pl.multiple_of(start, 16), count)


def greet(devices):
    barrier = pltpu.get_barrier_semaphore()
    for device in devices:
        pl.semaphore_signal(barrier, inc=1, device_id=device, device_id_type=MESH)
    pl.semaphore_wait(barrier, len(devices))


class Reduction:
    def __init__(self, wire, index, bits, acc, out, recv, base, count):
        self.wire, self.acc, self.out, self.recv = wire, acc, out, recv
        self.base, self.count = base, count
        self.start, self.size = jnp.int32(base), count
        self.fills = base
        self.index, self.bits = index, bits
        self.trail = []

    def send_half(self, step):
        other, digit = flipped(self.index, self.bits[step])
        half = self.size // 2
        keep = self.start + digit * half
        give = self.start + (1 - digit) * half
        land = self.recv.at[pl.ds(self.fills, half), :]
        self.moving = self.wire.start(self.acc.at[rows_at(give, half), :], land, {"batch": other})
        self.trail.append((self.start, self.size, other))
        self.start, self.size = keep, half

    def add_half(self):
        self.moving.wait_recv()
        span = rows_at(self.start, self.size)
        landed = self.recv[self.fills : self.fills + self.size, :]
        total = self.acc[span, :].astype(F32) + landed.astype(F32)
        self.acc[span, :] = total.astype(BF16)
        self.fills += self.size

    def turn(self):
        span = rows_at(self.start, self.size)
        self.out[span, :] = self.acc[span, :]

    def send_whole(self):
        start, size, other = self.trail.pop()
        here = self.out.at[rows_at(self.start, self.size), :]
        self.moving = self.wire.start(here, here, {"batch": other})
        self.start, self.size = start, size

    def take_whole(self):
        self.moving.wait_recv()


def solution(mesh):
    batch_size = mesh.shape["batch"]
    assert mesh.shape["mp"] == 4

    def swap(values, bit):
        return lax.ppermute(values, "mp", [(i, i ^ bit) for i in range(4)])

    def shards(
        block_input,
        first_values,
        norm1_gain,
        norm1_bias,
        query_weight,
        key_weight,
        value_weight,
        out_weight,
        norm2_gain,
        norm2_bias,
        up_weight,
        down_weight,
        out_grad,
        doc_lengths,
    ):
        rows, width = block_input.shape
        cols = query_weight.shape[1]
        hid = up_weight.shape[1]
        half_width = value_weight.shape[1]
        docs = doc_lengths.shape[1]
        seg = rows // 2
        own = rows // 4
        assert seg == min(rows, CONTEXT)
        member = lax.axis_index("mp")
        c = member % 2
        gain1, bias1 = norm1_gain.reshape(1, -1), norm1_bias.reshape(1, -1)
        gain2, bias2 = norm2_gain.reshape(1, -1), norm2_bias.reshape(1, -1)


        def project(normed, w, q, k):
            q[...] = mm(normed, w[:cols, :], NT).astype(BF16)
            k[...] = mm(normed, w[cols : 2 * cols, :], NT).astype(BF16)

        def head_kernel(
            lengths,
            x,
            og,
            fv,
            g1,
            b1,
            g2,
            b2,
            wq,
            wk,
            wo,
            wv,
            wu,
            wd,
            n1,
            qo,
            ko,
            vo,
            mo,
            lo,
            qf,
            kf,
            vf,
            mf,
            lf,
            w_far,
            through,
            da,
            bo_part,
            feed_far,
            w_grads,
            vec,
            bias,
            x_seg,
            fv_seg,
            n2,
            og2,
            act,
            dup,
            wu_sib,
            wd_sib,
            att_send,
            att_recv,
            dn2_own,
            dn2_send,
            dn2_recv,
            g_send,
            g_recv,
            send_sems,
            recv_sems,
            local_sems,
        ):
            me = lax.axis_index("mp")
            sibling, core = flipped(me, 1)
            across, chip = flipped(me, 2)
            to_sib, to_far = {"mp": sibling}, {"mp": across}
            wire = Wire(send_sems, recv_sems)
            loads = []
            for source, rows_from, count, target in (
                (x, chip * seg, seg, x_seg),
                (fv, chip * seg, seg, fv_seg),
                (og, me * own, own, og2.at[pl.ds(0, own), :]),
                (og, across * own, own, og2.at[pl.ds(own, own), :]),
            ):
                load = pltpu.make_async_copy(
                    source.at[rows_at(rows_from, count), :], target, local_sems.at[len(loads)]
                )
                load.start()
                loads.append(load)
            greet([to_sib, to_far])
            swaps = [
                wire.start(w, w_far.at[pl.ds(i * cols, cols), :], to_far)
                for i, w in enumerate((wq, wk, wo))
            ]
            up_swap = wire.start(wu, wu_sib, to_sib)
            down_swap = wire.start(wd, wd_sib, to_sib)
            scalars = (chip, core, *[lengths[i] for i in range(docs)])
            fill_bias(scalars, bias, seg, docs)
            for load in loads:
                load.wait()

            hat, _ = normalise(x_seg[...].astype(F32))
            normed = (hat * g1[...] + b1[...]).astype(BF16)
            n1[...] = normed
            qo[...] = mm(normed, wq[...], NT).astype(BF16)
            ko[...] = mm(normed, wk[...], NT).astype(BF16)
            value_cols = jnp.where(core == 0, wv[:, :cols], wv[:, cols : 2 * cols])
            fresh = mm(normed, value_cols).astype(BF16)
            reused = jnp.where(core == 0, fv_seg[:, :cols], fv_seg[:, cols : 2 * cols])
            vo[...] = jnp.where(chip == 0, fresh, reused)
            vf[...] = jnp.where(chip == 0, reused, fresh)
            attention_forward(bias, qo, ko, vo, mo, lo, seg, cols)
            swaps[0].wait_recv()
            swaps[1].wait_recv()
            project(n1[...], w_far, qf, kf)
            attention_forward(bias, qf, kf, vf, mf, lf, seg, cols)
            swaps[2].wait_recv()

            def out_part(start):
                span = rows_at(start, own)
                left = mm(mo[span, :], wo[...]).astype(BF16).astype(F32)
                right = mm(mf[span, :], w_far[2 * cols :, :]).astype(BF16).astype(F32)
                return (left + right).astype(BF16)

            att_send[...] = out_part((1 - core) * own)
            att_swap = wire.start(att_send, att_recv, to_sib)
            kept = out_part(core * own)
            att_swap.wait_recv()
            attention = kept.astype(F32) + att_recv[...].astype(F32)
            bo_part[...] = attention
            hidden = x_seg[rows_at(core * own, own), :].astype(F32) + attention
            chunk = own // 2
            n2_swaps = []
            for part in range(2):
                span = slice(part * chunk, (part + 1) * chunk)
                hat, _ = normalise(hidden[span])
                n2[span, :] = (hat * g2[...] + b2[...]).astype(BF16)
                n2_swaps.append(
                    wire.start(
                        n2.at[pl.ds(part * chunk, chunk), :],
                        n2.at[pl.ds(own + part * chunk, chunk), :],
                        to_far,
                    )
                )
            through[...] = hidden
            up_swap.wait_recv()
            down_swap.wait_recv()

            def mlp(start, count):
                span = slice(start, start + count)
                step = min(hid, 256)
                for at, (up_w, down_w) in enumerate(((wu, wd), (wu_sib, wd_sib))):
                    for tile in range(hid // step):
                        part = slice(tile * step, (tile + 1) * step)
                        place = slice(at * hid + tile * step, at * hid + (tile + 1) * step)
                        up = mm(n2[span, :], up_w[:, part])
                        back = mm(og2[span, :], down_w[part, :], NT)
                        square = up * up
                        slope = jnp.tanh(GELU_C * up * (1.0 + GELU_A * square))
                        bell = 0.5 * (1.0 + slope)
                        act[span, place] = (up * bell).astype(BF16)
                        inner = GELU_C * (1.0 + 3.0 * GELU_A * square)
                        deriv = bell + 0.5 * up * (1.0 - slope * slope) * inner
                        dup[span, place] = (back * deriv).astype(BF16)
                total = mm(dup[span, :hid], wu[...], NT)
                return total + mm(dup[span, hid:], wu_sib[...], NT)

            def feed(start, count):
                span = slice(start, start + count)
                return mm(act[span, :hid], wd[...]) + mm(act[span, hid:], wd_sib[...])

            dn2_own[...] = mlp(0, own).astype(BF16)
            bo_part[...] += feed(0, own)
            dn2_swaps = []
            for part in range(2):
                n2_swaps[part].wait_recv()
                span = slice(part * chunk, (part + 1) * chunk)
                dn2_send[span, :] = mlp(own + part * chunk, chunk).astype(BF16)
                block = pl.ds(part * chunk, chunk)
                dn2_swaps.append(wire.start(dn2_send.at[block, :], dn2_recv.at[block, :], to_far))
            g_send[:hid, :] = mm(act[:, hid:], og2[...], TN).astype(BF16)
            g_send[hid:, :] = mm(n2[...], dup[:, hid:], TN).astype(BF16)
            g_swap = wire.start(g_send, g_recv, to_sib)
            feed_far[...] = feed(own, own).astype(BF16)
            down_own = mm(act[:, :hid], og2[...], TN)
            up_own = mm(n2[...], dup[:, :hid], TN)
            g_swap.wait_recv()
            w_grads[:hid, :] = (down_own + g_recv[:hid, :].astype(F32)).astype(BF16)
            w_grads[hid:, :] = (up_own + g_recv[hid:, :].astype(F32)).astype(BF16)

            for swap in dn2_swaps:
                swap.wait_recv()
            d_norm = dn2_own[...].astype(F32) + dn2_recv[...].astype(F32)
            back, d_gain, d_bias = norm_backward(d_norm, through[...], g2[...])
            through[...] = back
            da[...] = (og2[:own, :].astype(F32) + back).astype(BF16)
            vec[...] = jnp.concatenate([d_gain, d_bias, jnp.zeros((6, width), F32)], axis=0)
            wire.drain()

        def norm_backward(d_norm, values, gain):
            hat, inverse = normalise(values)
            d_gain = jnp.sum(d_norm * hat, axis=0, keepdims=True)
            d_bias = jnp.sum(d_norm, axis=0, keepdims=True)
            scaled = d_norm * gain
            mean1 = jnp.mean(scaled, axis=-1, keepdims=True)
            mean2 = jnp.mean(scaled * hat, axis=-1, keepdims=True)
            return (scaled - mean1 - hat * mean2) * inverse, d_gain, d_bias

        vm = pl.BlockSpec(memory_space=pltpu.VMEM)
        hbm = pl.BlockSpec(memory_space=pl.ANY)
        smem = pl.BlockSpec(memory_space=pltpu.SMEM)
        attn_flops = 2 * 2 * seg * seg * cols * 4
        query_rows, key_rows = query_weight.T, key_weight.T
        heads_of_shard = [*[sds((seg, cols), BF16)] * 4, sds((seg, 2 * HEAD), F32)]
        n_head_copies = 16
        (
            n1,
            q_own,
            k_own,
            v_own,
            mixed_own,
            lse_own,
            q_far,
            k_far,
            v_far,
            mixed_far,
            lse_far,
            w_far,
            through,
            d_att,
            bo_part,
            feed_far,
            w_grads,
            vec2,
        ) = pl.pallas_call(
            head_kernel,
            name="head",
            out_shape=[
                sds((seg, width), BF16),
                *heads_of_shard,
                *heads_of_shard,
                sds((3 * cols, width), BF16),
                sds((own, width), F32),
                sds((own, width), BF16),
                sds((own, width), F32),
                sds((own, width), BF16),
                sds((2 * hid, width), BF16),
                sds((8, width), F32),
            ],
            in_specs=[smem, hbm, hbm, hbm, *[vm] * 10],
            out_specs=[vm] * 18,
            scratch_shapes=[
                pltpu.VMEM((seg, seg), F32),
                pltpu.VMEM((seg, width), BF16),
                pltpu.VMEM((seg, half_width), BF16),
                pltpu.VMEM((2 * own, width), BF16),
                pltpu.VMEM((2 * own, width), BF16),
                pltpu.VMEM((2 * own, 2 * hid), BF16),
                pltpu.VMEM((2 * own, 2 * hid), BF16),
                pltpu.VMEM((width, hid), BF16),
                pltpu.VMEM((hid, width), BF16),
                *[pltpu.VMEM((own, width), BF16)] * 5,
                pltpu.VMEM((2 * hid, width), BF16),
                pltpu.VMEM((2 * hid, width), BF16),
                pltpu.SemaphoreType.DMA((n_head_copies,)),
                pltpu.SemaphoreType.DMA((n_head_copies,)),
                pltpu.SemaphoreType.DMA((4,)),
            ],
            cost_estimate=pl.CostEstimate(
                flops=attn_flops * 8, bytes_accessed=30000000, transcendentals=0
            ),
            compiler_params=pltpu.CompilerParams(
                collective_id=1, has_side_effects=True, vmem_limit_bytes=VMEM_LIMIT
            ),
        )(
            doc_lengths[0],
            block_input,
            out_grad,
            first_values,
            gain1,
            bias1,
            gain2,
            bias2,
            query_rows,
            key_rows,
            out_weight,
            value_weight,
            up_weight,
            down_weight,
        )

        bits = [1 << i for i in range(batch_size.bit_length() - 1)]
        assert 1 << len(bits) == batch_size
        granule = 16 * batch_size
        a_count = 2 if 2 * cols % granule == 0 else 1
        a_stream = -(-4 * cols // a_count // granule) * granule
        a_rows = a_count * a_stream
        orders = (bits, bits[1:] + bits[:1])
        w_count = 4 if hid % (2 * granule // 4) == 0 else 1
        w_stream = -(-2 * hid // w_count // granule) * granule
        w_rows = w_count * w_stream
        n_copies = 16 + (6 + 2 * w_count) * len(bits)

        def attention_backward(bias, wo, mixed, lse, q, k, v, da, dm, dkt, dvt, dq, dk, dv, tick):
            dm[...] = mm(da[...], wo, NT).astype(BF16)
            dkt[...] = jnp.zeros_like(dkt)
            dvt[...] = jnp.zeros_like(dvt)
            lane = lax.broadcasted_iota(jnp.int32, (QROWS, 2 * HEAD), 1)
            for block in range(seg // QROWS):
                low, keys = block * QROWS, (block + 1) * QROWS
                held = None
                for head, (first, last, half) in enumerate(head_parts(cols)):
                    query = pick(q[low:keys, first:last], half) * jnp.asarray(SCALE, BF16)
                    grad = pick(dm[low:keys, first:last], half)
                    scores = mm(query, k[:keys, first:last], NT) + bias[low:keys, :keys]
                    weights = jnp.exp(scores - lse[low:keys, head : head + 1])
                    d_weights = mm(grad, v[:keys, first:last], NT)
                    inner = jnp.sum(
                        grad.astype(F32) * mixed[low:keys, first:last].astype(F32),
                        axis=-1,
                        keepdims=True,
                    )
                    d_scores = (weights * (d_weights - inner)).astype(BF16)
                    dvt[:keys, first:last] += mm(weights.astype(BF16), grad, TN)
                    dkt[:keys, first:last] += mm(d_scores, query, TN)
                    d_query = mm(d_scores, k[:keys, first:last]) * SCALE
                    tick(1)
                    if half == 0:
                        held = d_query
                    elif half == 1:
                        both = jnp.where(lane < HEAD, held, d_query)
                        dq[low:keys, first:last] = both.astype(BF16)
                    else:
                        dq[low:keys, first:last] = d_query.astype(BF16)
            dk[...] = dkt[...].astype(BF16)
            dv[...] = dvt[...].astype(BF16)

        def tail_kernel(
            lengths,
            x,
            through,
            da_own,
            bo_part,
            feed_far,
            vec2,
            g1,
            wq,
            wk,
            wo,
            w_far,
            wv,
            n1,
            w_grads,
            mo,
            lo,
            qo,
            ko,
            vo,
            mf,
            lf,
            qf,
            kf,
            vf,
            bo_all,
            ig_all,
            fv_all,
            total,
            w_total,
            vec,
            bias,
            x_here,
            da,
            dm,
            dkt,
            dvt,
            dqo,
            dko,
            dvo,
            dqf,
            dkf,
            dvf,
            fresh,
            g_send,
            g_recv,
            v_recv,
            dn_send,
            dn_recv,
            feed_recv,
            acc,
            landing,
            w_acc,
            w_landing,
            vec_send,
            vec_recv,
            send_sems,
            recv_sems,
            local_sems,
        ):
            me = lax.axis_index("mp")
            row = lax.axis_index("batch")
            sibling, core = flipped(me, 1)
            across, chip = flipped(me, 2)
            to_sib, to_far = {"mp": sibling}, {"mp": across}
            wire = Wire(send_sems, recv_sems)
            here = rows_at(me * own, own)
            there = rows_at(across * own, own)
            load = pltpu.make_async_copy(x.at[here, :], x_here, local_sems.at[0])
            load.start()
            greet([to_sib, to_far, *[{"batch": flipped(row, bit)[0]} for bit in bits]])
            mine = rows_at(core * own, own)
            da[mine, :] = da_own[...]
            da_swap = wire.start(da.at[mine, :], da.at[mine, :], to_sib)
            feed_swap = wire.start(feed_far, feed_recv, to_far)
            w_acc[: 2 * hid, :] = w_grads[...]
            if w_rows > 2 * hid:
                w_acc[2 * hid :, :] = jnp.zeros((w_rows - 2 * hid, width), BF16)
            w_streams = [
                Reduction(wire, row, bits, w_acc, w_total, w_landing, i * w_stream, w_stream)
                for i in range(w_count)
            ]
            for one in w_streams:
                one.send_half(0)
            fill_bias((chip, core, *[lengths[i] for i in range(docs)]), bias, seg, docs)
            load.wait()
            da_swap.wait_recv()

            agenda = []
            last_step = len(bits) - 1

            def halve(one, step):
                one.add_half()
                if step < last_step:
                    one.send_half(step + 1)
                else:
                    one.turn()
                    one.send_whole()

            def double(one, step):
                one.take_whole()
                if step < last_step:
                    one.send_whole()

            for at, one in enumerate(w_streams):
                due = 8 + 7 * at
                for step in range(len(bits)):
                    agenda.append((due, at, functools.partial(halve, one, step)))
                    due += 5
                for step in range(len(bits)):
                    agenda.append((due, at, functools.partial(double, one, step)))
                    due += 5 if step < last_step - 1 else 8
            agenda.sort(key=lambda item: item[:2])
            clock = [0]

            def tick(count):
                clock[0] += count
                while agenda and agenda[0][0] <= clock[0]:
                    agenda.pop(0)[2]()

            far_out = w_far[2 * cols :, :]
            attention_backward(
                bias, far_out, mf, lf, qf, kf, vf, da, dm, dkt, dvt, dqf, dkf, dvf, tick
            )
            g_send[:cols, :] = mm(dqf[...], n1[...], TN).astype(BF16)
            g_send[cols : 2 * cols, :] = mm(dkf[...], n1[...], TN).astype(BF16)
            g_send[2 * cols : 3 * cols, :] = mm(mf[...], da[...], TN).astype(BF16)
            g_swap = wire.start(g_send.at[pl.ds(0, 3 * cols), :], g_recv, to_far)
            attention_backward(
                bias, wo[...], mo, lo, qo, ko, vo, da, dm, dkt, dvt, dqo, dko, dvo, tick
            )

            low_chip = chip == 0
            fresh[...] = jnp.where(low_chip, dvo[...], dvf[...])
            fv_all[pl.ds(me, 1)] = jnp.where(low_chip, dvf[...], dvo[...])[None]
            value_cols = jnp.where(core == 0, wv[:, :cols], wv[:, cols : 2 * cols])

            def dn1_part(start):
                span = rows_at(start, own)
                part = mm(dqo[span, :], wq[...])
                part = part + mm(dko[span, :], wk[...])
                part = part + mm(dqf[span, :], w_far[:cols, :])
                part = part + mm(dkf[span, :], w_far[cols : 2 * cols, :])
                return (part + mm(fresh[span, :], value_cols, NT)).astype(BF16)

            dn_send[...] = dn1_part((1 - core) * own)
            dn_swap = wire.start(dn_send, dn_recv, to_sib)
            tick(2)
            v_grad = mm(fresh[...], n1[...], TN).astype(BF16)
            g_send[3 * cols :, :] = v_grad
            v_swap = wire.start(g_send.at[pl.ds(3 * cols, cols), :], v_recv, to_far)
            kept = dn1_part(core * own).astype(F32)
            tick(2)
            dn_swap.wait_recv()
            d_norm = kept + dn_recv[...].astype(F32)
            back, d_gain1, d_bias1 = norm_backward(d_norm, x_here[...].astype(F32), g1[...])
            ig_all[here, :] = (back + through[...]).astype(BF16)
            ig_far = wire.start(ig_all.at[here, :], ig_all.at[here, :], to_far)
            ig_near = wire.start(ig_all.at[here, :], ig_all.at[here, :], to_sib)
            fv_far = wire.start(fv_all.at[pl.ds(me, 1)], fv_all.at[pl.ds(me, 1)], to_far)
            fv_near = wire.start(fv_all.at[pl.ds(me, 1)], fv_all.at[pl.ds(me, 1)], to_sib)
            feed_swap.wait_recv()
            bo_all[here, :] = (bo_part[...] + feed_recv[...].astype(F32)).astype(BF16)
            bo_far = wire.start(bo_all.at[here, :], bo_all.at[here, :], to_far)
            bo_near = wire.start(bo_all.at[here, :], bo_all.at[here, :], to_sib)
            tick(4)

            acc[:cols, :] = mm(dqo[...], n1[...], TN).astype(BF16)
            acc[cols : 2 * cols, :] = mm(dko[...], n1[...], TN).astype(BF16)
            acc[2 * cols : 3 * cols, :] = mm(mo[...], da[...], TN).astype(BF16)
            if a_rows > 4 * cols:
                acc[4 * cols :, :] = jnp.zeros((a_rows - 4 * cols, width), BF16)
            tick(3)
            g_swap.wait_recv()
            shared = acc[: 3 * cols, :].astype(F32) + g_recv[...].astype(F32)
            acc[: 3 * cols, :] = shared.astype(BF16)
            v_swap.wait_recv()
            acc[3 * cols : 4 * cols, :] = (
                g_send[3 * cols :, :].astype(F32) + v_recv[...].astype(F32)
            ).astype(BF16)

            ranks = [to_sib, to_far, *[{"batch": flipped(row, bit)[0]} for bit in bits]]
            vec_send[0] = jnp.concatenate(
                [d_gain1, d_bias1, vec2[:2, :], jnp.zeros((4, width), F32)], axis=0
            )
            streams = [
                Reduction(wire, row, orders[i], acc, total, landing, i * a_stream, a_stream)
                for i in range(a_count)
            ]

            def vector_step(at):
                if at < len(ranks):
                    return wire.start(vec_send.at[at], vec_recv.at[at], ranks[at])
                return None

            def vector_add(at, moving):
                if moving is not None:
                    moving.wait_recv()
                    vec_send[at + 1] = vec_send[at] + vec_recv[at]

            for step in range(len(bits)):
                for one in streams:
                    one.send_half(step)
                moving = vector_step(step)
                tick(4)
                for one in streams:
                    one.add_half()
                vector_add(step, moving)
            for one in streams:
                one.turn()
            for step in range(len(bits)):
                for one in streams:
                    one.send_whole()
                moving = vector_step(len(bits) + step)
                if step == 0:
                    ig_far.wait_recv()
                    ig_diag = wire.start(ig_all.at[there, :], ig_all.at[there, :], to_sib)
                tick(5)
                for one in streams:
                    one.take_whole()
                vector_add(len(bits) + step, moving)
            vec[...] = vec_send[len(ranks)]
            tick(1000)
            bo_far.wait_recv()
            bo_diag = wire.start(bo_all.at[there, :], bo_all.at[there, :], to_sib)
            fv_far.wait_recv()
            fv_there = fv_all.at[pl.ds(across, 1)]
            fv_diag = wire.start(fv_there, fv_there, to_sib)
            for moving in (bo_near, bo_diag, ig_near, ig_diag, fv_near, fv_diag):
                moving.wait_recv()
            wire.drain()

        tail_args = (
            doc_lengths[0],
            block_input,
            through,
            d_att,
            bo_part,
            feed_far,
            vec2,
            gain1,
            query_rows,
            key_rows,
            out_weight,
            w_far,
            value_weight,
            n1,
            w_grads,
            mixed_own,
            lse_own,
            q_own,
            k_own,
            v_own,
            mixed_far,
            lse_far,
            q_far,
            k_far,
            v_far,
        )
        bo_all, ig_all, fv_all, attn_sum, w_total, vectors = pl.pallas_call(
            tail_kernel,
            name="tail",
            out_shape=[
                sds((rows, width), BF16),
                sds((rows, width), BF16),
                sds((4, seg, cols), BF16),
                sds((a_rows, width), BF16),
                sds((w_rows, width), BF16),
                sds((8, width), F32),
            ],
            in_specs=[smem, hbm, *[vm] * 23],
            out_specs=[vm] * 6,
            scratch_shapes=[
                pltpu.VMEM((seg, seg), F32),
                pltpu.VMEM((own, width), BF16),
                pltpu.VMEM((seg, width), BF16),
                pltpu.VMEM((seg, cols), BF16),
                pltpu.VMEM((seg, cols), F32),
                pltpu.VMEM((seg, cols), F32),
                *[pltpu.VMEM((seg, cols), BF16)] * 7,
                pltpu.VMEM((4 * cols, width), BF16),
                pltpu.VMEM((3 * cols, width), BF16),
                pltpu.VMEM((cols, width), BF16),
                pltpu.VMEM((own, width), BF16),
                pltpu.VMEM((own, width), BF16),
                pltpu.VMEM((own, width), BF16),
                pltpu.VMEM((a_rows, width), BF16),
                pltpu.VMEM((a_rows, width), BF16),
                pltpu.VMEM((w_rows, width), BF16),
                pltpu.VMEM((w_rows, width), BF16),
                pltpu.VMEM((len(bits) + 3, 8, width), F32),
                pltpu.VMEM((len(bits) + 2, 8, width), F32),
                pltpu.SemaphoreType.DMA((n_copies,)),
                pltpu.SemaphoreType.DMA((n_copies,)),
                pltpu.SemaphoreType.DMA((1,)),
            ],
            cost_estimate=pl.CostEstimate(
                flops=attn_flops * 12, bytes_accessed=30000000, transcendentals=0
            ),
            compiler_params=pltpu.CompilerParams(
                collective_id=0, has_side_effects=True, vmem_limit_bytes=VMEM_LIMIT
            ),
        )(*tail_args)
        block_out = block_input.astype(F32) + bo_all.astype(F32)
        input_grad = out_grad.astype(F32) + ig_all.astype(F32)
        first_values_grad = jnp.concatenate(
            [
                jnp.concatenate([fv_all[0], fv_all[1]], axis=1),
                jnp.concatenate([fv_all[2], fv_all[3]], axis=1),
            ],
            axis=0,
        ).astype(F32)
        v_mine = attn_sum[3 * cols : 4 * cols]
        v_sib = swap(v_mine, 1)
        value_grad = jnp.where(
            c == 0,
            jnp.concatenate([v_mine, v_sib], 0),
            jnp.concatenate([v_sib, v_mine], 0),
        ).astype(F32).T
        query_grad = attn_sum[:cols].astype(F32).T
        key_grad = attn_sum[cols : 2 * cols].astype(F32).T
        out_sum = attn_sum[2 * cols : 3 * cols].astype(F32)
        down_grad, up_grad = w_total[:hid].astype(F32), w_total[hid : 2 * hid].astype(F32)
        return (
            block_out,
            input_grad,
            first_values_grad,
            vectors[0],
            vectors[1],
            query_grad,
            key_grad,
            value_grad,
            out_sum,
            vectors[2],
            vectors[3],
            up_grad,
            down_grad,
        )

    return jax.shard_map(
        shards,
        mesh=mesh,
        in_specs=(
            P("batch", None),
            P("batch", None),
            P(),
            P(),
            P(None, "mp"),
            P(None, "mp"),
            P(),
            P("mp", None),
            P(),
            P(),
            P(None, "mp"),
            P("mp", None),
            P("batch", None),
            P("batch", None),
        ),
        out_specs=(
            P("batch", None),
            P("batch", None),
            P("batch", None),
            P(),
            P(),
            P(None, "mp"),
            P(None, "mp"),
            P(),
            P("mp", None),
            P(),
            P(),
            P(None, "mp"),
            P("mp", None),
        ),
        check_vma=False,
    )
```

```python
import functools

import jax
import jax.numpy as jnp
from jax import lax
from jax.experimental import pallas as pl
from jax.experimental.pallas import tpu as pltpu
from jax.sharding import PartitionSpec as P

HEAD = 64
CONTEXT = 1024
EPS = 1e-05
MASKED = -1e30
QROWS = 256
SCALE = HEAD ** (-0.5)
GELU_C = 0.7978845608028654
GELU_A = 0.044715

F32 = jnp.float32
BF16 = jnp.bfloat16
HEAD_VMEM = 60 * 1024 * 1024
TAIL_VMEM = 50 * 1024 * 1024

NN = (((1,), (0,)), ((), ()))
NT = (((1,), (1,)), ((), ()))
TN = (((0,), (0,)), ((), ()))


def mm(left, right, dims=NN):
    return lax.dot_general(left, right, dims, preferred_element_type=F32)


def normalise(values):
    average = jnp.mean(values, axis=-1, keepdims=True)
    centred = values - average
    variance = jnp.mean(centred * centred, axis=-1, keepdims=True)
    inverse = lax.rsqrt(variance + EPS)
    return centred * inverse, inverse


def sds(shape, dtype):
    return jax.ShapeDtypeStruct(shape, dtype)


def fill_bias(s_ref, bias_ref, seg, docs):
    base = s_ref[0] * seg
    for block in range(seg // QROWS):
        low, keys = block * QROWS, (block + 1) * QROWS
        row = lax.broadcasted_iota(jnp.int32, (QROWS, 1), 0) + low
        start = jnp.zeros((QROWS, 1), jnp.int32)
        end = jnp.int32(0)
        for doc in range(docs):
            end = end + s_ref[2 + doc]
            rel = end - base
            start = jnp.maximum(start, jnp.where(rel <= row, rel, 0))
        col = lax.broadcasted_iota(jnp.int32, (QROWS, keys), 1)
        seen = (col >= start) & (col <= row)
        bias_ref[low:keys, :keys] = jnp.where(seen, 0.0, MASKED)


def head_parts(width):
    parts = []
    for head in range(width // HEAD):
        pair = head // 2 * 2 * HEAD
        if pair + 2 * HEAD <= width:
            parts.append((pair, pair + 2 * HEAD, head % 2))
        else:
            parts.append((pair, pair + HEAD, None))
    return parts


def pick(values, half):
    if half is None:
        return values
    lane = lax.broadcasted_iota(jnp.int32, values.shape, 1)
    keep = (lane < HEAD) if half == 0 else (lane >= HEAD)
    return jnp.where(keep, values, jnp.zeros_like(values))


def attention_forward(bias_ref, q_ref, k_ref, v_ref, mixed_ref, lse_ref, seg, width):
    lane = lax.broadcasted_iota(jnp.int32, (QROWS, 2 * HEAD), 1)
    for block in range(seg // QROWS):
        low, keys = block * QROWS, (block + 1) * QROWS
        held = None
        stats = []
        for first, last, half in head_parts(width):
            query = pick(q_ref[low:keys, first:last], half) * jnp.asarray(SCALE, BF16)
            scores = mm(query, k_ref[:keys, first:last], NT) + bias_ref[low:keys, :keys]
            highest = jnp.max(scores, axis=-1, keepdims=True)
            weights = jnp.exp(scores - highest)
            total = jnp.sum(weights, axis=-1, keepdims=True)
            mixed = mm(weights.astype(BF16), v_ref[:keys, first:last]) / total
            stats.append(highest + jnp.log(total))
            if half == 0:
                held = mixed
            elif half == 1:
                both = jnp.where(lane < HEAD, held, mixed)
                mixed_ref[low:keys, first:last] = both.astype(BF16)
            else:
                mixed_ref[low:keys, first:last] = mixed.astype(BF16)
        for head, stat in enumerate(stats):
            lse_ref[low:keys, head : head + 1] = stat


MESH = pl.DeviceIdType.MESH


def flipped(index, bit):
    digit = lax.rem(lax.div(index, jnp.int32(bit)), jnp.int32(2))
    return index + bit - 2 * bit * digit, digit


class Wire:
    def __init__(self, send, recv):
        self.send, self.recv, self.used, self.sent = send, recv, 0, []

    def copy(self, src, dst, device):
        at = self.used
        self.used += 1
        return pltpu.make_async_remote_copy(
            src_ref=src,
            dst_ref=dst,
            send_sem=self.send.at[at],
            recv_sem=self.recv.at[at],
            device_id=device,
            device_id_type=MESH,
        )

    def start(self, src, dst, device):
        moving = self.copy(src, dst, device)
        moving.start()
        self.sent.append(moving)
        return moving

    def drain(self):
        for moving in self.sent:
            moving.wait_send()


def rows_at(start, count):
    return pl.ds(pl.multiple_of(start, 16), count)


def greet(devices):
    barrier = pltpu.get_barrier_semaphore()
    for device in devices:
        pl.semaphore_signal(barrier, inc=1, device_id=device, device_id_type=MESH)
    pl.semaphore_wait(barrier, len(devices))


class Reduction:
    def __init__(self, wire, index, bits, acc, out, recv, base, count):
        self.wire, self.acc, self.out, self.recv = wire, acc, out, recv
        self.base, self.count = base, count
        self.start, self.size = jnp.int32(base), count
        self.fills = base
        self.index, self.bits = index, bits
        self.trail = []

    def send_half(self, step):
        other, digit = flipped(self.index, self.bits[step])
        half = self.size // 2
        keep = self.start + digit * half
        give = self.start + (1 - digit) * half
        land = self.recv.at[pl.ds(self.fills, half), :]
        self.moving = self.wire.start(self.acc.at[rows_at(give, half), :], land, {"batch": other})
        self.trail.append((self.start, self.size, other))
        self.start, self.size = keep, half

    def add_half(self):
        self.moving.wait_recv()
        span = rows_at(self.start, self.size)
        landed = self.recv[self.fills : self.fills + self.size, :]
        total = self.acc[span, :].astype(F32) + landed.astype(F32)
        self.acc[span, :] = total.astype(BF16)
        self.fills += self.size

    def turn(self):
        span = rows_at(self.start, self.size)
        self.out[span, :] = self.acc[span, :]

    def send_whole(self):
        start, size, other = self.trail.pop()
        here = self.out.at[rows_at(self.start, self.size), :]
        self.moving = self.wire.start(here, here, {"batch": other})
        self.start, self.size = start, size

    def take_whole(self):
        self.moving.wait_recv()


def solution(mesh):
    batch_size = mesh.shape["batch"]
    assert mesh.shape["mp"] == 4

    def shards(
        block_input,
        first_values,
        norm1_gain,
        norm1_bias,
        query_weight,
        key_weight,
        value_weight,
        out_weight,
        norm2_gain,
        norm2_bias,
        up_weight,
        down_weight,
        out_grad,
        doc_lengths,
    ):
        rows, width = block_input.shape
        cols = query_weight.shape[1]
        hid = up_weight.shape[1]
        half_width = value_weight.shape[1]
        docs = doc_lengths.shape[1]
        seg = rows // 2
        own = rows // 4
        assert seg == min(rows, CONTEXT)
        norms = jnp.stack([norm1_gain, norm1_bias, norm2_gain, norm2_bias])


        def project(normed, w, q, k):
            q[...] = mm(normed, w[:cols, :], NT).astype(BF16)
            k[...] = mm(normed, w[cols : 2 * cols, :], NT).astype(BF16)

        def head_kernel(
            lengths,
            x,
            og,
            fv,
            norms,
            wq,
            wk,
            wo,
            wv,
            wu,
            wd,
            n1,
            qo,
            ko,
            vo,
            mo,
            lo,
            qf,
            kf,
            vf,
            mf,
            lf,
            w_far,
            through,
            da,
            bo_part,
            feed_far,
            w_grads,
            vec,
            bias,
            x_seg,
            fv_seg,
            n2,
            og2,
            act,
            dup,
            wu_sib,
            wd_sib,
            att_send,
            att_recv,
            dn2_own,
            dn2_send,
            dn2_recv,
            g_send,
            g_recv,
            send_sems,
            recv_sems,
            local_sems,
        ):
            me = lax.axis_index("mp")
            sibling, core = flipped(me, 1)
            across, chip = flipped(me, 2)
            to_sib, to_far = {"mp": sibling}, {"mp": across}
            wire = Wire(send_sems, recv_sems)
            loads = []
            for source, rows_from, count, target in (
                (x, chip * seg, seg, x_seg),
                (fv, chip * seg, seg, fv_seg),
                (og, me * own, own, og2.at[pl.ds(0, own), :]),
                (og, across * own, own, og2.at[pl.ds(own, own), :]),
            ):
                load = pltpu.make_async_copy(
                    source.at[rows_at(rows_from, count), :], target, local_sems.at[len(loads)]
                )
                load.start()
                loads.append(load)
            greet([to_sib, to_far])
            swaps = [
                wire.start(w, w_far.at[pl.ds(i * cols, cols), :], to_far)
                for i, w in enumerate((wq, wk, wo))
            ]
            up_swap = wire.start(wu, wu_sib, to_sib)
            down_swap = wire.start(wd, wd_sib, to_sib)
            scalars = (chip, core, *[lengths[i] for i in range(docs)])
            fill_bias(scalars, bias, seg, docs)
            for load in loads:
                load.wait()

            hat, _ = normalise(x_seg[...].astype(F32))
            normed = (hat * norms[0:1, :] + norms[1:2, :]).astype(BF16)
            n1[...] = normed
            qo[...] = mm(normed, wq[...], NT).astype(BF16)
            ko[...] = mm(normed, wk[...], NT).astype(BF16)
            value_cols = jnp.where(core == 0, wv[:, :cols], wv[:, cols : 2 * cols])
            fresh = mm(normed, value_cols).astype(BF16)
            reused = jnp.where(core == 0, fv_seg[:, :cols], fv_seg[:, cols : 2 * cols])
            vo[...] = jnp.where(chip == 0, fresh, reused)
            vf[...] = jnp.where(chip == 0, reused, fresh)
            attention_forward(bias, qo, ko, vo, mo, lo, seg, cols)
            swaps[0].wait_recv()
            swaps[1].wait_recv()
            project(n1[...], w_far, qf, kf)
            attention_forward(bias, qf, kf, vf, mf, lf, seg, cols)
            swaps[2].wait_recv()

            def out_part(start):
                span = rows_at(start, own)
                left = mm(mo[span, :], wo[...]).astype(BF16).astype(F32)
                right = mm(mf[span, :], w_far[2 * cols :, :]).astype(BF16).astype(F32)
                return (left + right).astype(BF16)

            att_send[...] = out_part((1 - core) * own)
            att_swap = wire.start(att_send, att_recv, to_sib)
            kept = out_part(core * own)
            att_swap.wait_recv()
            attention = kept.astype(F32) + att_recv[...].astype(F32)
            bo_part[...] = attention
            hidden = x_seg[rows_at(core * own, own), :].astype(F32) + attention
            chunk = own // 2
            n2_swaps = []
            for part in range(2):
                span = slice(part * chunk, (part + 1) * chunk)
                hat, _ = normalise(hidden[span])
                n2[span, :] = (hat * norms[2:3, :] + norms[3:4, :]).astype(BF16)
                n2_swaps.append(
                    wire.start(
                        n2.at[pl.ds(part * chunk, chunk), :],
                        n2.at[pl.ds(own + part * chunk, chunk), :],
                        to_far,
                    )
                )
            through[...] = hidden
            up_swap.wait_recv()
            down_swap.wait_recv()

            def mlp(start, count):
                span = slice(start, start + count)
                step = min(hid, 256)
                for at, (up_w, down_w) in enumerate(((wu, wd), (wu_sib, wd_sib))):
                    for tile in range(hid // step):
                        part = slice(tile * step, (tile + 1) * step)
                        place = slice(at * hid + tile * step, at * hid + (tile + 1) * step)
                        up = mm(n2[span, :], up_w[:, part])
                        back = mm(og2[span, :], down_w[part, :], NT)
                        square = up * up
                        slope = jnp.tanh(GELU_C * up * (1.0 + GELU_A * square))
                        bell = 0.5 * (1.0 + slope)
                        act[span, place] = (up * bell).astype(BF16)
                        inner = GELU_C * (1.0 + 3.0 * GELU_A * square)
                        deriv = bell + 0.5 * up * (1.0 - slope * slope) * inner
                        dup[span, place] = (back * deriv).astype(BF16)
                total = mm(dup[span, :hid], wu[...], NT)
                return total + mm(dup[span, hid:], wu_sib[...], NT)

            def feed(start, count):
                span = slice(start, start + count)
                return mm(act[span, :hid], wd[...]) + mm(act[span, hid:], wd_sib[...])

            dn2_own[...] = mlp(0, own).astype(BF16)
            bo_part[...] += feed(0, own)
            dn2_swaps = []
            for part in range(2):
                n2_swaps[part].wait_recv()
                span = slice(part * chunk, (part + 1) * chunk)
                dn2_send[span, :] = mlp(own + part * chunk, chunk).astype(BF16)
                block = pl.ds(part * chunk, chunk)
                dn2_swaps.append(wire.start(dn2_send.at[block, :], dn2_recv.at[block, :], to_far))
            g_send[:hid, :] = mm(act[:, hid:], og2[...], TN).astype(BF16)
            g_send[hid:, :] = mm(n2[...], dup[:, hid:], TN).astype(BF16)
            g_swap = wire.start(g_send, g_recv, to_sib)
            feed_far[...] = feed(own, own).astype(BF16)
            down_own = mm(act[:, :hid], og2[...], TN)
            up_own = mm(n2[...], dup[:, :hid], TN)
            g_swap.wait_recv()
            w_grads[:hid, :] = (down_own + g_recv[:hid, :].astype(F32)).astype(BF16)
            w_grads[hid:, :] = (up_own + g_recv[hid:, :].astype(F32)).astype(BF16)

            for swap in dn2_swaps:
                swap.wait_recv()
            d_norm = dn2_own[...].astype(F32) + dn2_recv[...].astype(F32)
            back, d_gain, d_bias = norm_backward(d_norm, through[...], norms[2:3, :])
            through[...] = back
            da[...] = (og2[:own, :].astype(F32) + back).astype(BF16)
            vec[...] = jnp.concatenate([d_gain, d_bias, jnp.zeros((6, width), F32)], axis=0)
            wire.drain()

        def norm_backward(d_norm, values, gain):
            hat, inverse = normalise(values)
            d_gain = jnp.sum(d_norm * hat, axis=0, keepdims=True)
            d_bias = jnp.sum(d_norm, axis=0, keepdims=True)
            scaled = d_norm * gain
            mean1 = jnp.mean(scaled, axis=-1, keepdims=True)
            mean2 = jnp.mean(scaled * hat, axis=-1, keepdims=True)
            return (scaled - mean1 - hat * mean2) * inverse, d_gain, d_bias

        vm = pl.BlockSpec(memory_space=pltpu.VMEM)
        hbm = pl.BlockSpec(memory_space=pl.ANY)
        smem = pl.BlockSpec(memory_space=pltpu.SMEM)
        attn_flops = 2 * 2 * seg * seg * cols * 4
        query_rows, key_rows = query_weight.T, key_weight.T
        heads_of_shard = [*[sds((seg, cols), BF16)] * 4, sds((seg, 2 * HEAD), F32)]
        n_head_copies = 16
        (
            n1,
            q_own,
            k_own,
            v_own,
            mixed_own,
            lse_own,
            q_far,
            k_far,
            v_far,
            mixed_far,
            lse_far,
            w_far,
            through,
            d_att,
            bo_part,
            feed_far,
            w_grads,
            vec2,
        ) = pl.pallas_call(
            head_kernel,
            name="head",
            out_shape=[
                sds((seg, width), BF16),
                *heads_of_shard,
                *heads_of_shard,
                sds((3 * cols, width), BF16),
                sds((own, width), F32),
                sds((own, width), BF16),
                sds((own, width), F32),
                sds((own, width), BF16),
                sds((2 * hid, width), BF16),
                sds((8, width), F32),
            ],
            in_specs=[smem, hbm, hbm, hbm, *[vm] * 7],
            out_specs=[vm] * 18,
            scratch_shapes=[
                pltpu.VMEM((seg, seg), F32),
                pltpu.VMEM((seg, width), BF16),
                pltpu.VMEM((seg, half_width), BF16),
                pltpu.VMEM((2 * own, width), BF16),
                pltpu.VMEM((2 * own, width), BF16),
                pltpu.VMEM((2 * own, 2 * hid), BF16),
                pltpu.VMEM((2 * own, 2 * hid), BF16),
                pltpu.VMEM((width, hid), BF16),
                pltpu.VMEM((hid, width), BF16),
                *[pltpu.VMEM((own, width), BF16)] * 5,
                pltpu.VMEM((2 * hid, width), BF16),
                pltpu.VMEM((2 * hid, width), BF16),
                pltpu.SemaphoreType.DMA((n_head_copies,)),
                pltpu.SemaphoreType.DMA((n_head_copies,)),
                pltpu.SemaphoreType.DMA((4,)),
            ],
            cost_estimate=pl.CostEstimate(
                flops=attn_flops * 8, bytes_accessed=30000000, transcendentals=0
            ),
            compiler_params=pltpu.CompilerParams(
                collective_id=1, has_side_effects=True, vmem_limit_bytes=HEAD_VMEM
            ),
        )(
            doc_lengths[0],
            block_input,
            out_grad,
            first_values,
            norms,
            query_rows,
            key_rows,
            out_weight,
            value_weight,
            up_weight,
            down_weight,
        )

        bits = [1 << i for i in range(batch_size.bit_length() - 1)]
        assert 1 << len(bits) == batch_size
        granule = 16 * batch_size
        a_count = 2 if 2 * cols % granule == 0 else 1
        a_stream = -(-4 * cols // a_count // granule) * granule
        a_rows = a_count * a_stream
        orders = (bits, bits[1:] + bits[:1])
        w_count = 4 if hid % (2 * granule // 4) == 0 else 1
        w_stream = -(-2 * hid // w_count // granule) * granule
        w_rows = w_count * w_stream
        n_copies = 24 + (6 + 2 * w_count) * len(bits)

        def attention_backward(bias, wo, mixed, lse, q, k, v, da, dm, dkt, dvt, dq, dk, dv, tick):
            dm[...] = mm(da[...], wo, NT).astype(BF16)
            dkt[...] = jnp.zeros_like(dkt)
            dvt[...] = jnp.zeros_like(dvt)
            lane = lax.broadcasted_iota(jnp.int32, (QROWS, 2 * HEAD), 1)
            for block in range(seg // QROWS):
                low, keys = block * QROWS, (block + 1) * QROWS
                held = None
                for head, (first, last, half) in enumerate(head_parts(cols)):
                    query = pick(q[low:keys, first:last], half) * jnp.asarray(SCALE, BF16)
                    grad = pick(dm[low:keys, first:last], half)
                    scores = mm(query, k[:keys, first:last], NT) + bias[low:keys, :keys]
                    weights = jnp.exp(scores - lse[low:keys, head : head + 1])
                    d_weights = mm(grad, v[:keys, first:last], NT)
                    inner = jnp.sum(
                        grad.astype(F32) * mixed[low:keys, first:last].astype(F32),
                        axis=-1,
                        keepdims=True,
                    )
                    d_scores = (weights * (d_weights - inner)).astype(BF16)
                    dvt[:keys, first:last] += mm(weights.astype(BF16), grad, TN)
                    dkt[:keys, first:last] += mm(d_scores, query, TN)
                    d_query = mm(d_scores, k[:keys, first:last]) * SCALE
                    tick(1)
                    if half == 0:
                        held = d_query
                    elif half == 1:
                        both = jnp.where(lane < HEAD, held, d_query)
                        dq[low:keys, first:last] = both.astype(BF16)
                    else:
                        dq[low:keys, first:last] = d_query.astype(BF16)
            dk[...] = dkt[...].astype(BF16)
            dv[...] = dvt[...].astype(BF16)

        def tail_kernel(
            lengths,
            x,
            og,
            through,
            da_own,
            bo_part,
            feed_far,
            vec2,
            norms,
            wq,
            wk,
            wo,
            w_far,
            wv,
            n1,
            w_grads,
            mo,
            lo,
            qo,
            ko,
            vo,
            mf,
            lf,
            qf,
            kf,
            vf,
            bo_all,
            ig_all,
            fv_out,
            total,
            w_total,
            value_out,
            vec,
            bias,
            x_here,
            og_here,
            fv_all,
            v_total,
            da,
            dm,
            dkt,
            dvt,
            dqo,
            dko,
            dvo,
            dqf,
            dkf,
            dvf,
            fresh,
            g_send,
            g_recv,
            v_recv,
            dn_send,
            dn_recv,
            feed_recv,
            acc,
            landing,
            w_acc,
            w_landing,
            vec_send,
            vec_recv,
            send_sems,
            recv_sems,
            local_sems,
        ):
            me = lax.axis_index("mp")
            row = lax.axis_index("batch")
            sibling, core = flipped(me, 1)
            across, chip = flipped(me, 2)
            to_sib, to_far = {"mp": sibling}, {"mp": across}
            wire = Wire(send_sems, recv_sems)
            here = rows_at(me * own, own)
            there = rows_at(across * own, own)
            loads = [
                pltpu.make_async_copy(x.at[here, :], x_here, local_sems.at[0]),
                pltpu.make_async_copy(og.at[here, :], og_here, local_sems.at[1]),
            ]
            for load in loads:
                load.start()
            greet([to_sib, to_far, *[{"batch": flipped(row, bit)[0]} for bit in bits]])
            mine = rows_at(core * own, own)
            da[mine, :] = da_own[...]
            da_swap = wire.start(da.at[mine, :], da.at[mine, :], to_sib)
            feed_swap = wire.start(feed_far, feed_recv, to_far)
            w_acc[: 2 * hid, :] = w_grads[...]
            if w_rows > 2 * hid:
                w_acc[2 * hid :, :] = jnp.zeros((w_rows - 2 * hid, width), BF16)
            w_streams = [
                Reduction(wire, row, bits, w_acc, w_total, w_landing, i * w_stream, w_stream)
                for i in range(w_count)
            ]
            for one in w_streams:
                one.send_half(0)
            fill_bias((chip, core, *[lengths[i] for i in range(docs)]), bias, seg, docs)
            for load in loads:
                load.wait()
            da_swap.wait_recv()

            agenda = []
            last_step = len(bits) - 1

            def halve(one, step):
                one.add_half()
                if step < last_step:
                    one.send_half(step + 1)
                else:
                    one.turn()
                    one.send_whole()

            def double(one, step):
                one.take_whole()
                if step < last_step:
                    one.send_whole()

            for at, one in enumerate(w_streams):
                due = 8 + 7 * at
                for step in range(len(bits)):
                    agenda.append((due, at, functools.partial(halve, one, step)))
                    due += 5
                for step in range(len(bits)):
                    agenda.append((due, at, functools.partial(double, one, step)))
                    due += 5 if step < last_step - 1 else 8
            bo_near, bo_far, bo_diag = [], [], []

            def send_out(part):
                if part == 0:
                    feed_swap.wait_recv()
                    out = bo_part[...] + feed_recv[...].astype(F32) + x_here[...].astype(F32)
                    bo_all[here, :] = out.astype(BF16)
                    bo_near.append(wire.start(bo_all.at[here, :], bo_all.at[here, :], to_sib))
                block = rows_at(me * own + part * (own // 2), own // 2)
                bo_far.append(wire.start(bo_all.at[block, :], bo_all.at[block, :], to_far))

            def pass_out(part):
                bo_far[part].wait_recv()
                block = rows_at(across * own + part * (own // 2), own // 2)
                bo_diag.append(wire.start(bo_all.at[block, :], bo_all.at[block, :], to_sib))

            agenda.append((19, -1, functools.partial(send_out, 0)))
            agenda.sort(key=lambda item: item[:2])
            clock = [0]

            def tick(count):
                clock[0] += count
                while agenda and agenda[0][0] <= clock[0]:
                    agenda.pop(0)[2]()

            far_out = w_far[2 * cols :, :]
            attention_backward(
                bias, far_out, mf, lf, qf, kf, vf, da, dm, dkt, dvt, dqf, dkf, dvf, tick
            )
            g_send[:cols, :] = mm(dqf[...], n1[...], TN).astype(BF16)
            g_send[cols : 2 * cols, :] = mm(dkf[...], n1[...], TN).astype(BF16)
            g_send[2 * cols : 3 * cols, :] = mm(mf[...], da[...], TN).astype(BF16)
            g_swap = wire.start(g_send.at[pl.ds(0, 3 * cols), :], g_recv, to_far)
            attention_backward(
                bias, wo[...], mo, lo, qo, ko, vo, da, dm, dkt, dvt, dqo, dko, dvo, tick
            )

            low_chip = chip == 0
            fresh[...] = jnp.where(low_chip, dvo[...], dvf[...])
            reused = jnp.where(low_chip, dvf[...], dvo[...])
            fv_all[pl.ds(me, 1)] = jnp.concatenate([reused[:own], reused[own:]], axis=1)[None]
            value_cols = jnp.where(core == 0, wv[:, :cols], wv[:, cols : 2 * cols])

            def dn1_part(start):
                span = rows_at(start, own)
                part = mm(dqo[span, :], wq[...])
                part = part + mm(dko[span, :], wk[...])
                part = part + mm(dqf[span, :], w_far[:cols, :])
                part = part + mm(dkf[span, :], w_far[cols : 2 * cols, :])
                return (part + mm(fresh[span, :], value_cols, NT)).astype(BF16)

            dn_send[...] = dn1_part((1 - core) * own)
            dn_swap = wire.start(dn_send, dn_recv, to_sib)
            tick(2)
            v_grad = mm(fresh[...], n1[...], TN).astype(BF16)
            g_send[3 * cols :, :] = v_grad
            v_swap = wire.start(g_send.at[pl.ds(3 * cols, cols), :], v_recv, to_far)
            kept = dn1_part(core * own).astype(F32)
            tick(2)
            dn_swap.wait_recv()
            d_norm = kept + dn_recv[...].astype(F32)
            back, d_gain1, d_bias1 = norm_backward(
                d_norm, x_here[...].astype(F32), norms[0:1, :]
            )
            ig_all[here, :] = (og_here[...].astype(F32) + back + through[...]).astype(BF16)
            ig_far = wire.start(ig_all.at[here, :], ig_all.at[here, :], to_far)
            ig_near = wire.start(ig_all.at[here, :], ig_all.at[here, :], to_sib)
            fv_mine, fv_there = fv_all.at[pl.ds(me, 1)], fv_all.at[pl.ds(across, 1)]
            fv_near = wire.start(fv_mine, fv_mine, to_sib)
            tick(4)

            acc[:cols, :] = mm(dqo[...], n1[...], TN).astype(BF16)
            acc[cols : 2 * cols, :] = mm(dko[...], n1[...], TN).astype(BF16)
            acc[2 * cols : 3 * cols, :] = mm(mo[...], da[...], TN).astype(BF16)
            if a_rows > 4 * cols:
                acc[4 * cols :, :] = jnp.zeros((a_rows - 4 * cols, width), BF16)
            tick(3)
            g_swap.wait_recv()
            shared = acc[: 3 * cols, :].astype(F32) + g_recv[...].astype(F32)
            acc[: 3 * cols, :] = shared.astype(BF16)
            v_swap.wait_recv()
            acc[3 * cols : 4 * cols, :] = (
                g_send[3 * cols :, :].astype(F32) + v_recv[...].astype(F32)
            ).astype(BF16)

            ranks = [to_sib, to_far, *[{"batch": flipped(row, bit)[0]} for bit in bits]]
            vec_send[0] = jnp.concatenate(
                [d_gain1, d_bias1, vec2[:2, :], jnp.zeros((4, width), F32)], axis=0
            )
            streams = [
                Reduction(wire, row, orders[i], acc, total, landing, i * a_stream, a_stream)
                for i in range(a_count)
            ]

            def vector_step(at):
                if at < len(ranks):
                    return wire.start(vec_send.at[at], vec_recv.at[at], ranks[at])
                return None

            def vector_add(at, moving):
                if moving is not None:
                    moving.wait_recv()
                    vec_send[at + 1] = vec_send[at] + vec_recv[at]

            for step in range(len(bits)):
                for one in streams:
                    one.send_half(step)
                moving = vector_step(step)
                tick(4)
                if step == 1:
                    fv_far = wire.start(fv_mine, fv_mine, to_far)
                for one in streams:
                    one.add_half()
                vector_add(step, moving)
            for one in streams:
                one.turn()
            for step in range(len(bits)):
                for one in streams:
                    one.send_whole()
                moving = vector_step(len(bits) + step)
                tick(5)
                if step == 0:
                    pass_out(0)
                    ig_far.wait_recv()
                    ig_diag = wire.start(ig_all.at[there, :], ig_all.at[there, :], to_sib)
                    send_out(1)
                for one in streams:
                    one.take_whole()
                vector_add(len(bits) + step, moving)
            tick(1000)
            vec[...] = vec_send[len(ranks)]

            v_rows = total.at[pl.ds(3 * cols, cols), :]
            half = rows_at(core * cols, cols)
            v_near = wire.start(v_rows, v_total.at[half, :], to_sib)
            v_total[half, :] = total[3 * cols : 4 * cols, :]
            fv_far.wait_recv()
            fv_diag = wire.start(fv_there, fv_there, to_sib)
            v_near.wait_recv()
            value_out[...] = v_total[...].astype(F32).T.astype(BF16)
            fv_near.wait_recv()
            fv_diag.wait_recv()
            for part in range(rows // own):
                first = part // 2 * 2
                lanes = slice(part % 2 * cols, (part % 2 + 1) * cols)
                fv_out[part * own : (part + 1) * own, :] = jnp.concatenate(
                    [fv_all[first][:, lanes], fv_all[first + 1][:, lanes]], axis=1
                )
            pass_out(1)
            for moving in (*bo_near, *bo_diag, ig_near, ig_diag):
                moving.wait_recv()
            wire.drain()

        tail_args = (
            doc_lengths[0],
            block_input,
            out_grad,
            through,
            d_att,
            bo_part,
            feed_far,
            vec2,
            norms,
            query_rows,
            key_rows,
            out_weight,
            w_far,
            value_weight,
            n1,
            w_grads,
            mixed_own,
            lse_own,
            q_own,
            k_own,
            v_own,
            mixed_far,
            lse_far,
            q_far,
            k_far,
            v_far,
        )
        bo_all, ig_all, fv_out, attn_sum, w_total, value_out, vectors = pl.pallas_call(
            tail_kernel,
            name="tail",
            out_shape=[
                pltpu.VMEM((rows, width), BF16),
                pltpu.VMEM((rows, width), BF16),
                pltpu.VMEM((rows, half_width), BF16),
                pltpu.VMEM((a_rows, width), BF16),
                pltpu.VMEM((w_rows, width), BF16),
                pltpu.VMEM((width, half_width), BF16),
                pltpu.VMEM((8, width), F32),
            ],
            in_specs=[smem, hbm, hbm, *[vm] * 23],
            out_specs=[vm] * 7,
            scratch_shapes=[
                pltpu.VMEM((seg, seg), F32),
                pltpu.VMEM((own, width), BF16),
                pltpu.VMEM((own, width), BF16),
                pltpu.VMEM((4, own, 2 * cols), BF16),
                pltpu.VMEM((2 * cols, width), BF16),
                pltpu.VMEM((seg, width), BF16),
                pltpu.VMEM((seg, cols), BF16),
                pltpu.VMEM((seg, cols), F32),
                pltpu.VMEM((seg, cols), F32),
                *[pltpu.VMEM((seg, cols), BF16)] * 7,
                pltpu.VMEM((4 * cols, width), BF16),
                pltpu.VMEM((3 * cols, width), BF16),
                pltpu.VMEM((cols, width), BF16),
                pltpu.VMEM((own, width), BF16),
                pltpu.VMEM((own, width), BF16),
                pltpu.VMEM((own, width), BF16),
                pltpu.VMEM((a_rows, width), BF16),
                pltpu.VMEM((a_rows, width), BF16),
                pltpu.VMEM((w_rows, width), BF16),
                pltpu.VMEM((w_rows, width), BF16),
                pltpu.VMEM((len(bits) + 3, 8, width), F32),
                pltpu.VMEM((len(bits) + 2, 8, width), F32),
                pltpu.SemaphoreType.DMA((n_copies,)),
                pltpu.SemaphoreType.DMA((n_copies,)),
                pltpu.SemaphoreType.DMA((2,)),
            ],
            cost_estimate=pl.CostEstimate(
                flops=attn_flops * 12, bytes_accessed=30000000, transcendentals=0
            ),
            compiler_params=pltpu.CompilerParams(
                collective_id=0, has_side_effects=True, vmem_limit_bytes=TAIL_VMEM
            ),
        )(*tail_args)
        block_out, input_grad = bo_all.astype(F32), ig_all.astype(F32)
        first_values_grad, value_grad = fv_out.astype(F32), value_out.astype(F32)
        query_grad = attn_sum[:cols].astype(F32).T
        key_grad = attn_sum[cols : 2 * cols].astype(F32).T
        out_sum = attn_sum[2 * cols : 3 * cols].astype(F32)
        down_grad, up_grad = w_total[:hid].astype(F32), w_total[hid : 2 * hid].astype(F32)
        return (
            block_out,
            input_grad,
            first_values_grad,
            vectors[0],
            vectors[1],
            query_grad,
            key_grad,
            value_grad,
            out_sum,
            vectors[2],
            vectors[3],
            up_grad,
            down_grad,
        )

    return jax.shard_map(
        shards,
        mesh=mesh,
        in_specs=(
            P("batch", None),
            P("batch", None),
            P(),
            P(),
            P(None, "mp"),
            P(None, "mp"),
            P(),
            P("mp", None),
            P(),
            P(),
            P(None, "mp"),
            P("mp", None),
            P("batch", None),
            P("batch", None),
        ),
        out_specs=(
            P("batch", None),
            P("batch", None),
            P("batch", None),
            P(),
            P(),
            P(None, "mp"),
            P(None, "mp"),
            P(),
            P("mp", None),
            P(),
            P(),
            P(None, "mp"),
            P("mp", None),
        ),
        check_vma=False,
    )
```

```python
import functools

import jax
import jax.numpy as jnp
from jax import lax
from jax.experimental import pallas as pl
from jax.experimental.pallas import tpu as pltpu
from jax.sharding import PartitionSpec as P

HEAD = 64
CONTEXT = 1024
EPS = 1e-05
MASKED = -1e30
QROWS = 256
SCALE = HEAD ** (-0.5)
GELU_C = 0.7978845608028654
GELU_A = 0.044715

F32 = jnp.float32
BF16 = jnp.bfloat16
HEAD_VMEM = 60 * 1024 * 1024
TAIL_VMEM = 50 * 1024 * 1024

NN = (((1,), (0,)), ((), ()))
NT = (((1,), (1,)), ((), ()))
TN = (((0,), (0,)), ((), ()))


def mm(left, right, dims=NN):
    return lax.dot_general(left, right, dims, preferred_element_type=F32)


def normalise(values):
    average = jnp.mean(values, axis=-1, keepdims=True)
    centred = values - average
    variance = jnp.mean(centred * centred, axis=-1, keepdims=True)
    inverse = lax.rsqrt(variance + EPS)
    return centred * inverse, inverse


def sds(shape, dtype):
    return jax.ShapeDtypeStruct(shape, dtype)


def fill_bias(s_ref, bias_ref, seg, docs):
    base = s_ref[0] * seg
    for block in range(seg // QROWS):
        low, keys = block * QROWS, (block + 1) * QROWS
        row = lax.broadcasted_iota(jnp.int32, (QROWS, 1), 0) + low
        start = jnp.zeros((QROWS, 1), jnp.int32)
        end = jnp.int32(0)
        for doc in range(docs):
            end = end + s_ref[2 + doc]
            rel = end - base
            start = jnp.maximum(start, jnp.where(rel <= row, rel, 0))
        col = lax.broadcasted_iota(jnp.int32, (QROWS, keys), 1)
        seen = (col >= start) & (col <= row)
        bias_ref[low:keys, :keys] = jnp.where(seen, 0.0, MASKED)


def head_parts(width):
    parts = []
    for head in range(width // HEAD):
        pair = head // 2 * 2 * HEAD
        if pair + 2 * HEAD <= width:
            parts.append((pair, pair + 2 * HEAD, head % 2))
        else:
            parts.append((pair, pair + HEAD, None))
    return parts


def pick(values, half):
    if half is None:
        return values
    lane = lax.broadcasted_iota(jnp.int32, values.shape, 1)
    keep = (lane < HEAD) if half == 0 else (lane >= HEAD)
    return jnp.where(keep, values, jnp.zeros_like(values))


def attention_forward(bias_ref, q_ref, k_ref, v_ref, mixed_ref, lse_ref, seg, width):
    lane = lax.broadcasted_iota(jnp.int32, (QROWS, 2 * HEAD), 1)
    for block in range(seg // QROWS):
        low, keys = block * QROWS, (block + 1) * QROWS
        held = None
        stats = []
        for first, last, half in head_parts(width):
            query = pick(q_ref[low:keys, first:last], half) * jnp.asarray(SCALE, BF16)
            scores = mm(query, k_ref[:keys, first:last], NT) + bias_ref[low:keys, :keys]
            highest = jnp.max(scores, axis=-1, keepdims=True)
            weights = jnp.exp(scores - highest)
            total = jnp.sum(weights, axis=-1, keepdims=True)
            mixed = mm(weights.astype(BF16), v_ref[:keys, first:last]) / total
            stats.append(highest + jnp.log(total))
            if half == 0:
                held = mixed
            elif half == 1:
                both = jnp.where(lane < HEAD, held, mixed)
                mixed_ref[low:keys, first:last] = both.astype(BF16)
            else:
                mixed_ref[low:keys, first:last] = mixed.astype(BF16)
        for head, stat in enumerate(stats):
            lse_ref[low:keys, head : head + 1] = stat


MESH = pl.DeviceIdType.MESH


def flipped(index, bit):
    digit = lax.rem(lax.div(index, jnp.int32(bit)), jnp.int32(2))
    return index + bit - 2 * bit * digit, digit


class Wire:
    def __init__(self, send, recv):
        self.send, self.recv, self.used, self.sent = send, recv, 0, []

    def copy(self, src, dst, device):
        at = self.used
        self.used += 1
        return pltpu.make_async_remote_copy(
            src_ref=src,
            dst_ref=dst,
            send_sem=self.send.at[at],
            recv_sem=self.recv.at[at],
            device_id=device,
            device_id_type=MESH,
        )

    def start(self, src, dst, device):
        moving = self.copy(src, dst, device)
        moving.start()
        self.sent.append(moving)
        return moving

    def drain(self):
        for moving in self.sent:
            moving.wait_send()


def rows_at(start, count):
    return pl.ds(pl.multiple_of(start, 16), count)


def greet(devices):
    barrier = pltpu.get_barrier_semaphore()
    for device in devices:
        pl.semaphore_signal(barrier, inc=1, device_id=device, device_id_type=MESH)
    pl.semaphore_wait(barrier, len(devices))


class Reduction:
    def __init__(self, wire, index, bits, acc, out, recv, base, count):
        self.wire, self.acc, self.out, self.recv = wire, acc, out, recv
        self.base, self.count = base, count
        self.start, self.size = jnp.int32(base), count
        self.fills = base
        self.index, self.bits = index, bits
        self.trail = []

    def send_half(self, step):
        other, digit = flipped(self.index, self.bits[step])
        half = self.size // 2
        keep = self.start + digit * half
        give = self.start + (1 - digit) * half
        land = self.recv.at[pl.ds(self.fills, half), :]
        self.moving = self.wire.start(self.acc.at[rows_at(give, half), :], land, {"batch": other})
        self.trail.append((self.start, self.size, other))
        self.start, self.size = keep, half

    def add_half(self):
        self.moving.wait_recv()
        span = rows_at(self.start, self.size)
        landed = self.recv[self.fills : self.fills + self.size, :]
        total = self.acc[span, :].astype(F32) + landed.astype(F32)
        self.acc[span, :] = total.astype(BF16)
        self.fills += self.size

    def turn(self):
        span = rows_at(self.start, self.size)
        self.out[span, :] = self.acc[span, :]

    def send_whole(self):
        start, size, other = self.trail.pop()
        here = self.out.at[rows_at(self.start, self.size), :]
        self.moving = self.wire.start(here, here, {"batch": other})
        self.start, self.size = start, size

    def take_whole(self):
        self.moving.wait_recv()


def solution(mesh):
    batch_size = mesh.shape["batch"]
    assert mesh.shape["mp"] == 4

    def shards(
        block_input,
        first_values,
        norm1_gain,
        norm1_bias,
        query_weight,
        key_weight,
        value_weight,
        out_weight,
        norm2_gain,
        norm2_bias,
        up_weight,
        down_weight,
        out_grad,
        doc_lengths,
    ):
        rows, width = block_input.shape
        cols = query_weight.shape[1]
        hid = up_weight.shape[1]
        half_width = value_weight.shape[1]
        docs = doc_lengths.shape[1]
        seg = rows // 2
        own = rows // 4
        assert seg == min(rows, CONTEXT)


        def project(normed, w, q, k):
            q[...] = mm(normed, w[:cols, :], NT).astype(BF16)
            k[...] = mm(normed, w[cols : 2 * cols, :], NT).astype(BF16)

        def head_kernel(
            lengths,
            x,
            og,
            fv,
            g1,
            b1,
            g2,
            b2,
            wq,
            wk,
            wo,
            wv,
            wu_hbm,
            wd_hbm,
            n1_hbm,
            qo_hbm,
            ko_hbm,
            vo_hbm,
            mo_hbm,
            lo_hbm,
            qf_hbm,
            kf_hbm,
            vf_hbm,
            mf_hbm,
            lf_hbm,
            w_far_hbm,
            through_hbm,
            da_hbm,
            bo_part_hbm,
            feed_far_hbm,
            w_grads_hbm,
            vec,
            bias,
            wu,
            wd,
            n1,
            qo,
            ko,
            vo,
            mo,
            lo,
            qf,
            kf,
            vf,
            mf,
            lf,
            w_far,
            through,
            da,
            bo_part,
            feed_far,
            w_grads,
            x_seg,
            fv_seg,
            n2,
            og2,
            act,
            dup,
            wu_sib,
            wd_sib,
            att_send,
            att_recv,
            dn2_own,
            dn2_send,
            dn2_recv,
            g_send,
            g_recv,
            send_sems,
            recv_sems,
            local_sems,
        ):
            me = lax.axis_index("mp")
            sibling, core = flipped(me, 1)
            across, chip = flipped(me, 2)
            to_sib, to_far = {"mp": sibling}, {"mp": across}
            wire = Wire(send_sems, recv_sems)
            weight_loads = [
                pltpu.make_async_copy(wu_hbm, wu, local_sems.at[4]),
                pltpu.make_async_copy(wd_hbm, wd, local_sems.at[5]),
            ]
            stores = []

            def store(source, target):
                stores.append(
                    pltpu.make_async_copy(source, target, local_sems.at[6 + len(stores)])
                )
                stores[-1].start()

            loads = []
            for source, rows_from, count, target in (
                (x, chip * seg, seg, x_seg),
                (fv, chip * seg, seg, fv_seg),
                (og, me * own, own, og2.at[pl.ds(0, own), :]),
                (og, across * own, own, og2.at[pl.ds(own, own), :]),
            ):
                load = pltpu.make_async_copy(
                    source.at[rows_at(rows_from, count), :], target, local_sems.at[len(loads)]
                )
                load.start()
                loads.append(load)
            for load in weight_loads:
                load.start()
            greet([to_sib, to_far])
            swaps = [
                wire.start(w, w_far.at[pl.ds(i * cols, cols), :], to_far)
                for i, w in enumerate((wq, wk))
            ]
            up_swap = wire.start(wu_hbm, wu_sib, to_sib)
            down_swap = wire.start(wd_hbm, wd_sib, to_sib)
            scalars = (chip, core, *[lengths[i] for i in range(docs)])
            fill_bias(scalars, bias, seg, docs)
            for load in loads:
                load.wait()

            hat, _ = normalise(x_seg[...].astype(F32))
            normed = (hat * g1[...][None] + b1[...][None]).astype(BF16)
            n1[...] = normed
            qo[...] = mm(normed, wq[...], NT).astype(BF16)
            ko[...] = mm(normed, wk[...], NT).astype(BF16)
            value_cols = jnp.where(core == 0, wv[:, :cols], wv[:, cols : 2 * cols])
            fresh = mm(normed, value_cols).astype(BF16)
            reused = jnp.where(core == 0, fv_seg[:, :cols], fv_seg[:, cols : 2 * cols])
            vo[...] = jnp.where(chip == 0, fresh, reused)
            vf[...] = jnp.where(chip == 0, reused, fresh)
            for name in ((n1, n1_hbm), (qo, qo_hbm), (ko, ko_hbm), (vo, vo_hbm), (vf, vf_hbm)):
                store(*name)
            attention_forward(bias, qo, ko, vo, mo, lo, seg, cols)
            store(mo, mo_hbm)
            store(lo, lo_hbm)
            swaps[0].wait_recv()
            swaps[1].wait_recv()
            out_swap = wire.start(wo, w_far.at[pl.ds(2 * cols, cols), :], to_far)
            project(n1[...], w_far, qf, kf)
            store(qf, qf_hbm)
            store(kf, kf_hbm)
            attention_forward(bias, qf, kf, vf, mf, lf, seg, cols)
            store(mf, mf_hbm)
            store(lf, lf_hbm)
            out_swap.wait_recv()
            store(w_far, w_far_hbm)

            def out_part(start):
                span = rows_at(start, own)
                left = mm(mo[span, :], wo[...]).astype(BF16).astype(F32)
                right = mm(mf[span, :], w_far[2 * cols :, :]).astype(BF16).astype(F32)
                return (left + right).astype(BF16)

            att_send[...] = out_part((1 - core) * own)
            att_swap = wire.start(att_send, att_recv, to_sib)
            kept = out_part(core * own)
            att_swap.wait_recv()
            attention = kept.astype(F32) + att_recv[...].astype(F32)
            bo_part[...] = attention
            hidden = x_seg[rows_at(core * own, own), :].astype(F32) + attention
            chunk = own // 2
            n2_swaps = []
            for part in range(2):
                span = slice(part * chunk, (part + 1) * chunk)
                hat, _ = normalise(hidden[span])
                n2[span, :] = (hat * g2[...][None] + b2[...][None]).astype(BF16)
                n2_swaps.append(
                    wire.start(
                        n2.at[pl.ds(part * chunk, chunk), :],
                        n2.at[pl.ds(own + part * chunk, chunk), :],
                        to_far,
                    )
                )
            through[...] = hidden
            up_swap.wait_recv()
            down_swap.wait_recv()
            for load in weight_loads:
                load.wait()

            def mlp(start, count):
                span = slice(start, start + count)
                step = min(hid, 256)
                for at, (up_w, down_w) in enumerate(((wu, wd), (wu_sib, wd_sib))):
                    for tile in range(hid // step):
                        part = slice(tile * step, (tile + 1) * step)
                        place = slice(at * hid + tile * step, at * hid + (tile + 1) * step)
                        up = mm(n2[span, :], up_w[:, part])
                        back = mm(og2[span, :], down_w[part, :], NT)
                        square = up * up
                        slope = jnp.tanh(GELU_C * up * (1.0 + GELU_A * square))
                        bell = 0.5 * (1.0 + slope)
                        act[span, place] = (up * bell).astype(BF16)
                        inner = GELU_C * (1.0 + 3.0 * GELU_A * square)
                        deriv = bell + 0.5 * up * (1.0 - slope * slope) * inner
                        dup[span, place] = (back * deriv).astype(BF16)
                total = mm(dup[span, :hid], wu[...], NT)
                return total + mm(dup[span, hid:], wu_sib[...], NT)

            def feed(start, count):
                span = slice(start, start + count)
                return mm(act[span, :hid], wd[...]) + mm(act[span, hid:], wd_sib[...])

            dn2_own[...] = mlp(0, own).astype(BF16)
            bo_part[...] += feed(0, own)
            store(bo_part, bo_part_hbm)
            dn2_swaps = []
            for part in range(2):
                n2_swaps[part].wait_recv()
                span = slice(part * chunk, (part + 1) * chunk)
                dn2_send[span, :] = mlp(own + part * chunk, chunk).astype(BF16)
                block = pl.ds(part * chunk, chunk)
                dn2_swaps.append(wire.start(dn2_send.at[block, :], dn2_recv.at[block, :], to_far))
            g_send[:hid, :] = mm(act[:, hid:], og2[...], TN).astype(BF16)
            g_send[hid:, :] = mm(n2[...], dup[:, hid:], TN).astype(BF16)
            g_swap = wire.start(g_send, g_recv, to_sib)
            feed_far[...] = feed(own, own).astype(BF16)
            store(feed_far, feed_far_hbm)
            down_own = mm(act[:, :hid], og2[...], TN)
            up_own = mm(n2[...], dup[:, :hid], TN)
            g_swap.wait_recv()
            w_grads[:hid, :] = (down_own + g_recv[:hid, :].astype(F32)).astype(BF16)
            w_grads[hid:, :] = (up_own + g_recv[hid:, :].astype(F32)).astype(BF16)
            store(w_grads, w_grads_hbm)

            for swap in dn2_swaps:
                swap.wait_recv()
            d_norm = dn2_own[...].astype(F32) + dn2_recv[...].astype(F32)
            back, d_gain, d_bias = norm_backward(d_norm, through[...], g2[...][None])
            through[...] = back
            da[...] = (og2[:own, :].astype(F32) + back).astype(BF16)
            store(through, through_hbm)
            store(da, da_hbm)
            vec[...] = jnp.concatenate([d_gain, d_bias, jnp.zeros((6, width), F32)], axis=0)
            for moving in stores:
                moving.wait()
            wire.drain()

        def norm_backward(d_norm, values, gain):
            hat, inverse = normalise(values)
            d_gain = jnp.sum(d_norm * hat, axis=0, keepdims=True)
            d_bias = jnp.sum(d_norm, axis=0, keepdims=True)
            scaled = d_norm * gain
            mean1 = jnp.mean(scaled, axis=-1, keepdims=True)
            mean2 = jnp.mean(scaled * hat, axis=-1, keepdims=True)
            return (scaled - mean1 - hat * mean2) * inverse, d_gain, d_bias

        vm = pl.BlockSpec(memory_space=pltpu.VMEM)
        hbm = pl.BlockSpec(memory_space=pl.ANY)
        smem = pl.BlockSpec(memory_space=pltpu.SMEM)
        attn_flops = 2 * 2 * seg * seg * cols * 4
        query_rows, key_rows = query_weight.T, key_weight.T
        heads_of_shard = [*[sds((seg, cols), BF16)] * 4, sds((seg, 2 * HEAD), F32)]
        shard_scratch = [*[pltpu.VMEM((seg, cols), BF16)] * 4, pltpu.VMEM((seg, 2 * HEAD), F32)]
        n_head_copies = 16
        (
            n1,
            q_own,
            k_own,
            v_own,
            mixed_own,
            lse_own,
            q_far,
            k_far,
            v_far,
            mixed_far,
            lse_far,
            w_far,
            through,
            d_att,
            bo_part,
            feed_far,
            w_grads,
            vec2,
        ) = pl.pallas_call(
            head_kernel,
            name="head",
            out_shape=[
                sds((seg, width), BF16),
                *heads_of_shard,
                *heads_of_shard,
                sds((3 * cols, width), BF16),
                sds((own, width), F32),
                sds((own, width), BF16),
                sds((own, width), F32),
                sds((own, width), BF16),
                sds((2 * hid, width), BF16),
                sds((8, width), F32),
            ],
            in_specs=[smem, hbm, hbm, hbm, *[vm] * 8, hbm, hbm],
            out_specs=[*[hbm] * 17, vm],
            scratch_shapes=[
                pltpu.VMEM((seg, seg), F32),
                pltpu.VMEM((width, hid), BF16),
                pltpu.VMEM((hid, width), BF16),
                pltpu.VMEM((seg, width), BF16),
                *shard_scratch,
                *shard_scratch,
                pltpu.VMEM((3 * cols, width), BF16),
                pltpu.VMEM((own, width), F32),
                pltpu.VMEM((own, width), BF16),
                pltpu.VMEM((own, width), F32),
                pltpu.VMEM((own, width), BF16),
                pltpu.VMEM((2 * hid, width), BF16),
                pltpu.VMEM((seg, width), BF16),
                pltpu.VMEM((seg, half_width), BF16),
                pltpu.VMEM((2 * own, width), BF16),
                pltpu.VMEM((2 * own, width), BF16),
                pltpu.VMEM((2 * own, 2 * hid), BF16),
                pltpu.VMEM((2 * own, 2 * hid), BF16),
                pltpu.VMEM((width, hid), BF16),
                pltpu.VMEM((hid, width), BF16),
                *[pltpu.VMEM((own, width), BF16)] * 5,
                pltpu.VMEM((2 * hid, width), BF16),
                pltpu.VMEM((2 * hid, width), BF16),
                pltpu.SemaphoreType.DMA((n_head_copies,)),
                pltpu.SemaphoreType.DMA((n_head_copies,)),
                pltpu.SemaphoreType.DMA((6 + 17,)),
            ],
            cost_estimate=pl.CostEstimate(
                flops=attn_flops * 8, bytes_accessed=30000000, transcendentals=0
            ),
            compiler_params=pltpu.CompilerParams(
                collective_id=1, has_side_effects=True, vmem_limit_bytes=HEAD_VMEM
            ),
        )(
            doc_lengths[0],
            block_input,
            out_grad,
            first_values,
            norm1_gain,
            norm1_bias,
            norm2_gain,
            norm2_bias,
            query_rows,
            key_rows,
            out_weight,
            value_weight,
            up_weight,
            down_weight,
        )

        bits = [1 << i for i in range(batch_size.bit_length() - 1)]
        assert 1 << len(bits) == batch_size and len(bits) >= 2
        granule = 16 * batch_size
        a_count = 2 if 2 * cols % granule == 0 else 1
        a_stream = -(-4 * cols // a_count // granule) * granule
        a_rows = a_count * a_stream
        orders = (bits, bits[1:] + bits[:1])
        w_count = 4 if hid % (2 * granule // 4) == 0 else 1
        w_stream = -(-2 * hid // w_count // granule) * granule
        w_rows = w_count * w_stream
        n_copies = 24 + (6 + 2 * w_count) * len(bits)

        def attention_backward(bias, wo, mixed, lse, q, k, v, da, dm, dkt, dvt, dq, dk, dv, tick):
            dm[...] = mm(da[...], wo, NT).astype(BF16)
            dkt[...] = jnp.zeros_like(dkt)
            dvt[...] = jnp.zeros_like(dvt)
            lane = lax.broadcasted_iota(jnp.int32, (QROWS, 2 * HEAD), 1)
            for block in range(seg // QROWS):
                low, keys = block * QROWS, (block + 1) * QROWS
                held = None
                for head, (first, last, half) in enumerate(head_parts(cols)):
                    query = pick(q[low:keys, first:last], half) * jnp.asarray(SCALE, BF16)
                    grad = pick(dm[low:keys, first:last], half)
                    scores = mm(query, k[:keys, first:last], NT) + bias[low:keys, :keys]
                    weights = jnp.exp(scores - lse[low:keys, head : head + 1])
                    d_weights = mm(grad, v[:keys, first:last], NT)
                    inner = jnp.sum(
                        grad.astype(F32) * mixed[low:keys, first:last].astype(F32),
                        axis=-1,
                        keepdims=True,
                    )
                    d_scores = (weights * (d_weights - inner)).astype(BF16)
                    dvt[:keys, first:last] += mm(weights.astype(BF16), grad, TN)
                    dkt[:keys, first:last] += mm(d_scores, query, TN)
                    d_query = mm(d_scores, k[:keys, first:last]) * SCALE
                    tick(1)
                    if half == 0:
                        held = d_query
                    elif half == 1:
                        both = jnp.where(lane < HEAD, held, d_query)
                        dq[low:keys, first:last] = both.astype(BF16)
                    else:
                        dq[low:keys, first:last] = d_query.astype(BF16)
            dk[...] = dkt[...].astype(BF16)
            dv[...] = dvt[...].astype(BF16)

        def tail_kernel(
            lengths,
            x,
            og,
            through_hbm,
            da_own,
            bo_part_hbm,
            feed_far,
            vec2,
            g1,
            wq_hbm,
            wk_hbm,
            wo_hbm,
            w_far_hbm,
            wv_hbm,
            n1_hbm,
            w_grads,
            mo_hbm,
            lo_hbm,
            qo_hbm,
            ko_hbm,
            vo_hbm,
            mf_hbm,
            lf_hbm,
            qf_hbm,
            kf_hbm,
            vf_hbm,
            bo_all,
            ig_all,
            fv_out,
            total,
            w_total,
            value_out,
            vec,
            bias,
            through,
            bo_part,
            wq,
            wk,
            wo,
            w_far,
            wv,
            n1,
            mo,
            lo,
            qo,
            ko,
            vo,
            mf,
            lf,
            qf,
            kf,
            vf,
            x_here,
            og_here,
            fv_all,
            v_total,
            da,
            dm,
            dkt,
            dvt,
            dqo,
            dko,
            dvo,
            dqf,
            dkf,
            dvf,
            fresh,
            g_send,
            g_recv,
            v_recv,
            dn_send,
            dn_recv,
            feed_recv,
            acc,
            landing,
            w_acc,
            w_landing,
            vec_send,
            vec_recv,
            send_sems,
            recv_sems,
            local_sems,
        ):
            me = lax.axis_index("mp")
            row = lax.axis_index("batch")
            sibling, core = flipped(me, 1)
            across, chip = flipped(me, 2)
            to_sib, to_far = {"mp": sibling}, {"mp": across}
            wire = Wire(send_sems, recv_sems)
            here = rows_at(me * own, own)
            there = rows_at(across * own, own)
            mine = rows_at(core * own, own)
            loads = {}

            def load(name, source, target):
                loads[name] = pltpu.make_async_copy(source, target, local_sems.at[len(loads)])
                loads[name].start()

            load("da", da_own, da.at[mine, :])
            load("w", w_grads, w_acc.at[pl.ds(0, 2 * hid), :])
            load("w_far", w_far_hbm, w_far)
            load("qf", qf_hbm, qf)
            load("kf", kf_hbm, kf)
            load("vf", vf_hbm, vf)
            load("mf", mf_hbm, mf)
            load("lf", lf_hbm, lf)
            load("n1", n1_hbm, n1)
            load("wo", wo_hbm, wo)
            load("qo", qo_hbm, qo)
            load("ko", ko_hbm, ko)
            load("vo", vo_hbm, vo)
            load("mo", mo_hbm, mo)
            load("lo", lo_hbm, lo)
            load("wq", wq_hbm, wq)
            load("wk", wk_hbm, wk)
            load("wv", wv_hbm, wv)
            load("through", through_hbm, through)
            load("bo_part", bo_part_hbm, bo_part)
            load("x", x.at[here, :], x_here)
            load("og", og.at[here, :], og_here)

            def loaded(*which):
                for name in which or tuple(loads):
                    loads.pop(name).wait()

            greet([to_sib, to_far, *[{"batch": flipped(row, bit)[0]} for bit in bits]])
            feed_swap = wire.start(feed_far, feed_recv, to_far)
            da_swap = wire.start(da_own, da.at[mine, :], to_sib)
            if w_rows > 2 * hid:
                w_acc[2 * hid :, :] = jnp.zeros((w_rows - 2 * hid, width), BF16)
            loaded("w")
            w_streams = [
                Reduction(
                    wire, row, bits, w_acc, w_total, w_landing, i * w_stream, w_stream
                )
                for i in range(w_count)
            ]
            for one in w_streams:
                one.send_half(0)
            fill_bias((chip, core, *[lengths[i] for i in range(docs)]), bias, seg, docs)
            loaded("da", "w_far", "qf", "kf", "vf", "mf", "lf")
            da_swap.wait_recv()

            agenda = []
            last_step = len(bits) - 1

            def halve(one, step):
                one.add_half()
                if step < last_step:
                    one.send_half(step + 1)
                else:
                    one.turn()
                    one.send_whole()

            def double(one, step):
                one.take_whole()
                if step < last_step:
                    one.send_whole()

            for at, one in enumerate(w_streams):
                due = 8 + 7 * at
                for step in range(len(bits)):
                    agenda.append((due, at, functools.partial(halve, one, step)))
                    due += 5
                for step in range(len(bits)):
                    agenda.append((due, at, functools.partial(double, one, step)))
                    due += 5 if step < last_step - 1 else 8
            bo_near, bo_far, bo_diag = [], [], []

            def send_out(part):
                if part == 0:
                    feed_swap.wait_recv()
                    out = bo_part[...] + feed_recv[...].astype(F32) + x_here[...].astype(F32)
                    bo_all[here, :] = out.astype(BF16)
                    bo_near.append(wire.start(bo_all.at[here, :], bo_all.at[here, :], to_sib))
                block = rows_at(me * own + part * (own // 2), own // 2)
                bo_far.append(wire.start(bo_all.at[block, :], bo_all.at[block, :], to_far))

            def pass_out(part):
                bo_far[part].wait_recv()
                block = rows_at(across * own + part * (own // 2), own // 2)
                bo_diag.append(wire.start(bo_all.at[block, :], bo_all.at[block, :], to_sib))

            agenda.sort(key=lambda item: item[:2])
            clock = [0]

            def tick(count):
                clock[0] += count
                while agenda and agenda[0][0] <= clock[0]:
                    agenda.pop(0)[2]()

            far_out = w_far[2 * cols :, :]
            attention_backward(
                bias, far_out, mf, lf, qf, kf, vf, da, dm, dkt, dvt, dqf, dkf, dvf, tick
            )
            loaded()
            g_send[:cols, :] = mm(dqf[...], n1[...], TN).astype(BF16)
            g_send[cols : 2 * cols, :] = mm(dkf[...], n1[...], TN).astype(BF16)
            g_send[2 * cols :, :] = mm(mf[...], da[...], TN).astype(BF16)
            g_swap = wire.start(g_send, g_recv, to_far)
            attention_backward(
                bias, wo[...], mo, lo, qo, ko, vo, da, dm, dkt, dvt, dqo, dko, dvo, tick
            )

            low_chip = chip == 0
            fresh[...] = jnp.where(low_chip, dvo[...], dvf[...])
            reused = jnp.where(low_chip, dvf[...], dvo[...])
            fv_all[pl.ds(me, 1)] = jnp.concatenate([reused[:own], reused[own:]], axis=1)[None]
            value_cols = jnp.where(core == 0, wv[:, :cols], wv[:, cols : 2 * cols])

            def dn1_part(start):
                span = rows_at(start, own)
                part = mm(dqo[span, :], wq[...])
                part = part + mm(dko[span, :], wk[...])
                part = part + mm(dqf[span, :], w_far[:cols, :])
                part = part + mm(dkf[span, :], w_far[cols : 2 * cols, :])
                return (part + mm(fresh[span, :], value_cols, NT)).astype(BF16)

            dn_send[...] = dn1_part((1 - core) * own)
            dn_swap = wire.start(dn_send, dn_recv, to_sib)
            tick(2)
            acc[3 * cols : 4 * cols, :] = mm(fresh[...], n1[...], TN).astype(BF16)
            kept = dn1_part(core * own).astype(F32)
            tick(2)
            dn_swap.wait_recv()
            d_norm = kept + dn_recv[...].astype(F32)
            back, d_gain1, d_bias1 = norm_backward(
                d_norm, x_here[...].astype(F32), g1[...][None]
            )
            ig_all[here, :] = (og_here[...].astype(F32) + back + through[...]).astype(BF16)
            ig_far = wire.start(ig_all.at[here, :], ig_all.at[here, :], to_far)
            ig_near = wire.start(ig_all.at[here, :], ig_all.at[here, :], to_sib)
            fv_mine, fv_there = fv_all.at[pl.ds(me, 1)], fv_all.at[pl.ds(across, 1)]
            fv_near = wire.start(fv_mine, fv_mine, to_sib)
            tick(4)

            acc[:cols, :] = mm(dqo[...], n1[...], TN).astype(BF16)
            acc[cols : 2 * cols, :] = mm(dko[...], n1[...], TN).astype(BF16)
            acc[2 * cols : 3 * cols, :] = mm(mo[...], da[...], TN).astype(BF16)
            if a_rows > 4 * cols:
                acc[4 * cols :, :] = jnp.zeros((a_rows - 4 * cols, width), BF16)
            tick(3)
            g_swap.wait_recv()
            shared = acc[: 3 * cols, :].astype(F32) + g_recv[...].astype(F32)
            acc[: 3 * cols, :] = shared.astype(BF16)

            ranks = [to_sib, to_far, *[{"batch": flipped(row, bit)[0]} for bit in bits]]
            vec_send[0] = jnp.concatenate(
                [d_gain1, d_bias1, vec2[:2, :], jnp.zeros((4, width), F32)], axis=0
            )
            streams = [
                Reduction(wire, row, orders[i], acc, total, landing, i * a_stream, a_stream)
                for i in range(a_count)
            ]

            def vector_step(at):
                if at < len(ranks):
                    return wire.start(vec_send.at[at], vec_recv.at[at], ranks[at])
                return None

            def vector_add(at, moving):
                if moving is not None:
                    moving.wait_recv()
                    vec_send[at + 1] = vec_send[at] + vec_recv[at]

            for step in range(len(bits)):
                for one in streams:
                    one.send_half(step)
                moving = vector_step(step)
                tick(4)
                if step == 1:
                    send_out(0)
                for one in streams:
                    one.add_half()
                vector_add(step, moving)
            last = streams[-1]
            v_span = rows_at(last.start, last.size)
            v_swap = wire.start(acc.at[v_span, :], v_recv, to_far)
            for one in streams[:-1]:
                one.turn()
                one.send_whole()
            v_swap.wait_recv()
            fv_far = wire.start(fv_mine, fv_mine, to_far)
            at_row = last.start + lax.broadcasted_iota(jnp.int32, (last.size, 1), 0)
            is_value = (at_row >= 3 * cols) & (at_row < 4 * cols)
            other = jnp.where(is_value, v_recv[...].astype(F32), 0.0)
            total[v_span, :] = (acc[v_span, :].astype(F32) + other).astype(BF16)
            last.send_whole()
            for step in range(len(bits)):
                if step > 0:
                    for one in streams:
                        one.send_whole()
                moving = vector_step(len(bits) + step)
                tick(5)
                if step == 0:
                    ig_far.wait_recv()
                    ig_diag = wire.start(ig_all.at[there, :], ig_all.at[there, :], to_sib)
                    send_out(1)
                for one in streams:
                    one.take_whole()
                if step == 0:
                    pass_out(0)
                vector_add(len(bits) + step, moving)
            tick(1000)
            vec[...] = vec_send[len(ranks)]

            v_rows = total.at[pl.ds(3 * cols, cols), :]
            half = rows_at(core * cols, cols)
            v_near = wire.start(v_rows, v_total.at[half, :], to_sib)
            v_total[half, :] = total[3 * cols : 4 * cols, :]
            fv_far.wait_recv()
            fv_diag = wire.start(fv_there, fv_there, to_sib)
            v_near.wait_recv()
            value_out[...] = v_total[...].astype(F32).T.astype(BF16)
            fv_near.wait_recv()
            fv_diag.wait_recv()
            for part in range(rows // own):
                first = part // 2 * 2
                lanes = slice(part % 2 * cols, (part % 2 + 1) * cols)
                fv_out[part * own : (part + 1) * own, :] = jnp.concatenate(
                    [fv_all[first][:, lanes], fv_all[first + 1][:, lanes]], axis=1
                )
            pass_out(1)
            for moving in (*bo_near, *bo_diag, ig_near, ig_diag):
                moving.wait_recv()
            wire.drain()

        tail_args = (
            doc_lengths[0],
            block_input,
            out_grad,
            through,
            d_att,
            bo_part,
            feed_far,
            vec2,
            norm1_gain,
            query_rows,
            key_rows,
            out_weight,
            w_far,
            value_weight,
            n1,
            w_grads,
            mixed_own,
            lse_own,
            q_own,
            k_own,
            v_own,
            mixed_far,
            lse_far,
            q_far,
            k_far,
            v_far,
        )
        bo_all, ig_all, fv_out, attn_sum, w_total, value_out, vectors = pl.pallas_call(
            tail_kernel,
            name="tail",
            out_shape=[
                pltpu.VMEM((rows, width), BF16),
                pltpu.VMEM((rows, width), BF16),
                pltpu.VMEM((rows, half_width), BF16),
                pltpu.VMEM((a_rows, width), BF16),
                pltpu.VMEM((w_rows, width), BF16),
                pltpu.VMEM((width, half_width), BF16),
                pltpu.VMEM((8, width), F32),
            ],
            in_specs=[smem, *[hbm] * 6, vm, vm, *[hbm] * 17],
            out_specs=[vm] * 7,
            scratch_shapes=[
                pltpu.VMEM((seg, seg), F32),
                pltpu.VMEM((own, width), F32),
                pltpu.VMEM((own, width), F32),
                pltpu.VMEM((cols, width), BF16),
                pltpu.VMEM((cols, width), BF16),
                pltpu.VMEM((cols, width), BF16),
                pltpu.VMEM((3 * cols, width), BF16),
                pltpu.VMEM((width, half_width), BF16),
                pltpu.VMEM((seg, width), BF16),
                pltpu.VMEM((seg, cols), BF16),
                pltpu.VMEM((seg, 2 * HEAD), F32),
                pltpu.VMEM((seg, cols), BF16),
                pltpu.VMEM((seg, cols), BF16),
                pltpu.VMEM((seg, cols), BF16),
                pltpu.VMEM((seg, cols), BF16),
                pltpu.VMEM((seg, 2 * HEAD), F32),
                pltpu.VMEM((seg, cols), BF16),
                pltpu.VMEM((seg, cols), BF16),
                pltpu.VMEM((seg, cols), BF16),
                pltpu.VMEM((own, width), BF16),
                pltpu.VMEM((own, width), BF16),
                pltpu.VMEM((4, own, 2 * cols), BF16),
                pltpu.VMEM((2 * cols, width), BF16),
                pltpu.VMEM((seg, width), BF16),
                pltpu.VMEM((seg, cols), BF16),
                pltpu.VMEM((seg, cols), F32),
                pltpu.VMEM((seg, cols), F32),
                *[pltpu.VMEM((seg, cols), BF16)] * 7,
                pltpu.VMEM((3 * cols, width), BF16),
                pltpu.VMEM((3 * cols, width), BF16),
                pltpu.VMEM((a_stream // batch_size, width), BF16),
                pltpu.VMEM((own, width), BF16),
                pltpu.VMEM((own, width), BF16),
                pltpu.VMEM((own, width), BF16),
                pltpu.VMEM((a_rows, width), BF16),
                pltpu.VMEM((a_rows, width), BF16),
                pltpu.VMEM((w_rows, width), BF16),
                pltpu.VMEM((w_rows, width), BF16),
                pltpu.VMEM((len(bits) + 3, 8, width), F32),
                pltpu.VMEM((len(bits) + 2, 8, width), F32),
                pltpu.SemaphoreType.DMA((n_copies,)),
                pltpu.SemaphoreType.DMA((n_copies,)),
                pltpu.SemaphoreType.DMA((22,)),
            ],
            cost_estimate=pl.CostEstimate(
                flops=attn_flops * 12, bytes_accessed=30000000, transcendentals=0
            ),
            compiler_params=pltpu.CompilerParams(
                collective_id=0, has_side_effects=True, vmem_limit_bytes=TAIL_VMEM
            ),
        )(*tail_args)
        block_out, input_grad = bo_all.astype(F32), ig_all.astype(F32)
        first_values_grad, value_grad = fv_out.astype(F32), value_out.astype(F32)
        query_grad = attn_sum[:cols].astype(F32).T
        key_grad = attn_sum[cols : 2 * cols].astype(F32).T
        out_sum = attn_sum[2 * cols : 3 * cols].astype(F32)
        down_grad, up_grad = w_total[:hid].astype(F32), w_total[hid : 2 * hid].astype(F32)
        return (
            block_out,
            input_grad,
            first_values_grad,
            vectors[0],
            vectors[1],
            query_grad,
            key_grad,
            value_grad,
            out_sum,
            vectors[2],
            vectors[3],
            up_grad,
            down_grad,
        )

    return jax.shard_map(
        shards,
        mesh=mesh,
        in_specs=(
            P("batch", None),
            P("batch", None),
            P(),
            P(),
            P(None, "mp"),
            P(None, "mp"),
            P(),
            P("mp", None),
            P(),
            P(),
            P(None, "mp"),
            P("mp", None),
            P("batch", None),
            P("batch", None),
        ),
        out_specs=(
            P("batch", None),
            P("batch", None),
            P("batch", None),
            P(),
            P(),
            P(None, "mp"),
            P(None, "mp"),
            P(),
            P("mp", None),
            P(),
            P(),
            P(None, "mp"),
            P("mp", None),
        ),
        check_vma=False,
    )
```

```python
import functools

import jax
import jax.numpy as jnp
from jax import lax
from jax.experimental import pallas as pl
from jax.experimental.pallas import tpu as pltpu
from jax.sharding import PartitionSpec as P

HEAD = 64
CONTEXT = 1024
EPS = 1e-05
MASKED = -1e30
QROWS = 256
SCALE = HEAD ** (-0.5)
GELU_C = 0.7978845608028654
GELU_A = 0.044715

F32 = jnp.float32
BF16 = jnp.bfloat16
HEAD_VMEM = 60 * 1024 * 1024
TAIL_VMEM = 50 * 1024 * 1024

NN = (((1,), (0,)), ((), ()))
NT = (((1,), (1,)), ((), ()))
TN = (((0,), (0,)), ((), ()))


def mm(left, right, dims=NN):
    return lax.dot_general(left, right, dims, preferred_element_type=F32)


def normalise(values):
    average = jnp.mean(values, axis=-1, keepdims=True)
    centred = values - average
    variance = jnp.mean(centred * centred, axis=-1, keepdims=True)
    inverse = lax.rsqrt(variance + EPS)
    return centred * inverse, inverse


def sds(shape, dtype):
    return jax.ShapeDtypeStruct(shape, dtype)


def fill_bias(s_ref, bias_ref, seg, docs):
    base = s_ref[0] * seg
    for block in range(seg // QROWS):
        low, keys = block * QROWS, (block + 1) * QROWS
        row = lax.broadcasted_iota(jnp.int32, (QROWS, 1), 0) + low
        start = jnp.zeros((QROWS, 1), jnp.int32)
        end = jnp.int32(0)
        for doc in range(docs):
            end = end + s_ref[2 + doc]
            rel = end - base
            start = jnp.maximum(start, jnp.where(rel <= row, rel, 0))
        col = lax.broadcasted_iota(jnp.int32, (QROWS, keys), 1)
        seen = (col >= start) & (col <= row)
        bias_ref[low:keys, :keys] = jnp.where(seen, 0.0, MASKED)


def head_parts(width):
    parts = []
    for head in range(width // HEAD):
        pair = head // 2 * 2 * HEAD
        if pair + 2 * HEAD <= width:
            parts.append((pair, pair + 2 * HEAD, head % 2))
        else:
            parts.append((pair, pair + HEAD, None))
    return parts


def pick(values, half):
    if half is None:
        return values
    lane = lax.broadcasted_iota(jnp.int32, values.shape, 1)
    keep = (lane < HEAD) if half == 0 else (lane >= HEAD)
    return jnp.where(keep, values, jnp.zeros_like(values))


def attention_forward(bias_ref, q_ref, k_ref, v_ref, mixed_ref, lse_ref, seg, heads):
    lane = lax.broadcasted_iota(jnp.int32, (QROWS, 2 * HEAD), 1)
    for block in range(seg // QROWS):
        low, keys = block * QROWS, (block + 1) * QROWS
        held = None
        stats = []
        for _, (first, last, half) in heads:
            query = pick(q_ref[low:keys, first:last], half) * jnp.asarray(SCALE, BF16)
            scores = mm(query, k_ref[:keys, first:last], NT) + bias_ref[low:keys, :keys]
            highest = jnp.max(scores, axis=-1, keepdims=True)
            weights = jnp.exp(scores - highest)
            total = jnp.sum(weights, axis=-1, keepdims=True)
            mixed = mm(weights.astype(BF16), v_ref[:keys, first:last]) / total
            stats.append(highest + jnp.log(total))
            if half == 0:
                held = mixed
            elif half == 1:
                both = jnp.where(lane < HEAD, held, mixed)
                mixed_ref[low:keys, first:last] = both.astype(BF16)
            else:
                mixed_ref[low:keys, first:last] = mixed.astype(BF16)
        for (head, _), stat in zip(heads, stats):
            lse_ref[low:keys, head : head + 1] = stat


MESH = pl.DeviceIdType.MESH


def flipped(index, bit):
    digit = lax.rem(lax.div(index, jnp.int32(bit)), jnp.int32(2))
    return index + bit - 2 * bit * digit, digit


class Wire:
    def __init__(self, send, recv):
        self.send, self.recv, self.used, self.sent = send, recv, 0, []

    def copy(self, src, dst, device):
        at = self.used
        self.used += 1
        return pltpu.make_async_remote_copy(
            src_ref=src,
            dst_ref=dst,
            send_sem=self.send.at[at],
            recv_sem=self.recv.at[at],
            device_id=device,
            device_id_type=MESH,
        )

    def start(self, src, dst, device):
        moving = self.copy(src, dst, device)
        moving.start()
        self.sent.append(moving)
        return moving

    def drain(self):
        for moving in self.sent:
            moving.wait_send()


def rows_at(start, count):
    return pl.ds(pl.multiple_of(start, 16), count)


def greet(devices):
    barrier = pltpu.get_barrier_semaphore()
    for device in devices:
        pl.semaphore_signal(barrier, inc=1, device_id=device, device_id_type=MESH)
    pl.semaphore_wait(barrier, len(devices))


class Reduction:
    def __init__(self, wire, index, bits, acc, out, recv, base, count):
        self.wire, self.acc, self.out, self.recv = wire, acc, out, recv
        self.base, self.count = base, count
        self.start, self.size = jnp.int32(base), count
        self.fills = base
        self.index, self.bits = index, bits
        self.trail = []

    def send_half(self, step):
        other, digit = flipped(self.index, self.bits[step])
        half = self.size // 2
        keep = self.start + digit * half
        give = self.start + (1 - digit) * half
        land = self.recv.at[pl.ds(self.fills, half), :]
        self.moving = self.wire.start(self.acc.at[rows_at(give, half), :], land, {"batch": other})
        self.trail.append((self.start, self.size, other))
        self.start, self.size = keep, half

    def add_half(self):
        self.moving.wait_recv()
        span = rows_at(self.start, self.size)
        landed = self.recv[self.fills : self.fills + self.size, :]
        total = self.acc[span, :].astype(F32) + landed.astype(F32)
        self.acc[span, :] = total.astype(BF16)
        self.fills += self.size

    def turn(self):
        span = rows_at(self.start, self.size)
        self.out[span, :] = self.acc[span, :]

    def send_whole(self):
        start, size, other = self.trail.pop()
        here = self.out.at[rows_at(self.start, self.size), :]
        self.moving = self.wire.start(here, here, {"batch": other})
        self.start, self.size = start, size

    def take_whole(self):
        self.moving.wait_recv()


def solution(mesh):
    batch_size = mesh.shape["batch"]
    assert mesh.shape["mp"] == 4

    def shards(
        block_input,
        first_values,
        norm1_gain,
        norm1_bias,
        query_weight,
        key_weight,
        value_weight,
        out_weight,
        norm2_gain,
        norm2_bias,
        up_weight,
        down_weight,
        out_grad,
        doc_lengths,
    ):
        rows, width = block_input.shape
        cols = query_weight.shape[1]
        hid = up_weight.shape[1]
        half_width = value_weight.shape[1]
        docs = doc_lengths.shape[1]
        seg = rows // 2
        own = rows // 4
        assert seg == min(rows, CONTEXT)


        bits = [1 << i for i in range(batch_size.bit_length() - 1)]
        assert 1 << len(bits) == batch_size and len(bits) >= 2
        granule = 16 * batch_size
        a_count = 2 if 2 * cols % granule == 0 else 1
        a_stream = -(-4 * cols // a_count // granule) * granule
        a_rows = a_count * a_stream
        orders = (bits, bits[1:] + bits[:1])
        w_count = 4 if hid % (2 * granule // 4) == 0 else 1
        w_stream = -(-2 * hid // w_count // granule) * granule
        w_rows = w_count * w_stream
        n_copies = 24 + (6 + 2 * w_count) * len(bits)

        def head_kernel(
            lengths,
            x,
            og,
            fv,
            g1,
            b1,
            g2,
            b2,
            wq,
            wk,
            wo,
            wv,
            wu_hbm,
            wd_hbm,
            n1_hbm,
            qo_hbm,
            ko_hbm,
            vo_hbm,
            mo_hbm,
            lo_hbm,
            qf_hbm,
            kf_hbm,
            vf_hbm,
            mf_hbm,
            lf_hbm,
            w_far_hbm,
            through_hbm,
            da_hbm,
            bo_part_hbm,
            feed_far_hbm,
            w_grads_hbm,
            vec,
            bias,
            wu,
            wd,
            n1,
            qo,
            ko,
            vo,
            mo,
            lo,
            qf,
            kf,
            vf,
            mf,
            lf,
            w_far,
            through,
            da,
            bo_part,
            feed_far,
            w_grads,
            x_seg,
            fv_seg,
            n2,
            og2,
            act,
            dup,
            wu_sib,
            wd_sib,
            att_send,
            att_recv,
            dn2_own,
            dn2_send,
            dn2_recv,
            g_send,
            g_recv,
            send_sems,
            recv_sems,
            local_sems,
        ):
            me = lax.axis_index("mp")
            sibling, core = flipped(me, 1)
            across, chip = flipped(me, 2)
            to_sib, to_far = {"mp": sibling}, {"mp": across}
            wire = Wire(send_sems, recv_sems)
            weight_loads = [
                pltpu.make_async_copy(wu_hbm, wu, local_sems.at[4]),
                pltpu.make_async_copy(wd_hbm, wd, local_sems.at[5]),
            ]
            stores = []

            def store(source, target):
                stores.append(
                    pltpu.make_async_copy(source, target, local_sems.at[6 + len(stores)])
                )
                stores[-1].start()

            loads = []
            for source, rows_from, count, target in (
                (x, chip * seg, seg, x_seg),
                (fv, chip * seg, seg, fv_seg),
                (og, me * own, own, og2.at[pl.ds(0, own), :]),
                (og, across * own, own, og2.at[pl.ds(own, own), :]),
            ):
                load = pltpu.make_async_copy(
                    source.at[rows_at(rows_from, count), :], target, local_sems.at[len(loads)]
                )
                load.start()
                loads.append(load)
            for load in weight_loads:
                load.start()
            greet([to_sib, to_far])
            cuts = [0, *range(2 * HEAD, cols, 2 * HEAD), cols]
            spans = list(zip(cuts[:-1], cuts[1:]))
            swaps = []
            for low, high in spans:
                for i, w in enumerate((wq, wk)):
                    swaps.append(
                        wire.start(
                            w.at[pl.ds(low, high - low), :],
                            w_far.at[pl.ds(i * cols + low, high - low), :],
                            to_far,
                        )
                    )
            up_swap = wire.start(wu_hbm, wu_sib, to_sib)
            down_swap = wire.start(wd_hbm, wd_sib, to_sib)
            scalars = (chip, core, *[lengths[i] for i in range(docs)])
            fill_bias(scalars, bias, seg, docs)
            for load in loads:
                load.wait()

            hat, _ = normalise(x_seg[...].astype(F32))
            normed = (hat * g1[...][None] + b1[...][None]).astype(BF16)
            n1[...] = normed
            qo[...] = mm(normed, wq[...], NT).astype(BF16)
            ko[...] = mm(normed, wk[...], NT).astype(BF16)
            value_cols = jnp.where(core == 0, wv[:, :cols], wv[:, cols : 2 * cols])
            fresh = mm(normed, value_cols).astype(BF16)
            reused = jnp.where(core == 0, fv_seg[:, :cols], fv_seg[:, cols : 2 * cols])
            vo[...] = jnp.where(chip == 0, fresh, reused)
            vf[...] = jnp.where(chip == 0, reused, fresh)
            for name in ((n1, n1_hbm), (qo, qo_hbm), (ko, ko_hbm), (vo, vo_hbm), (vf, vf_hbm)):
                store(*name)
            heads = list(enumerate(head_parts(cols)))
            attention_forward(bias, qo, ko, vo, mo, lo, seg, heads)
            store(mo, mo_hbm)
            store(lo, lo_hbm)
            out_swap = wire.start(wo, w_far.at[pl.ds(2 * cols, cols), :], to_far)
            for at, (low, high) in enumerate(spans):
                swaps[2 * at].wait_recv()
                swaps[2 * at + 1].wait_recv()
                normed = n1[...]
                qf[:, low:high] = mm(normed, w_far[low:high, :], NT).astype(BF16)
                kf[:, low:high] = mm(normed, w_far[cols + low : cols + high, :], NT).astype(BF16)
                here = [item for item in heads if item[1][0] == low]
                attention_forward(bias, qf, kf, vf, mf, lf, seg, here)
            store(qf, qf_hbm)
            store(kf, kf_hbm)
            store(mf, mf_hbm)
            store(lf, lf_hbm)
            out_swap.wait_recv()
            store(w_far, w_far_hbm)

            def out_part(start):
                span = rows_at(start, own)
                left = mm(mo[span, :], wo[...]).astype(BF16).astype(F32)
                right = mm(mf[span, :], w_far[2 * cols :, :]).astype(BF16).astype(F32)
                return (left + right).astype(BF16)

            att_send[...] = out_part((1 - core) * own)
            att_swap = wire.start(att_send, att_recv, to_sib)
            kept = out_part(core * own)
            att_swap.wait_recv()
            attention = kept.astype(F32) + att_recv[...].astype(F32)
            bo_part[...] = attention
            hidden = x_seg[rows_at(core * own, own), :].astype(F32) + attention
            chunk = own // 2
            n2_swaps = []
            for part in range(2):
                span = slice(part * chunk, (part + 1) * chunk)
                hat, _ = normalise(hidden[span])
                n2[span, :] = (hat * g2[...][None] + b2[...][None]).astype(BF16)
                n2_swaps.append(
                    wire.start(
                        n2.at[pl.ds(part * chunk, chunk), :],
                        n2.at[pl.ds(own + part * chunk, chunk), :],
                        to_far,
                    )
                )
            through[...] = hidden
            up_swap.wait_recv()
            down_swap.wait_recv()
            for load in weight_loads:
                load.wait()

            def mlp(start, count):
                span = slice(start, start + count)
                step = min(hid, 256)
                for at, (up_w, down_w) in enumerate(((wu, wd), (wu_sib, wd_sib))):
                    for tile in range(hid // step):
                        part = slice(tile * step, (tile + 1) * step)
                        place = slice(at * hid + tile * step, at * hid + (tile + 1) * step)
                        up = mm(n2[span, :], up_w[:, part])
                        back = mm(og2[span, :], down_w[part, :], NT)
                        square = up * up
                        slope = jnp.tanh(GELU_C * up * (1.0 + GELU_A * square))
                        bell = 0.5 * (1.0 + slope)
                        act[span, place] = (up * bell).astype(BF16)
                        inner = GELU_C * (1.0 + 3.0 * GELU_A * square)
                        deriv = bell + 0.5 * up * (1.0 - slope * slope) * inner
                        dup[span, place] = (back * deriv).astype(BF16)
                total = mm(dup[span, :hid], wu[...], NT)
                return total + mm(dup[span, hid:], wu_sib[...], NT)

            def feed(start, count):
                span = slice(start, start + count)
                return mm(act[span, :hid], wd[...]) + mm(act[span, hid:], wd_sib[...])

            dn2_own[...] = mlp(0, own).astype(BF16)
            bo_part[...] += feed(0, own)
            store(bo_part, bo_part_hbm)
            dn2_swaps = []
            for part in range(2):
                n2_swaps[part].wait_recv()
                span = slice(part * chunk, (part + 1) * chunk)
                dn2_send[span, :] = mlp(own + part * chunk, chunk).astype(BF16)
                block = pl.ds(part * chunk, chunk)
                dn2_swaps.append(wire.start(dn2_send.at[block, :], dn2_recv.at[block, :], to_far))
            g_send[:hid, :] = mm(act[:, hid:], og2[...], TN).astype(BF16)
            down_sum = wire.start(
                g_send.at[pl.ds(0, hid), :], g_recv.at[pl.ds(0, hid), :], to_sib
            )
            down_own = mm(act[:, :hid], og2[...], TN)
            down_sum.wait_recv()
            w_grads[:hid, :] = (down_own + g_recv[:hid, :].astype(F32)).astype(BF16)
            g_send[hid:, :] = mm(n2[...], dup[:, hid:], TN).astype(BF16)
            up_sum = wire.start(
                g_send.at[pl.ds(hid, hid), :], g_recv.at[pl.ds(hid, hid), :], to_sib
            )
            feed_far[...] = feed(own, own).astype(BF16)
            store(feed_far, feed_far_hbm)
            up_own = mm(n2[...], dup[:, :hid], TN)
            up_sum.wait_recv()
            w_grads[hid:, :] = (up_own + g_recv[hid:, :].astype(F32)).astype(BF16)
            store(w_grads, w_grads_hbm)

            for swap in dn2_swaps:
                swap.wait_recv()
            d_norm = dn2_own[...].astype(F32) + dn2_recv[...].astype(F32)
            back, d_gain, d_bias = norm_backward(d_norm, through[...], g2[...][None])
            through[...] = back
            da[...] = (og2[:own, :].astype(F32) + back).astype(BF16)
            store(through, through_hbm)
            store(da, da_hbm)
            vec[...] = jnp.concatenate([d_gain, d_bias, jnp.zeros((6, width), F32)], axis=0)
            for moving in stores:
                moving.wait()
            wire.drain()

        def norm_backward(d_norm, values, gain):
            hat, inverse = normalise(values)
            d_gain = jnp.sum(d_norm * hat, axis=0, keepdims=True)
            d_bias = jnp.sum(d_norm, axis=0, keepdims=True)
            scaled = d_norm * gain
            mean1 = jnp.mean(scaled, axis=-1, keepdims=True)
            mean2 = jnp.mean(scaled * hat, axis=-1, keepdims=True)
            return (scaled - mean1 - hat * mean2) * inverse, d_gain, d_bias

        vm = pl.BlockSpec(memory_space=pltpu.VMEM)
        hbm = pl.BlockSpec(memory_space=pl.ANY)
        smem = pl.BlockSpec(memory_space=pltpu.SMEM)
        attn_flops = 2 * 2 * seg * seg * cols * 4
        query_rows, key_rows = query_weight.T, key_weight.T
        heads_of_shard = [*[sds((seg, cols), BF16)] * 4, sds((seg, 2 * HEAD), F32)]
        shard_scratch = [*[pltpu.VMEM((seg, cols), BF16)] * 4, pltpu.VMEM((seg, 2 * HEAD), F32)]
        n_head_copies = 20
        (
            n1,
            q_own,
            k_own,
            v_own,
            mixed_own,
            lse_own,
            q_far,
            k_far,
            v_far,
            mixed_far,
            lse_far,
            w_far,
            through,
            d_att,
            bo_part,
            feed_far,
            w_grads,
            vec2,
        ) = pl.pallas_call(
            head_kernel,
            name="head",
            out_shape=[
                sds((seg, width), BF16),
                *heads_of_shard,
                *heads_of_shard,
                sds((3 * cols, width), BF16),
                sds((own, width), F32),
                sds((own, width), BF16),
                sds((own, width), F32),
                sds((own, width), BF16),
                sds((2 * hid, width), BF16),
                sds((8, width), F32),
            ],
            in_specs=[smem, hbm, hbm, hbm, *[vm] * 8, hbm, hbm],
            out_specs=[*[hbm] * 17, vm],
            scratch_shapes=[
                pltpu.VMEM((seg, seg), F32),
                pltpu.VMEM((width, hid), BF16),
                pltpu.VMEM((hid, width), BF16),
                pltpu.VMEM((seg, width), BF16),
                *shard_scratch,
                *shard_scratch,
                pltpu.VMEM((3 * cols, width), BF16),
                pltpu.VMEM((own, width), F32),
                pltpu.VMEM((own, width), BF16),
                pltpu.VMEM((own, width), F32),
                pltpu.VMEM((own, width), BF16),
                pltpu.VMEM((2 * hid, width), BF16),
                pltpu.VMEM((seg, width), BF16),
                pltpu.VMEM((seg, half_width), BF16),
                pltpu.VMEM((2 * own, width), BF16),
                pltpu.VMEM((2 * own, width), BF16),
                pltpu.VMEM((2 * own, 2 * hid), BF16),
                pltpu.VMEM((2 * own, 2 * hid), BF16),
                pltpu.VMEM((width, hid), BF16),
                pltpu.VMEM((hid, width), BF16),
                *[pltpu.VMEM((own, width), BF16)] * 5,
                pltpu.VMEM((2 * hid, width), BF16),
                pltpu.VMEM((2 * hid, width), BF16),
                pltpu.SemaphoreType.DMA((n_head_copies,)),
                pltpu.SemaphoreType.DMA((n_head_copies,)),
                pltpu.SemaphoreType.DMA((6 + 17,)),
            ],
            cost_estimate=pl.CostEstimate(
                flops=attn_flops * 8, bytes_accessed=30000000, transcendentals=0
            ),
            compiler_params=pltpu.CompilerParams(
                collective_id=1, has_side_effects=True, vmem_limit_bytes=HEAD_VMEM
            ),
        )(
            doc_lengths[0],
            block_input,
            out_grad,
            first_values,
            norm1_gain,
            norm1_bias,
            norm2_gain,
            norm2_bias,
            query_rows,
            key_rows,
            out_weight,
            value_weight,
            up_weight,
            down_weight,
        )

        def attention_backward(bias, wo, mixed, lse, q, k, v, da, dm, dkt, dvt, dq, dk, dv, tick):
            dm[...] = mm(da[...], wo, NT).astype(BF16)
            dkt[...] = jnp.zeros_like(dkt)
            dvt[...] = jnp.zeros_like(dvt)
            lane = lax.broadcasted_iota(jnp.int32, (QROWS, 2 * HEAD), 1)
            for block in range(seg // QROWS):
                low, keys = block * QROWS, (block + 1) * QROWS
                held = None
                for head, (first, last, half) in enumerate(head_parts(cols)):
                    query = pick(q[low:keys, first:last], half) * jnp.asarray(SCALE, BF16)
                    grad = pick(dm[low:keys, first:last], half)
                    scores = mm(query, k[:keys, first:last], NT) + bias[low:keys, :keys]
                    weights = jnp.exp(scores - lse[low:keys, head : head + 1])
                    d_weights = mm(grad, v[:keys, first:last], NT)
                    inner = jnp.sum(
                        grad.astype(F32) * mixed[low:keys, first:last].astype(F32),
                        axis=-1,
                        keepdims=True,
                    )
                    d_scores = (weights * (d_weights - inner)).astype(BF16)
                    dvt[:keys, first:last] += mm(weights.astype(BF16), grad, TN)
                    dkt[:keys, first:last] += mm(d_scores, query, TN)
                    d_query = mm(d_scores, k[:keys, first:last]) * SCALE
                    tick(0.95)
                    if half == 0:
                        held = d_query
                    elif half == 1:
                        both = jnp.where(lane < HEAD, held, d_query)
                        dq[low:keys, first:last] = both.astype(BF16)
                    else:
                        dq[low:keys, first:last] = d_query.astype(BF16)
            dk[...] = dkt[...].astype(BF16)
            dv[...] = dvt[...].astype(BF16)

        def tail_kernel(
            lengths,
            x,
            og,
            through_hbm,
            da_own,
            bo_part_hbm,
            feed_far,
            vec2,
            g1,
            wq_hbm,
            wk_hbm,
            wo_hbm,
            w_far_hbm,
            wv_hbm,
            n1_hbm,
            w_grads,
            mo_hbm,
            lo_hbm,
            qo_hbm,
            ko_hbm,
            vo_hbm,
            mf_hbm,
            lf_hbm,
            qf_hbm,
            kf_hbm,
            vf_hbm,
            bo_all,
            ig_all,
            fv_out,
            total,
            w_total,
            value_out,
            vec,
            bias,
            through,
            bo_part,
            wq,
            wk,
            wo,
            w_far,
            wv,
            n1,
            mo,
            lo,
            qo,
            ko,
            vo,
            mf,
            lf,
            qf,
            kf,
            vf,
            x_here,
            og_here,
            fv_all,
            v_total,
            da,
            dm,
            dkt,
            dvt,
            dqo,
            dko,
            dvo,
            dqf,
            dkf,
            dvf,
            fresh,
            o_send,
            o_recv,
            g_send,
            g_recv,
            v_recv,
            dn_send,
            dn_recv,
            feed_recv,
            acc,
            landing,
            w_acc,
            w_landing,
            vec_send,
            vec_recv,
            send_sems,
            recv_sems,
            local_sems,
        ):
            me = lax.axis_index("mp")
            row = lax.axis_index("batch")
            sibling, core = flipped(me, 1)
            across, chip = flipped(me, 2)
            to_sib, to_far = {"mp": sibling}, {"mp": across}
            wire = Wire(send_sems, recv_sems)
            here = rows_at(me * own, own)
            there = rows_at(across * own, own)
            mine = rows_at(core * own, own)
            loads = {}

            def load(name, source, target):
                loads[name] = pltpu.make_async_copy(source, target, local_sems.at[len(loads)])
                loads[name].start()

            load("da", da_own, da.at[mine, :])
            load("w", w_grads, w_acc.at[pl.ds(0, 2 * hid), :])
            load("w_far", w_far_hbm, w_far)
            load("qf", qf_hbm, qf)
            load("kf", kf_hbm, kf)
            load("vf", vf_hbm, vf)
            load("mf", mf_hbm, mf)
            load("lf", lf_hbm, lf)
            load("n1", n1_hbm, n1)
            load("wo", wo_hbm, wo)
            load("qo", qo_hbm, qo)
            load("ko", ko_hbm, ko)
            load("vo", vo_hbm, vo)
            load("mo", mo_hbm, mo)
            load("lo", lo_hbm, lo)
            load("wq", wq_hbm, wq)
            load("wk", wk_hbm, wk)
            load("wv", wv_hbm, wv)
            load("through", through_hbm, through)
            load("bo_part", bo_part_hbm, bo_part)
            load("x", x.at[here, :], x_here)
            load("og", og.at[here, :], og_here)

            def loaded(*which):
                for name in which or tuple(loads):
                    loads.pop(name).wait()

            greet([to_sib, to_far, *[{"batch": flipped(row, bit)[0]} for bit in bits]])
            half_rows = [pl.ds(part * (own // 2), own // 2) for part in range(2)]
            feed_swaps = []

            def send_feed(part):
                block = half_rows[part]
                feed_swaps.append(
                    wire.start(feed_far.at[block, :], feed_recv.at[block, :], to_far)
                )

            send_feed(0)
            da_swap = wire.start(da_own, da.at[mine, :], to_sib)
            if w_rows > 2 * hid:
                w_acc[2 * hid :, :] = jnp.zeros((w_rows - 2 * hid, width), BF16)
            loaded("w")
            w_streams = [
                Reduction(
                    wire, row, bits, w_acc, w_total, w_landing, i * w_stream, w_stream
                )
                for i in range(w_count)
            ]
            for one in w_streams:
                one.send_half(0)
            fill_bias((chip, core, *[lengths[i] for i in range(docs)]), bias, seg, docs)
            loaded("da", "w_far", "qf", "kf", "vf", "mf", "lf")
            da_swap.wait_recv()

            agenda = []
            last_step = len(bits) - 1

            def halve(one, step):
                one.add_half()
                if step < last_step:
                    one.send_half(step + 1)
                else:
                    one.turn()
                    one.send_whole()

            def double(one, step):
                one.take_whole()
                if step < last_step:
                    one.send_whole()

            def plan(due, action, *args):
                agenda.append((due, len(agenda), functools.partial(action, *args)))
                agenda.sort(key=lambda item: item[:2])

            for at, one in enumerate(w_streams):
                due = 13 + 7 * at
                for step in range(len(bits)):
                    plan(due, halve, one, step)
                    due += 6.5
                for step in range(len(bits)):
                    plan(due, double, one, step)
                    due += 5.5 if step < last_step - 1 else 10
            clock = [2.0]

            def tick(count):
                clock[0] += count
                while agenda and agenda[0][0] <= clock[0]:
                    agenda.pop(0)[2]()

            bo_near, bo_far, bo_diag = [], [], []

            def send_out(part):
                feed_swaps[part].wait_recv()
                block = slice(part * (own // 2), (part + 1) * (own // 2))
                out = bo_part[block, :] + feed_recv[block, :].astype(F32)
                out = out + x_here[block, :].astype(F32)
                place = rows_at(me * own + part * (own // 2), own // 2)
                bo_all[place, :] = out.astype(BF16)
                bo_near.append(wire.start(bo_all.at[place, :], bo_all.at[place, :], to_sib))
                bo_far.append(wire.start(bo_all.at[place, :], bo_all.at[place, :], to_far))

            def pass_out(part):
                bo_far[part].wait_recv()
                block = rows_at(across * own + part * (own // 2), own // 2)
                bo_diag.append(wire.start(bo_all.at[block, :], bo_all.at[block, :], to_sib))

            o_send[...] = mm(mf[...], da[...], TN).astype(BF16)
            o_swap = wire.start(o_send, o_recv, to_far)

            far_out = w_far[2 * cols :, :]
            attention_backward(
                bias, far_out, mf, lf, qf, kf, vf, da, dm, dkt, dvt, dqf, dkf, dvf, tick
            )
            loaded()
            g_send[:cols, :] = mm(dqf[...], n1[...], TN).astype(BF16)
            g_send[cols : 2 * cols, :] = mm(dkf[...], n1[...], TN).astype(BF16)
            g_swap = wire.start(g_send, g_recv, to_far)
            send_feed(1)
            tick(1.5)
            attention_backward(
                bias, wo[...], mo, lo, qo, ko, vo, da, dm, dkt, dvt, dqo, dko, dvo, tick
            )

            low_chip = chip == 0
            fresh[...] = jnp.where(low_chip, dvo[...], dvf[...])
            reused = jnp.where(low_chip, dvf[...], dvo[...])
            fv_all[pl.ds(me, 1)] = jnp.concatenate([reused[:own], reused[own:]], axis=1)[None]
            value_cols = jnp.where(core == 0, wv[:, :cols], wv[:, cols : 2 * cols])

            def dn1_part(start):
                span = rows_at(start, own)
                part = mm(dqo[span, :], wq[...])
                part = part + mm(dko[span, :], wk[...])
                part = part + mm(dqf[span, :], w_far[:cols, :])
                part = part + mm(dkf[span, :], w_far[cols : 2 * cols, :])
                return (part + mm(fresh[span, :], value_cols, NT)).astype(BF16)

            dn_send[...] = dn1_part((1 - core) * own)
            dn_swap = wire.start(dn_send, dn_recv, to_sib)
            tick(1.2)
            acc[3 * cols : 4 * cols, :] = mm(fresh[...], n1[...], TN).astype(BF16)
            kept = dn1_part(core * own).astype(F32)
            tick(1.5)
            dn_swap.wait_recv()
            d_norm = kept + dn_recv[...].astype(F32)
            back, d_gain1, d_bias1 = norm_backward(
                d_norm, x_here[...].astype(F32), g1[...][None]
            )
            ig_all[here, :] = (og_here[...].astype(F32) + back + through[...]).astype(BF16)
            ig_far = wire.start(ig_all.at[here, :], ig_all.at[here, :], to_far)
            ig_near = wire.start(ig_all.at[here, :], ig_all.at[here, :], to_sib)
            fv_mine, fv_there = fv_all.at[pl.ds(me, 1)], fv_all.at[pl.ds(across, 1)]
            fv_near = wire.start(fv_mine, fv_mine, to_sib)
            tick(1.5)

            acc[:cols, :] = mm(dqo[...], n1[...], TN).astype(BF16)
            acc[cols : 2 * cols, :] = mm(dko[...], n1[...], TN).astype(BF16)
            acc[2 * cols : 3 * cols, :] = mm(mo[...], da[...], TN).astype(BF16)
            if a_rows > 4 * cols:
                acc[4 * cols :, :] = jnp.zeros((a_rows - 4 * cols, width), BF16)
            tick(1.5)
            o_swap.wait_recv()
            o_rows = slice(2 * cols, 3 * cols)
            acc[o_rows, :] = (acc[o_rows, :].astype(F32) + o_recv[...].astype(F32)).astype(BF16)
            g_swap.wait_recv()
            shared = acc[: 2 * cols, :].astype(F32) + g_recv[...].astype(F32)
            acc[: 2 * cols, :] = shared.astype(BF16)

            ranks = [to_sib, to_far, *[{"batch": flipped(row, bit)[0]} for bit in bits]]
            vec_send[0] = jnp.concatenate(
                [d_gain1, d_bias1, vec2[:2, :], jnp.zeros((4, width), F32)], axis=0
            )
            streams = [
                Reduction(wire, row, bits, acc, total, landing, i * a_stream, a_stream)
                for i in range(a_count)
            ]

            def vector_step(at):
                if at < len(ranks):
                    return wire.start(vec_send.at[at], vec_recv.at[at], ranks[at])
                return None

            def vector_add(at, moving):
                if moving is not None:
                    moving.wait_recv()
                    vec_send[at + 1] = vec_send[at] + vec_recv[at]

            riding = []

            def start_vector(at):
                riding.append(vector_step(at))

            last = streams[-1]
            v_swaps, diag = [], {}

            def halve_all(step):
                for one in streams:
                    one.add_half()
                    if step < last_step:
                        one.send_half(step + 1)
                vector_add(step, riding[step])
                start_vector(step + 1)
                if step == last_step:
                    span = rows_at(last.start, last.size)
                    v_swaps.append(wire.start(acc.at[span, :], v_recv, to_far))
                    for one in streams[:-1]:
                        one.turn()
                        one.send_whole()
                    send_out(0)
                    send_first()
                    send_out(1)

            def merge_values():
                v_swaps[0].wait_recv()
                span = rows_at(last.start, last.size)
                at_row = last.start + lax.broadcasted_iota(jnp.int32, (last.size, 1), 0)
                is_value = (at_row >= 3 * cols) & (at_row < 4 * cols)
                other = jnp.where(is_value, v_recv[...].astype(F32), 0.0)
                total[span, :] = (acc[span, :].astype(F32) + other).astype(BF16)
                last.send_whole()

            def double_all(step):
                for one in streams:
                    one.take_whole()
                    if step < last_step:
                        one.send_whole()
                vector_add(len(bits) + step, riding[len(bits) + step])
                if step < last_step:
                    start_vector(len(bits) + step + 1)
                else:
                    v_rows = total.at[pl.ds(3 * cols, cols), :]
                    half = rows_at(core * cols, cols)
                    diag["v"] = wire.start(v_rows, v_total.at[half, :], to_sib)
                    v_total[half, :] = total[3 * cols : 4 * cols, :]

            def send_first():
                diag["fv far"] = wire.start(fv_mine, fv_mine, to_far)

            def pass_first():
                diag["fv far"].wait_recv()
                diag["fv"] = wire.start(fv_there, fv_there, to_sib)

            def pass_grad():
                ig_far.wait_recv()
                diag["ig"] = wire.start(ig_all.at[there, :], ig_all.at[there, :], to_sib)

            for one in streams:
                one.send_half(0)
            start_vector(0)
            turn = 43 + 5 * len(bits)
            for step in range(len(bits)):
                plan(43 + 5 * step, halve_all, step)
                plan(turn + 4 + 6 * step, double_all, step)
            plan(turn + 0.5, merge_values)
            plan(turn + 2, pass_grad)
            plan(turn + 17, pass_out, 0)
            plan(turn + 24, pass_first)
            plan(turn + 33, pass_out, 1)
            tick(10000)
            vec[...] = vec_send[len(ranks)]

            diag["v"].wait_recv()
            value_out[...] = v_total[...].astype(F32).T.astype(BF16)
            fv_near.wait_recv()
            diag["fv"].wait_recv()
            for part in range(rows // own):
                first = part // 2 * 2
                lanes = slice(part % 2 * cols, (part % 2 + 1) * cols)
                fv_out[part * own : (part + 1) * own, :] = jnp.concatenate(
                    [fv_all[first][:, lanes], fv_all[first + 1][:, lanes]], axis=1
                )
            for moving in (*bo_near, *bo_diag, ig_near, diag["ig"]):
                moving.wait_recv()
            wire.drain()

        tail_args = (
            doc_lengths[0],
            block_input,
            out_grad,
            through,
            d_att,
            bo_part,
            feed_far,
            vec2,
            norm1_gain,
            query_rows,
            key_rows,
            out_weight,
            w_far,
            value_weight,
            n1,
            w_grads,
            mixed_own,
            lse_own,
            q_own,
            k_own,
            v_own,
            mixed_far,
            lse_far,
            q_far,
            k_far,
            v_far,
        )
        bo_all, ig_all, fv_out, attn_sum, w_total, value_out, vectors = pl.pallas_call(
            tail_kernel,
            name="tail",
            out_shape=[
                pltpu.VMEM((rows, width), BF16),
                pltpu.VMEM((rows, width), BF16),
                pltpu.VMEM((rows, half_width), BF16),
                pltpu.VMEM((a_rows, width), BF16),
                pltpu.VMEM((w_rows, width), BF16),
                pltpu.VMEM((width, half_width), BF16),
                pltpu.VMEM((8, width), F32),
            ],
            in_specs=[smem, *[hbm] * 6, vm, vm, *[hbm] * 17],
            out_specs=[vm] * 7,
            scratch_shapes=[
                pltpu.VMEM((seg, seg), F32),
                pltpu.VMEM((own, width), F32),
                pltpu.VMEM((own, width), F32),
                pltpu.VMEM((cols, width), BF16),
                pltpu.VMEM((cols, width), BF16),
                pltpu.VMEM((cols, width), BF16),
                pltpu.VMEM((3 * cols, width), BF16),
                pltpu.VMEM((width, half_width), BF16),
                pltpu.VMEM((seg, width), BF16),
                pltpu.VMEM((seg, cols), BF16),
                pltpu.VMEM((seg, 2 * HEAD), F32),
                pltpu.VMEM((seg, cols), BF16),
                pltpu.VMEM((seg, cols), BF16),
                pltpu.VMEM((seg, cols), BF16),
                pltpu.VMEM((seg, cols), BF16),
                pltpu.VMEM((seg, 2 * HEAD), F32),
                pltpu.VMEM((seg, cols), BF16),
                pltpu.VMEM((seg, cols), BF16),
                pltpu.VMEM((seg, cols), BF16),
                pltpu.VMEM((own, width), BF16),
                pltpu.VMEM((own, width), BF16),
                pltpu.VMEM((4, own, 2 * cols), BF16),
                pltpu.VMEM((2 * cols, width), BF16),
                pltpu.VMEM((seg, width), BF16),
                pltpu.VMEM((seg, cols), BF16),
                pltpu.VMEM((seg, cols), F32),
                pltpu.VMEM((seg, cols), F32),
                *[pltpu.VMEM((seg, cols), BF16)] * 7,
                pltpu.VMEM((cols, width), BF16),
                pltpu.VMEM((cols, width), BF16),
                pltpu.VMEM((2 * cols, width), BF16),
                pltpu.VMEM((2 * cols, width), BF16),
                pltpu.VMEM((a_stream // batch_size, width), BF16),
                pltpu.VMEM((own, width), BF16),
                pltpu.VMEM((own, width), BF16),
                pltpu.VMEM((own, width), BF16),
                pltpu.VMEM((a_rows, width), BF16),
                pltpu.VMEM((a_rows, width), BF16),
                pltpu.VMEM((w_rows, width), BF16),
                pltpu.VMEM((w_rows, width), BF16),
                pltpu.VMEM((len(bits) + 3, 8, width), F32),
                pltpu.VMEM((len(bits) + 2, 8, width), F32),
                pltpu.SemaphoreType.DMA((n_copies,)),
                pltpu.SemaphoreType.DMA((n_copies,)),
                pltpu.SemaphoreType.DMA((22,)),
            ],
            cost_estimate=pl.CostEstimate(
                flops=attn_flops * 12, bytes_accessed=30000000, transcendentals=0
            ),
            compiler_params=pltpu.CompilerParams(
                collective_id=0, has_side_effects=True, vmem_limit_bytes=TAIL_VMEM
            ),
        )(*tail_args)
        block_out, input_grad = bo_all.astype(F32), ig_all.astype(F32)
        first_values_grad, value_grad = fv_out.astype(F32), value_out.astype(F32)
        query_grad = attn_sum[:cols].astype(F32).T
        key_grad = attn_sum[cols : 2 * cols].astype(F32).T
        out_sum = attn_sum[2 * cols : 3 * cols].astype(F32)
        down_grad, up_grad = w_total[:hid].astype(F32), w_total[hid : 2 * hid].astype(F32)
        return (
            block_out,
            input_grad,
            first_values_grad,
            vectors[0],
            vectors[1],
            query_grad,
            key_grad,
            value_grad,
            out_sum,
            vectors[2],
            vectors[3],
            up_grad,
            down_grad,
        )

    return jax.shard_map(
        shards,
        mesh=mesh,
        in_specs=(
            P("batch", None),
            P("batch", None),
            P(),
            P(),
            P(None, "mp"),
            P(None, "mp"),
            P(),
            P("mp", None),
            P(),
            P(),
            P(None, "mp"),
            P("mp", None),
            P("batch", None),
            P("batch", None),
        ),
        out_specs=(
            P("batch", None),
            P("batch", None),
            P("batch", None),
            P(),
            P(),
            P(None, "mp"),
            P(None, "mp"),
            P(),
            P("mp", None),
            P(),
            P(),
            P(None, "mp"),
            P("mp", None),
        ),
        check_vma=False,
    )
```

```python
import functools

import jax
import jax.numpy as jnp
from jax import lax
from jax.experimental import pallas as pl
from jax.experimental.pallas import tpu as pltpu
from jax.sharding import PartitionSpec as P

HEAD = 64
CONTEXT = 1024
EPS = 1e-05
MASKED = -1e30
QROWS = 256
SCALE = HEAD ** (-0.5)
GELU_C = 0.7978845608028654
GELU_A = 0.044715

F32 = jnp.float32
BF16 = jnp.bfloat16
HEAD_VMEM = 60 * 1024 * 1024
TAIL_VMEM = 50 * 1024 * 1024

NN = (((1,), (0,)), ((), ()))
NT = (((1,), (1,)), ((), ()))
TN = (((0,), (0,)), ((), ()))


def mm(left, right, dims=NN):
    return lax.dot_general(left, right, dims, preferred_element_type=F32)


def normalise(values):
    average = jnp.mean(values, axis=-1, keepdims=True)
    centred = values - average
    variance = jnp.mean(centred * centred, axis=-1, keepdims=True)
    inverse = lax.rsqrt(variance + EPS)
    return centred * inverse, inverse


def sds(shape, dtype):
    return jax.ShapeDtypeStruct(shape, dtype)


def fill_bias(s_ref, bias_ref, seg, docs):
    base = s_ref[0] * seg
    for block in range(seg // QROWS):
        low, keys = block * QROWS, (block + 1) * QROWS
        row = lax.broadcasted_iota(jnp.int32, (QROWS, 1), 0) + low
        start = jnp.zeros((QROWS, 1), jnp.int32)
        end = jnp.int32(0)
        for doc in range(docs):
            end = end + s_ref[2 + doc]
            rel = end - base
            start = jnp.maximum(start, jnp.where(rel <= row, rel, 0))
        col = lax.broadcasted_iota(jnp.int32, (QROWS, keys), 1)
        seen = (col >= start) & (col <= row)
        bias_ref[low:keys, :keys] = jnp.where(seen, 0.0, MASKED)


def head_parts(width):
    parts = []
    for head in range(width // HEAD):
        pair = head // 2 * 2 * HEAD
        if pair + 2 * HEAD <= width:
            parts.append((pair, pair + 2 * HEAD, head % 2))
        else:
            parts.append((pair, pair + HEAD, None))
    return parts


def pick(values, half):
    if half is None:
        return values
    lane = lax.broadcasted_iota(jnp.int32, values.shape, 1)
    keep = (lane < HEAD) if half == 0 else (lane >= HEAD)
    return jnp.where(keep, values, jnp.zeros_like(values))


def attention_forward(bias_ref, q_ref, k_ref, v_ref, mixed_ref, lse_ref, seg, heads):
    lane = lax.broadcasted_iota(jnp.int32, (QROWS, 2 * HEAD), 1)
    for block in range(seg // QROWS):
        low, keys = block * QROWS, (block + 1) * QROWS
        held = None
        stats = []
        for _, (first, last, half) in heads:
            query = pick(q_ref[low:keys, first:last], half) * jnp.asarray(SCALE, BF16)
            scores = mm(query, k_ref[:keys, first:last], NT) + bias_ref[low:keys, :keys]
            highest = jnp.max(scores, axis=-1, keepdims=True)
            weights = jnp.exp(scores - highest)
            total = jnp.sum(weights, axis=-1, keepdims=True)
            mixed = mm(weights.astype(BF16), v_ref[:keys, first:last]) / total
            stats.append(highest + jnp.log(total))
            if half == 0:
                held = mixed
            elif half == 1:
                both = jnp.where(lane < HEAD, held, mixed)
                mixed_ref[low:keys, first:last] = both.astype(BF16)
            else:
                mixed_ref[low:keys, first:last] = mixed.astype(BF16)
        for (head, _), stat in zip(heads, stats):
            lse_ref[low:keys, head : head + 1] = stat


MESH = pl.DeviceIdType.MESH


def flipped(index, bit):
    digit = lax.rem(lax.div(index, jnp.int32(bit)), jnp.int32(2))
    return index + bit - 2 * bit * digit, digit


class Wire:
    def __init__(self, send, recv):
        self.send, self.recv, self.used, self.sent = send, recv, 0, []

    def copy(self, src, dst, device):
        at = self.used
        self.used += 1
        return pltpu.make_async_remote_copy(
            src_ref=src,
            dst_ref=dst,
            send_sem=self.send.at[at],
            recv_sem=self.recv.at[at],
            device_id=device,
            device_id_type=MESH,
        )

    def start(self, src, dst, device):
        moving = self.copy(src, dst, device)
        moving.start()
        self.sent.append(moving)
        return moving

    def drain(self):
        for moving in self.sent:
            moving.wait_send()


def rows_at(start, count):
    return pl.ds(pl.multiple_of(start, 16), count)


def greet(devices, meanwhile=None):
    barrier = pltpu.get_barrier_semaphore()
    for device in devices:
        pl.semaphore_signal(barrier, inc=1, device_id=device, device_id_type=MESH)
    if meanwhile is not None:
        meanwhile()
    pl.semaphore_wait(barrier, len(devices))


class Reduction:
    def __init__(self, wire, index, bits, acc, out, recv, base, count):
        self.wire, self.acc, self.out, self.recv = wire, acc, out, recv
        self.base, self.count = base, count
        self.start, self.size = jnp.int32(base), count
        self.fills = base
        self.index, self.bits = index, bits
        self.trail = []

    def send_half(self, step):
        other, digit = flipped(self.index, self.bits[step])
        half = self.size // 2
        keep = self.start + digit * half
        give = self.start + (1 - digit) * half
        land = self.recv.at[pl.ds(self.fills, half), :]
        self.moving = self.wire.start(self.acc.at[rows_at(give, half), :], land, {"batch": other})
        self.trail.append((self.start, self.size, other))
        self.start, self.size = keep, half

    def add_half(self):
        self.moving.wait_recv()
        span = rows_at(self.start, self.size)
        landed = self.recv[self.fills : self.fills + self.size, :]
        total = self.acc[span, :].astype(F32) + landed.astype(F32)
        self.acc[span, :] = total.astype(BF16)
        self.fills += self.size

    def turn(self):
        span = rows_at(self.start, self.size)
        self.out[span, :] = self.acc[span, :]

    def send_whole(self):
        start, size, other = self.trail.pop()
        here = self.out.at[rows_at(self.start, self.size), :]
        self.moving = self.wire.start(here, here, {"batch": other})
        self.start, self.size = start, size

    def take_whole(self):
        self.moving.wait_recv()


def solution(mesh):
    batch_size = mesh.shape["batch"]
    assert mesh.shape["mp"] == 4

    def shards(
        block_input,
        first_values,
        norm1_gain,
        norm1_bias,
        query_weight,
        key_weight,
        value_weight,
        out_weight,
        norm2_gain,
        norm2_bias,
        up_weight,
        down_weight,
        out_grad,
        doc_lengths,
    ):
        rows, width = block_input.shape
        cols = query_weight.shape[1]
        hid = up_weight.shape[1]
        half_width = value_weight.shape[1]
        docs = doc_lengths.shape[1]
        seg = rows // 2
        own = rows // 4
        assert seg == min(rows, CONTEXT)


        bits = [1 << i for i in range(batch_size.bit_length() - 1)]
        assert 1 << len(bits) == batch_size and len(bits) >= 2
        granule = 16 * batch_size
        a_count = 2 if 2 * cols % granule == 0 else 1
        a_stream = -(-4 * cols // a_count // granule) * granule
        a_rows = a_count * a_stream
        orders = (bits, bits[1:] + bits[:1])
        w_count = 4 if hid % (2 * granule // 4) == 0 else 1
        w_stream = -(-2 * hid // w_count // granule) * granule
        w_rows = w_count * w_stream
        n_copies = 24 + (6 + 2 * w_count) * len(bits)

        def head_kernel(
            lengths,
            x,
            og,
            fv,
            g1,
            b1,
            g2,
            b2,
            wq,
            wk,
            wo,
            wv,
            wu_hbm,
            wd_hbm,
            n1_hbm,
            qo_hbm,
            ko_hbm,
            vo_hbm,
            mo_hbm,
            lo_hbm,
            qf_hbm,
            kf_hbm,
            vf_hbm,
            mf_hbm,
            lf_hbm,
            w_far_hbm,
            through_hbm,
            da_hbm,
            bo_part_hbm,
            feed_far_hbm,
            w_grads_hbm,
            vec,
            bias,
            wu,
            wd,
            n1,
            qo,
            ko,
            vo,
            mo,
            lo,
            qf,
            kf,
            vf,
            mf,
            lf,
            w_far,
            through,
            da,
            bo_part,
            feed_far,
            w_grads,
            x_seg,
            fv_seg,
            n2,
            og2,
            act,
            dup,
            wu_sib,
            wd_sib,
            att_send,
            att_recv,
            dn2_own,
            dn2_send,
            dn2_recv,
            g_send,
            g_recv,
            send_sems,
            recv_sems,
            local_sems,
        ):
            me = lax.axis_index("mp")
            sibling, core = flipped(me, 1)
            across, chip = flipped(me, 2)
            to_sib, to_far = {"mp": sibling}, {"mp": across}
            wire = Wire(send_sems, recv_sems)
            weight_loads = [
                pltpu.make_async_copy(wu_hbm, wu, local_sems.at[4]),
                pltpu.make_async_copy(wd_hbm, wd, local_sems.at[5]),
            ]
            stores = []

            def store(source, target):
                stores.append(
                    pltpu.make_async_copy(source, target, local_sems.at[6 + len(stores)])
                )
                stores[-1].start()

            loads = []

            def begin():
                for source, rows_from, count, target in (
                    (x, chip * seg, seg, x_seg),
                    (fv, chip * seg, seg, fv_seg),
                    (og, me * own, own, og2.at[pl.ds(0, own), :]),
                    (og, across * own, own, og2.at[pl.ds(own, own), :]),
                ):
                    load = pltpu.make_async_copy(
                        source.at[rows_at(rows_from, count), :], target, local_sems.at[len(loads)]
                    )
                    load.start()
                    loads.append(load)
                for load in weight_loads:
                    load.start()

            greet([to_sib, to_far], begin)
            cuts = [0, *range(2 * HEAD, cols, 2 * HEAD), cols]
            spans = list(zip(cuts[:-1], cuts[1:]))
            swaps = []
            for low, high in spans:
                for i, w in enumerate((wq, wk)):
                    swaps.append(
                        wire.start(
                            w.at[pl.ds(low, high - low), :],
                            w_far.at[pl.ds(i * cols + low, high - low), :],
                            to_far,
                        )
                    )
            up_swap = wire.start(wu_hbm, wu_sib, to_sib)
            down_swap = wire.start(wd_hbm, wd_sib, to_sib)
            scalars = (chip, core, *[lengths[i] for i in range(docs)])
            fill_bias(scalars, bias, seg, docs)
            for load in loads:
                load.wait()

            hat, _ = normalise(x_seg[...].astype(F32))
            normed = (hat * g1[...][None] + b1[...][None]).astype(BF16)
            n1[...] = normed
            qo[...] = mm(normed, wq[...], NT).astype(BF16)
            ko[...] = mm(normed, wk[...], NT).astype(BF16)
            value_cols = jnp.where(core == 0, wv[:, :cols], wv[:, cols : 2 * cols])
            fresh = mm(normed, value_cols).astype(BF16)
            reused = jnp.where(core == 0, fv_seg[:, :cols], fv_seg[:, cols : 2 * cols])
            vo[...] = jnp.where(chip == 0, fresh, reused)
            vf[...] = jnp.where(chip == 0, reused, fresh)
            for name in ((n1, n1_hbm), (qo, qo_hbm), (ko, ko_hbm), (vo, vo_hbm), (vf, vf_hbm)):
                store(*name)
            heads = list(enumerate(head_parts(cols)))
            attention_forward(bias, qo, ko, vo, mo, lo, seg, heads)
            store(mo, mo_hbm)
            store(lo, lo_hbm)
            out_swap = wire.start(wo, w_far.at[pl.ds(2 * cols, cols), :], to_far)
            for at, (low, high) in enumerate(spans):
                swaps[2 * at].wait_recv()
                swaps[2 * at + 1].wait_recv()
                normed = n1[...]
                qf[:, low:high] = mm(normed, w_far[low:high, :], NT).astype(BF16)
                kf[:, low:high] = mm(normed, w_far[cols + low : cols + high, :], NT).astype(BF16)
                here = [item for item in heads if item[1][0] == low]
                attention_forward(bias, qf, kf, vf, mf, lf, seg, here)
            store(qf, qf_hbm)
            store(kf, kf_hbm)
            store(mf, mf_hbm)
            store(lf, lf_hbm)
            out_swap.wait_recv()
            store(w_far, w_far_hbm)

            def out_part(start):
                span = rows_at(start, own)
                left = mm(mo[span, :], wo[...]).astype(BF16).astype(F32)
                right = mm(mf[span, :], w_far[2 * cols :, :]).astype(BF16).astype(F32)
                return (left + right).astype(BF16)

            att_send[...] = out_part((1 - core) * own)
            att_swap = wire.start(att_send, att_recv, to_sib)
            kept = out_part(core * own)
            att_swap.wait_recv()
            attention = kept.astype(F32) + att_recv[...].astype(F32)
            bo_part[...] = attention
            hidden = x_seg[rows_at(core * own, own), :].astype(F32) + attention
            chunk = own // 2
            n2_swaps = []
            for part in range(2):
                span = slice(part * chunk, (part + 1) * chunk)
                hat, _ = normalise(hidden[span])
                n2[span, :] = (hat * g2[...][None] + b2[...][None]).astype(BF16)
                n2_swaps.append(
                    wire.start(
                        n2.at[pl.ds(part * chunk, chunk), :],
                        n2.at[pl.ds(own + part * chunk, chunk), :],
                        to_far,
                    )
                )
            through[...] = hidden
            up_swap.wait_recv()
            down_swap.wait_recv()
            for load in weight_loads:
                load.wait()

            def mlp(start, count):
                span = slice(start, start + count)
                step = min(hid, 256)
                for at, (up_w, down_w) in enumerate(((wu, wd), (wu_sib, wd_sib))):
                    for tile in range(hid // step):
                        part = slice(tile * step, (tile + 1) * step)
                        place = slice(at * hid + tile * step, at * hid + (tile + 1) * step)
                        up = mm(n2[span, :], up_w[:, part])
                        back = mm(og2[span, :], down_w[part, :], NT)
                        square = up * up
                        slope = jnp.tanh(GELU_C * up * (1.0 + GELU_A * square))
                        bell = 0.5 * (1.0 + slope)
                        act[span, place] = (up * bell).astype(BF16)
                        inner = GELU_C * (1.0 + 3.0 * GELU_A * square)
                        deriv = bell + 0.5 * up * (1.0 - slope * slope) * inner
                        dup[span, place] = (back * deriv).astype(BF16)
                total = mm(dup[span, :hid], wu[...], NT)
                return total + mm(dup[span, hid:], wu_sib[...], NT)

            def feed(start, count):
                span = slice(start, start + count)
                return mm(act[span, :hid], wd[...]) + mm(act[span, hid:], wd_sib[...])

            dn2_own[...] = mlp(0, own).astype(BF16)
            bo_part[...] += feed(0, own)
            store(bo_part, bo_part_hbm)
            dn2_swaps = []
            for part in range(2):
                n2_swaps[part].wait_recv()
                span = slice(part * chunk, (part + 1) * chunk)
                dn2_send[span, :] = mlp(own + part * chunk, chunk).astype(BF16)
                block = pl.ds(part * chunk, chunk)
                dn2_swaps.append(wire.start(dn2_send.at[block, :], dn2_recv.at[block, :], to_far))
            g_send[:hid, :] = mm(act[:, hid:], og2[...], TN).astype(BF16)
            down_sum = wire.start(
                g_send.at[pl.ds(0, hid), :], g_recv.at[pl.ds(0, hid), :], to_sib
            )
            down_own = mm(act[:, :hid], og2[...], TN)
            down_sum.wait_recv()
            w_grads[:hid, :] = (down_own + g_recv[:hid, :].astype(F32)).astype(BF16)
            g_send[hid:, :] = mm(n2[...], dup[:, hid:], TN).astype(BF16)
            up_sum = wire.start(
                g_send.at[pl.ds(hid, hid), :], g_recv.at[pl.ds(hid, hid), :], to_sib
            )
            feed_far[...] = feed(own, own).astype(BF16)
            store(feed_far, feed_far_hbm)
            up_own = mm(n2[...], dup[:, :hid], TN)
            up_sum.wait_recv()
            w_grads[hid:, :] = (up_own + g_recv[hid:, :].astype(F32)).astype(BF16)
            store(w_grads, w_grads_hbm)

            sums = []
            for part in range(2):
                block = slice(part * chunk, (part + 1) * chunk)
                dn2_swaps[part].wait_recv()
                d_norm = dn2_own[block, :].astype(F32) + dn2_recv[block, :].astype(F32)
                back, d_gain, d_bias = norm_backward(d_norm, through[block, :], g2[...][None])
                sums.append((d_gain, d_bias))
                through[block, :] = back
                da[block, :] = (og2[block, :].astype(F32) + back).astype(BF16)
                place = pl.ds(part * chunk, chunk)
                store(through.at[place, :], through_hbm.at[place, :])
                store(da.at[place, :], da_hbm.at[place, :])
            d_gain, d_bias = (first + second for first, second in zip(*sums))
            vec[...] = jnp.concatenate([d_gain, d_bias, jnp.zeros((6, width), F32)], axis=0)
            for moving in stores:
                moving.wait()
            wire.drain()

        def norm_backward(d_norm, values, gain):
            hat, inverse = normalise(values)
            d_gain = jnp.sum(d_norm * hat, axis=0, keepdims=True)
            d_bias = jnp.sum(d_norm, axis=0, keepdims=True)
            scaled = d_norm * gain
            mean1 = jnp.mean(scaled, axis=-1, keepdims=True)
            mean2 = jnp.mean(scaled * hat, axis=-1, keepdims=True)
            return (scaled - mean1 - hat * mean2) * inverse, d_gain, d_bias

        vm = pl.BlockSpec(memory_space=pltpu.VMEM)
        hbm = pl.BlockSpec(memory_space=pl.ANY)
        smem = pl.BlockSpec(memory_space=pltpu.SMEM)
        attn_flops = 2 * 2 * seg * seg * cols * 4
        query_rows, key_rows = query_weight.T, key_weight.T
        heads_of_shard = [*[sds((seg, cols), BF16)] * 4, sds((seg, 2 * HEAD), F32)]
        shard_scratch = [*[pltpu.VMEM((seg, cols), BF16)] * 4, pltpu.VMEM((seg, 2 * HEAD), F32)]
        n_head_copies = 20
        (
            n1,
            q_own,
            k_own,
            v_own,
            mixed_own,
            lse_own,
            q_far,
            k_far,
            v_far,
            mixed_far,
            lse_far,
            w_far,
            through,
            d_att,
            bo_part,
            feed_far,
            w_grads,
            vec2,
        ) = pl.pallas_call(
            head_kernel,
            name="head",
            out_shape=[
                sds((seg, width), BF16),
                *heads_of_shard,
                *heads_of_shard,
                sds((3 * cols, width), BF16),
                sds((own, width), F32),
                sds((own, width), BF16),
                sds((own, width), F32),
                sds((own, width), BF16),
                sds((2 * hid, width), BF16),
                sds((8, width), F32),
            ],
            in_specs=[smem, hbm, hbm, hbm, *[vm] * 8, hbm, hbm],
            out_specs=[*[hbm] * 17, vm],
            scratch_shapes=[
                pltpu.VMEM((seg, seg), F32),
                pltpu.VMEM((width, hid), BF16),
                pltpu.VMEM((hid, width), BF16),
                pltpu.VMEM((seg, width), BF16),
                *shard_scratch,
                *shard_scratch,
                pltpu.VMEM((3 * cols, width), BF16),
                pltpu.VMEM((own, width), F32),
                pltpu.VMEM((own, width), BF16),
                pltpu.VMEM((own, width), F32),
                pltpu.VMEM((own, width), BF16),
                pltpu.VMEM((2 * hid, width), BF16),
                pltpu.VMEM((seg, width), BF16),
                pltpu.VMEM((seg, half_width), BF16),
                pltpu.VMEM((2 * own, width), BF16),
                pltpu.VMEM((2 * own, width), BF16),
                pltpu.VMEM((2 * own, 2 * hid), BF16),
                pltpu.VMEM((2 * own, 2 * hid), BF16),
                pltpu.VMEM((width, hid), BF16),
                pltpu.VMEM((hid, width), BF16),
                *[pltpu.VMEM((own, width), BF16)] * 5,
                pltpu.VMEM((2 * hid, width), BF16),
                pltpu.VMEM((2 * hid, width), BF16),
                pltpu.SemaphoreType.DMA((n_head_copies,)),
                pltpu.SemaphoreType.DMA((n_head_copies,)),
                pltpu.SemaphoreType.DMA((6 + 19,)),
            ],
            cost_estimate=pl.CostEstimate(
                flops=attn_flops * 8, bytes_accessed=30000000, transcendentals=0
            ),
            compiler_params=pltpu.CompilerParams(
                collective_id=1, has_side_effects=True, vmem_limit_bytes=HEAD_VMEM
            ),
        )(
            doc_lengths[0],
            block_input,
            out_grad,
            first_values,
            norm1_gain,
            norm1_bias,
            norm2_gain,
            norm2_bias,
            query_rows,
            key_rows,
            out_weight,
            value_weight,
            up_weight,
            down_weight,
        )

        def attention_backward(bias, wo, mixed, lse, q, k, v, da, dm, dkt, dvt, dq, dk, dv, tick):
            dm[...] = mm(da[...], wo, NT).astype(BF16)
            dkt[...] = jnp.zeros_like(dkt)
            dvt[...] = jnp.zeros_like(dvt)
            lane = lax.broadcasted_iota(jnp.int32, (QROWS, 2 * HEAD), 1)
            for block in range(seg // QROWS):
                low, keys = block * QROWS, (block + 1) * QROWS
                held = None
                for head, (first, last, half) in enumerate(head_parts(cols)):
                    query = pick(q[low:keys, first:last], half) * jnp.asarray(SCALE, BF16)
                    grad = pick(dm[low:keys, first:last], half)
                    scores = mm(query, k[:keys, first:last], NT) + bias[low:keys, :keys]
                    weights = jnp.exp(scores - lse[low:keys, head : head + 1])
                    d_weights = mm(grad, v[:keys, first:last], NT)
                    inner = jnp.sum(
                        grad.astype(F32) * mixed[low:keys, first:last].astype(F32),
                        axis=-1,
                        keepdims=True,
                    )
                    d_scores = (weights * (d_weights - inner)).astype(BF16)
                    dvt[:keys, first:last] += mm(weights.astype(BF16), grad, TN)
                    dkt[:keys, first:last] += mm(d_scores, query, TN)
                    d_query = mm(d_scores, k[:keys, first:last]) * SCALE
                    tick(0.95)
                    if half == 0:
                        held = d_query
                    elif half == 1:
                        both = jnp.where(lane < HEAD, held, d_query)
                        dq[low:keys, first:last] = both.astype(BF16)
                    else:
                        dq[low:keys, first:last] = d_query.astype(BF16)
            dk[...] = dkt[...].astype(BF16)
            dv[...] = dvt[...].astype(BF16)

        def tail_kernel(
            lengths,
            x,
            og,
            through_hbm,
            da_own,
            bo_part_hbm,
            feed_far,
            vec2,
            g1,
            wq_hbm,
            wk_hbm,
            wo_hbm,
            w_far_hbm,
            wv_hbm,
            n1_hbm,
            w_grads,
            mo_hbm,
            lo_hbm,
            qo_hbm,
            ko_hbm,
            vo_hbm,
            mf_hbm,
            lf_hbm,
            qf_hbm,
            kf_hbm,
            vf_hbm,
            bo_all,
            ig_all,
            fv_out,
            total,
            w_total,
            value_out,
            vec,
            bias,
            through,
            bo_part,
            wq,
            wk,
            wo,
            w_far,
            wv,
            n1,
            mo,
            lo,
            qo,
            ko,
            vo,
            mf,
            lf,
            qf,
            kf,
            vf,
            x_here,
            og_here,
            fv_all,
            v_total,
            da,
            dm,
            dkt,
            dvt,
            dqo,
            dko,
            dvo,
            dqf,
            dkf,
            dvf,
            fresh,
            o_send,
            o_recv,
            g_send,
            g_recv,
            v_recv,
            dn_send,
            dn_recv,
            feed_recv,
            acc,
            landing,
            w_acc,
            w_landing,
            vec_send,
            vec_recv,
            send_sems,
            recv_sems,
            local_sems,
        ):
            me = lax.axis_index("mp")
            row = lax.axis_index("batch")
            sibling, core = flipped(me, 1)
            across, chip = flipped(me, 2)
            to_sib, to_far = {"mp": sibling}, {"mp": across}
            wire = Wire(send_sems, recv_sems)
            here = rows_at(me * own, own)
            there = rows_at(across * own, own)
            mine = rows_at(core * own, own)
            loads = {}

            def load(name, source, target):
                loads[name] = pltpu.make_async_copy(source, target, local_sems.at[len(loads)])
                loads[name].start()

            load("da", da_own, da.at[mine, :])
            load("w", w_grads, w_acc.at[pl.ds(0, 2 * hid), :])
            load("w_far", w_far_hbm, w_far)
            load("qf", qf_hbm, qf)
            load("kf", kf_hbm, kf)
            load("vf", vf_hbm, vf)
            load("mf", mf_hbm, mf)
            load("lf", lf_hbm, lf)
            load("n1", n1_hbm, n1)
            load("wo", wo_hbm, wo)
            load("qo", qo_hbm, qo)
            load("ko", ko_hbm, ko)
            load("vo", vo_hbm, vo)
            load("mo", mo_hbm, mo)
            load("lo", lo_hbm, lo)
            load("wq", wq_hbm, wq)
            load("wk", wk_hbm, wk)
            load("wv", wv_hbm, wv)
            load("through", through_hbm, through)
            load("bo_part", bo_part_hbm, bo_part)
            load("x", x.at[here, :], x_here)
            load("og", og.at[here, :], og_here)

            def loaded(*which):
                for name in which or tuple(loads):
                    loads.pop(name).wait()

            greet([to_sib, to_far, *[{"batch": flipped(row, bit)[0]} for bit in bits]])
            half_rows = [pl.ds(part * (own // 2), own // 2) for part in range(2)]
            feed_swaps = []

            def send_feed(part):
                block = half_rows[part]
                feed_swaps.append(
                    wire.start(feed_far.at[block, :], feed_recv.at[block, :], to_far)
                )

            send_feed(0)
            da_swap = wire.start(da_own, da.at[mine, :], to_sib)
            if w_rows > 2 * hid:
                w_acc[2 * hid :, :] = jnp.zeros((w_rows - 2 * hid, width), BF16)
            loaded("w")
            w_streams = [
                Reduction(
                    wire, row, ([bits[1], bits[0], *bits[2:]] if i == 0 else bits), w_acc, w_total, w_landing, i * w_stream, w_stream
                )
                for i in range(w_count)
            ]
            for one in w_streams:
                one.send_half(0)
            fill_bias((chip, core, *[lengths[i] for i in range(docs)]), bias, seg, docs)
            loaded("da", "w_far", "qf", "kf", "vf", "mf", "lf")
            da_swap.wait_recv()

            agenda = []
            last_step = len(bits) - 1

            def halve(one, step):
                one.add_half()
                if step < last_step:
                    one.send_half(step + 1)
                else:
                    one.turn()
                    one.send_whole()

            def double(one, step):
                one.take_whole()
                if step < last_step:
                    one.send_whole()

            def plan(due, action, *args):
                agenda.append((due, len(agenda), functools.partial(action, *args)))
                agenda.sort(key=lambda item: item[:2])

            for at, one in enumerate(w_streams):
                due = 12 if at == 0 else 6 + 7 * at
                for step in range(len(bits)):
                    plan(due, halve, one, step)
                    due += 16 if at == step == 0 else 6.5
                for step in range(len(bits)):
                    plan(due, double, one, step)
                    due += 7 if step < last_step - 1 else 10
            clock = [2.0]

            def tick(count):
                clock[0] += count
                while agenda and agenda[0][0] <= clock[0]:
                    agenda.pop(0)[2]()

            bo_near, bo_far, bo_diag = [], [], []

            def send_out(part):
                feed_swaps[part].wait_recv()
                block = slice(part * (own // 2), (part + 1) * (own // 2))
                out = bo_part[block, :] + feed_recv[block, :].astype(F32)
                out = out + x_here[block, :].astype(F32)
                place = rows_at(me * own + part * (own // 2), own // 2)
                bo_all[place, :] = out.astype(BF16)
                bo_near.append(wire.start(bo_all.at[place, :], bo_all.at[place, :], to_sib))
                bo_far.append(wire.start(bo_all.at[place, :], bo_all.at[place, :], to_far))

            def pass_out(part):
                bo_far[part].wait_recv()
                block = rows_at(across * own + part * (own // 2), own // 2)
                bo_diag.append(wire.start(bo_all.at[block, :], bo_all.at[block, :], to_sib))

            o_send[...] = mm(mf[...], da[...], TN).astype(BF16)
            o_swap = wire.start(o_send, o_recv, to_far)

            far_out = w_far[2 * cols :, :]
            attention_backward(
                bias, far_out, mf, lf, qf, kf, vf, da, dm, dkt, dvt, dqf, dkf, dvf, tick
            )
            loaded()
            g_send[:cols, :] = mm(dqf[...], n1[...], TN).astype(BF16)
            g_send[cols : 2 * cols, :] = mm(dkf[...], n1[...], TN).astype(BF16)
            g_swap = wire.start(g_send, g_recv, to_far)
            send_feed(1)
            tick(1.5)
            attention_backward(
                bias, wo[...], mo, lo, qo, ko, vo, da, dm, dkt, dvt, dqo, dko, dvo, tick
            )

            low_chip = chip == 0
            fresh[...] = jnp.where(low_chip, dvo[...], dvf[...])
            reused = jnp.where(low_chip, dvf[...], dvo[...])
            fv_all[pl.ds(me, 1)] = jnp.concatenate([reused[:own], reused[own:]], axis=1)[None]
            value_cols = jnp.where(core == 0, wv[:, :cols], wv[:, cols : 2 * cols])

            def dn1_part(start):
                span = rows_at(start, own)
                part = mm(dqo[span, :], wq[...])
                part = part + mm(dko[span, :], wk[...])
                part = part + mm(dqf[span, :], w_far[:cols, :])
                part = part + mm(dkf[span, :], w_far[cols : 2 * cols, :])
                return (part + mm(fresh[span, :], value_cols, NT)).astype(BF16)

            dn_send[...] = dn1_part((1 - core) * own)
            dn_swap = wire.start(dn_send, dn_recv, to_sib)
            tick(1.2)
            acc[3 * cols : 4 * cols, :] = mm(fresh[...], n1[...], TN).astype(BF16)
            kept = dn1_part(core * own).astype(F32)
            tick(1.5)
            dn_swap.wait_recv()
            d_norm = kept + dn_recv[...].astype(F32)
            back, d_gain1, d_bias1 = norm_backward(
                d_norm, x_here[...].astype(F32), g1[...][None]
            )
            ig_all[here, :] = (og_here[...].astype(F32) + back + through[...]).astype(BF16)
            ig_far = wire.start(ig_all.at[here, :], ig_all.at[here, :], to_far)
            ig_near = wire.start(ig_all.at[here, :], ig_all.at[here, :], to_sib)
            fv_mine, fv_there = fv_all.at[pl.ds(me, 1)], fv_all.at[pl.ds(across, 1)]
            fv_near = wire.start(fv_mine, fv_mine, to_sib)
            tick(1.5)

            acc[:cols, :] = mm(dqo[...], n1[...], TN).astype(BF16)
            acc[cols : 2 * cols, :] = mm(dko[...], n1[...], TN).astype(BF16)
            acc[2 * cols : 3 * cols, :] = mm(mo[...], da[...], TN).astype(BF16)
            if a_rows > 4 * cols:
                acc[4 * cols :, :] = jnp.zeros((a_rows - 4 * cols, width), BF16)
            tick(1.5)
            o_swap.wait_recv()
            o_rows = slice(2 * cols, 3 * cols)
            acc[o_rows, :] = (acc[o_rows, :].astype(F32) + o_recv[...].astype(F32)).astype(BF16)
            g_swap.wait_recv()
            shared = acc[: 2 * cols, :].astype(F32) + g_recv[...].astype(F32)
            acc[: 2 * cols, :] = shared.astype(BF16)

            ranks = [to_sib, to_far, *[{"batch": flipped(row, bit)[0]} for bit in bits]]
            vec_send[0] = jnp.concatenate(
                [d_gain1, d_bias1, vec2[:2, :], jnp.zeros((4, width), F32)], axis=0
            )
            streams = [
                Reduction(wire, row, bits, acc, total, landing, i * a_stream, a_stream)
                for i in range(a_count)
            ]

            def vector_step(at):
                if at < len(ranks):
                    return wire.start(vec_send.at[at], vec_recv.at[at], ranks[at])
                return None

            def vector_add(at, moving):
                if moving is not None:
                    moving.wait_recv()
                    vec_send[at + 1] = vec_send[at] + vec_recv[at]

            riding = []

            def start_vector(at):
                riding.append(vector_step(at))

            last = streams[-1]
            v_swaps, diag = [], {}

            def halve_all(step):
                for one in streams:
                    one.add_half()
                    if step < last_step:
                        one.send_half(step + 1)
                vector_add(step, riding[step])
                start_vector(step + 1)
                if step == last_step:
                    span = rows_at(last.start, last.size)
                    v_swaps.append(wire.start(acc.at[span, :], v_recv, to_far))
                    for one in streams[:-1]:
                        one.turn()
                        one.send_whole()
                    send_out(0)
                    send_first()
                    send_out(1)

            def merge_values():
                v_swaps[0].wait_recv()
                span = rows_at(last.start, last.size)
                at_row = last.start + lax.broadcasted_iota(jnp.int32, (last.size, 1), 0)
                is_value = (at_row >= 3 * cols) & (at_row < 4 * cols)
                other = jnp.where(is_value, v_recv[...].astype(F32), 0.0)
                total[span, :] = (acc[span, :].astype(F32) + other).astype(BF16)
                last.send_whole()

            def double_all(step):
                for one in streams:
                    one.take_whole()
                    if step < last_step:
                        one.send_whole()
                vector_add(len(bits) + step, riding[len(bits) + step])
                if step < last_step:
                    start_vector(len(bits) + step + 1)
                else:
                    v_rows = total.at[pl.ds(3 * cols, cols), :]
                    half = rows_at(core * cols, cols)
                    diag["v"] = wire.start(v_rows, v_total.at[half, :], to_sib)
                    v_total[half, :] = total[3 * cols : 4 * cols, :]

            def send_first():
                diag["fv far"] = wire.start(fv_mine, fv_mine, to_far)

            def pass_first():
                diag["fv far"].wait_recv()
                diag["fv"] = wire.start(fv_there, fv_there, to_sib)

            def pass_grad():
                ig_far.wait_recv()
                diag["ig"] = wire.start(ig_all.at[there, :], ig_all.at[there, :], to_sib)

            for one in streams:
                one.send_half(0)
            start_vector(0)
            turn = 46 + 5 * len(bits)
            for step in range(len(bits)):
                plan(46 + 5 * step, halve_all, step)
                plan(turn + 4 + 6 * step, double_all, step)
            plan(turn + 0.5, merge_values)
            plan(turn + 2, pass_grad)
            plan(turn + 17, pass_out, 0)
            plan(turn + 24, pass_first)
            plan(turn + 33, pass_out, 1)
            tick(10000)
            vec[...] = vec_send[len(ranks)]

            diag["v"].wait_recv()
            value_out[...] = v_total[...].astype(F32).T.astype(BF16)
            fv_near.wait_recv()
            diag["fv"].wait_recv()
            for part in range(rows // own):
                first = part // 2 * 2
                lanes = slice(part % 2 * cols, (part % 2 + 1) * cols)
                fv_out[part * own : (part + 1) * own, :] = jnp.concatenate(
                    [fv_all[first][:, lanes], fv_all[first + 1][:, lanes]], axis=1
                )
            for moving in (*bo_near, *bo_diag, ig_near, diag["ig"]):
                moving.wait_recv()
            wire.drain()

        tail_args = (
            doc_lengths[0],
            block_input,
            out_grad,
            through,
            d_att,
            bo_part,
            feed_far,
            vec2,
            norm1_gain,
            query_rows,
            key_rows,
            out_weight,
            w_far,
            value_weight,
            n1,
            w_grads,
            mixed_own,
            lse_own,
            q_own,
            k_own,
            v_own,
            mixed_far,
            lse_far,
            q_far,
            k_far,
            v_far,
        )
        bo_all, ig_all, fv_out, attn_sum, w_total, value_out, vectors = pl.pallas_call(
            tail_kernel,
            name="tail",
            out_shape=[
                pltpu.VMEM((rows, width), BF16),
                pltpu.VMEM((rows, width), BF16),
                pltpu.VMEM((rows, half_width), BF16),
                pltpu.VMEM((a_rows, width), BF16),
                pltpu.VMEM((w_rows, width), BF16),
                pltpu.VMEM((width, half_width), BF16),
                pltpu.VMEM((8, width), F32),
            ],
            in_specs=[smem, *[hbm] * 6, vm, vm, *[hbm] * 17],
            out_specs=[vm] * 7,
            scratch_shapes=[
                pltpu.VMEM((seg, seg), F32),
                pltpu.VMEM((own, width), F32),
                pltpu.VMEM((own, width), F32),
                pltpu.VMEM((cols, width), BF16),
                pltpu.VMEM((cols, width), BF16),
                pltpu.VMEM((cols, width), BF16),
                pltpu.VMEM((3 * cols, width), BF16),
                pltpu.VMEM((width, half_width), BF16),
                pltpu.VMEM((seg, width), BF16),
                pltpu.VMEM((seg, cols), BF16),
                pltpu.VMEM((seg, 2 * HEAD), F32),
                pltpu.VMEM((seg, cols), BF16),
                pltpu.VMEM((seg, cols), BF16),
                pltpu.VMEM((seg, cols), BF16),
                pltpu.VMEM((seg, cols), BF16),
                pltpu.VMEM((seg, 2 * HEAD), F32),
                pltpu.VMEM((seg, cols), BF16),
                pltpu.VMEM((seg, cols), BF16),
                pltpu.VMEM((seg, cols), BF16),
                pltpu.VMEM((own, width), BF16),
                pltpu.VMEM((own, width), BF16),
                pltpu.VMEM((4, own, 2 * cols), BF16),
                pltpu.VMEM((2 * cols, width), BF16),
                pltpu.VMEM((seg, width), BF16),
                pltpu.VMEM((seg, cols), BF16),
                pltpu.VMEM((seg, cols), F32),
                pltpu.VMEM((seg, cols), F32),
                *[pltpu.VMEM((seg, cols), BF16)] * 7,
                pltpu.VMEM((cols, width), BF16),
                pltpu.VMEM((cols, width), BF16),
                pltpu.VMEM((2 * cols, width), BF16),
                pltpu.VMEM((2 * cols, width), BF16),
                pltpu.VMEM((a_stream // batch_size, width), BF16),
                pltpu.VMEM((own, width), BF16),
                pltpu.VMEM((own, width), BF16),
                pltpu.VMEM((own, width), BF16),
                pltpu.VMEM((a_rows, width), BF16),
                pltpu.VMEM((a_rows, width), BF16),
                pltpu.VMEM((w_rows, width), BF16),
                pltpu.VMEM((w_rows, width), BF16),
                pltpu.VMEM((len(bits) + 3, 8, width), F32),
                pltpu.VMEM((len(bits) + 2, 8, width), F32),
                pltpu.SemaphoreType.DMA((n_copies,)),
                pltpu.SemaphoreType.DMA((n_copies,)),
                pltpu.SemaphoreType.DMA((22,)),
            ],
            cost_estimate=pl.CostEstimate(
                flops=attn_flops * 12, bytes_accessed=30000000, transcendentals=0
            ),
            compiler_params=pltpu.CompilerParams(
                collective_id=0, has_side_effects=True, vmem_limit_bytes=TAIL_VMEM
            ),
        )(*tail_args)
        block_out, input_grad = bo_all.astype(F32), ig_all.astype(F32)
        first_values_grad, value_grad = fv_out.astype(F32), value_out.astype(F32)
        query_grad = attn_sum[:cols].astype(F32).T
        key_grad = attn_sum[cols : 2 * cols].astype(F32).T
        out_sum = attn_sum[2 * cols : 3 * cols].astype(F32)
        down_grad, up_grad = w_total[:hid].astype(F32), w_total[hid : 2 * hid].astype(F32)
        return (
            block_out,
            input_grad,
            first_values_grad,
            vectors[0],
            vectors[1],
            query_grad,
            key_grad,
            value_grad,
            out_sum,
            vectors[2],
            vectors[3],
            up_grad,
            down_grad,
        )

    return jax.shard_map(
        shards,
        mesh=mesh,
        in_specs=(
            P("batch", None),
            P("batch", None),
            P(),
            P(),
            P(None, "mp"),
            P(None, "mp"),
            P(),
            P("mp", None),
            P(),
            P(),
            P(None, "mp"),
            P("mp", None),
            P("batch", None),
            P("batch", None),
        ),
        out_specs=(
            P("batch", None),
            P("batch", None),
            P("batch", None),
            P(),
            P(),
            P(None, "mp"),
            P(None, "mp"),
            P(),
            P("mp", None),
            P(),
            P(),
            P(None, "mp"),
            P("mp", None),
        ),
        check_vma=False,
    )
```

```python
import functools

import jax
import jax.numpy as jnp
from jax import lax
from jax.experimental import pallas as pl
from jax.experimental.pallas import tpu as pltpu
from jax.sharding import PartitionSpec as P

HEAD = 64
CONTEXT = 1024
EPS = 1e-05
MASKED = -1e30
QROWS = 256
SCALE = HEAD ** (-0.5)
GELU_C = 0.7978845608028654
GELU_A = 0.044715

F32 = jnp.float32
BF16 = jnp.bfloat16
HEAD_VMEM = 60 * 1024 * 1024
TAIL_VMEM = 50 * 1024 * 1024

NN = (((1,), (0,)), ((), ()))
NT = (((1,), (1,)), ((), ()))
TN = (((0,), (0,)), ((), ()))


def mm(left, right, dims=NN):
    return lax.dot_general(left, right, dims, preferred_element_type=F32)


def normalise(values):
    average = jnp.mean(values, axis=-1, keepdims=True)
    centred = values - average
    variance = jnp.mean(centred * centred, axis=-1, keepdims=True)
    inverse = lax.rsqrt(variance + EPS)
    return centred * inverse, inverse


def sds(shape, dtype):
    return jax.ShapeDtypeStruct(shape, dtype)


def fill_bias(s_ref, bias_ref, seg, docs):
    base = s_ref[0] * seg
    for block in range(seg // QROWS):
        low, keys = block * QROWS, (block + 1) * QROWS
        row = lax.broadcasted_iota(jnp.int32, (QROWS, 1), 0) + low
        start = jnp.zeros((QROWS, 1), jnp.int32)
        end = jnp.int32(0)
        for doc in range(docs):
            end = end + s_ref[2 + doc]
            rel = end - base
            start = jnp.maximum(start, jnp.where(rel <= row, rel, 0))
        col = lax.broadcasted_iota(jnp.int32, (QROWS, keys), 1)
        seen = (col >= start) & (col <= row)
        bias_ref[low:keys, :keys] = jnp.where(seen, 0.0, MASKED)


def head_parts(width):
    parts = []
    for head in range(width // HEAD):
        pair = head // 2 * 2 * HEAD
        if pair + 2 * HEAD <= width:
            parts.append((pair, pair + 2 * HEAD, head % 2))
        else:
            parts.append((pair, pair + HEAD, None))
    return parts


def pick(values, half):
    if half is None:
        return values
    lane = lax.broadcasted_iota(jnp.int32, values.shape, 1)
    keep = (lane < HEAD) if half == 0 else (lane >= HEAD)
    return jnp.where(keep, values, jnp.zeros_like(values))


def attention_forward(bias_ref, q_ref, k_ref, v_ref, mixed_ref, lse_ref, seg, heads):
    lane = lax.broadcasted_iota(jnp.int32, (QROWS, 2 * HEAD), 1)
    for block in range(seg // QROWS):
        low, keys = block * QROWS, (block + 1) * QROWS
        held = None
        stats = []
        for _, (first, last, half) in heads:
            query = pick(q_ref[low:keys, first:last], half) * jnp.asarray(SCALE, BF16)
            scores = mm(query, k_ref[:keys, first:last], NT) + bias_ref[low:keys, :keys]
            highest = jnp.max(scores, axis=-1, keepdims=True)
            weights = jnp.exp(scores - highest)
            total = jnp.sum(weights, axis=-1, keepdims=True)
            mixed = mm(weights.astype(BF16), v_ref[:keys, first:last]) / total
            stats.append(highest + jnp.log(total))
            if half == 0:
                held = mixed
            elif half == 1:
                both = jnp.where(lane < HEAD, held, mixed)
                mixed_ref[low:keys, first:last] = both.astype(BF16)
            else:
                mixed_ref[low:keys, first:last] = mixed.astype(BF16)
        for (head, _), stat in zip(heads, stats):
            lse_ref[low:keys, head : head + 1] = stat


MESH = pl.DeviceIdType.MESH


def flipped(index, bit):
    digit = lax.rem(lax.div(index, jnp.int32(bit)), jnp.int32(2))
    return index + bit - 2 * bit * digit, digit


class Wire:
    def __init__(self, send, recv):
        self.send, self.recv, self.used, self.sent = send, recv, 0, []

    def copy(self, src, dst, device):
        at = self.used
        self.used += 1
        return pltpu.make_async_remote_copy(
            src_ref=src,
            dst_ref=dst,
            send_sem=self.send.at[at],
            recv_sem=self.recv.at[at],
            device_id=device,
            device_id_type=MESH,
        )

    def start(self, src, dst, device):
        moving = self.copy(src, dst, device)
        moving.start()
        self.sent.append(moving)
        return moving

    def drain(self):
        for moving in self.sent:
            moving.wait_send()


def rows_at(start, count):
    return pl.ds(pl.multiple_of(start, 16), count)


def greet(devices, meanwhile=None):
    barrier = pltpu.get_barrier_semaphore()
    for device in devices:
        pl.semaphore_signal(barrier, inc=1, device_id=device, device_id_type=MESH)
    if meanwhile is not None:
        meanwhile()
    pl.semaphore_wait(barrier, len(devices))


class Reduction:
    def __init__(self, wire, index, bits, acc, out, recv, base, count):
        self.wire, self.acc, self.out, self.recv = wire, acc, out, recv
        self.base, self.count = base, count
        self.start, self.size = jnp.int32(base), count
        self.fills = base
        self.index, self.bits = index, bits
        self.trail = []

    def send_half(self, step):
        other, digit = flipped(self.index, self.bits[step])
        half = self.size // 2
        keep = self.start + digit * half
        give = self.start + (1 - digit) * half
        land = self.recv.at[pl.ds(self.fills, half), :]
        self.moving = self.wire.start(self.acc.at[rows_at(give, half), :], land, {"batch": other})
        self.trail.append((self.start, self.size, other))
        self.start, self.size = keep, half

    def add_half(self):
        self.moving.wait_recv()
        span = rows_at(self.start, self.size)
        landed = self.recv[self.fills : self.fills + self.size, :]
        total = self.acc[span, :].astype(F32) + landed.astype(F32)
        self.acc[span, :] = total.astype(BF16)
        self.fills += self.size

    def turn(self):
        span = rows_at(self.start, self.size)
        self.out[span, :] = self.acc[span, :]

    def send_whole(self):
        start, size, other = self.trail.pop()
        here = self.out.at[rows_at(self.start, self.size), :]
        self.moving = self.wire.start(here, here, {"batch": other})
        self.start, self.size = start, size

    def take_whole(self):
        self.moving.wait_recv()


def solution(mesh):
    batch_size = mesh.shape["batch"]
    assert mesh.shape["mp"] == 4

    def shards(
        block_input,
        first_values,
        norm1_gain,
        norm1_bias,
        query_weight,
        key_weight,
        value_weight,
        out_weight,
        norm2_gain,
        norm2_bias,
        up_weight,
        down_weight,
        out_grad,
        doc_lengths,
    ):
        rows, width = block_input.shape
        cols = query_weight.shape[1]
        hid = up_weight.shape[1]
        half_width = value_weight.shape[1]
        docs = doc_lengths.shape[1]
        seg = rows // 2
        own = rows // 4
        assert seg == min(rows, CONTEXT)


        bits = [1 << i for i in range(batch_size.bit_length() - 1)]
        assert 1 << len(bits) == batch_size and len(bits) >= 2
        granule = 16 * batch_size
        a_count = 2 if 2 * cols % granule == 0 else 1
        a_stream = -(-4 * cols // a_count // granule) * granule
        a_rows = a_count * a_stream
        orders = (bits, bits[1:] + bits[:1])
        w_count = 4 if hid % (2 * granule // 4) == 0 else 1
        w_stream = -(-2 * hid // w_count // granule) * granule
        w_rows = w_count * w_stream
        n_copies = 24 + (6 + 2 * w_count) * len(bits)

        def head_kernel(
            lengths,
            x,
            og,
            fv,
            g1,
            b1,
            g2,
            b2,
            wq,
            wk,
            wo,
            wv,
            wu_hbm,
            wd_hbm,
            n1_hbm,
            qo_hbm,
            ko_hbm,
            vo_hbm,
            mo_hbm,
            lo_hbm,
            qf_hbm,
            kf_hbm,
            vf_hbm,
            mf_hbm,
            lf_hbm,
            w_far_hbm,
            through_hbm,
            da_hbm,
            bo_part_hbm,
            feed_far_hbm,
            w_grads_hbm,
            vec,
            bias,
            wu,
            wd,
            n1,
            qo,
            ko,
            vo,
            mo,
            lo,
            qf,
            kf,
            vf,
            mf,
            lf,
            w_far,
            through,
            da,
            bo_part,
            feed_far,
            w_grads,
            x_seg,
            fv_seg,
            n2,
            og2,
            act,
            dup,
            wu_sib,
            wd_sib,
            att_send,
            att_recv,
            dn2_own,
            dn2_send,
            dn2_recv,
            g_send,
            g_recv,
            send_sems,
            recv_sems,
            local_sems,
        ):
            me = lax.axis_index("mp")
            sibling, core = flipped(me, 1)
            across, chip = flipped(me, 2)
            to_sib, to_far = {"mp": sibling}, {"mp": across}
            wire = Wire(send_sems, recv_sems)
            weight_loads = [
                pltpu.make_async_copy(wu_hbm, wu, local_sems.at[4]),
                pltpu.make_async_copy(wd_hbm, wd, local_sems.at[5]),
            ]
            stores = []

            def store(source, target):
                stores.append(
                    pltpu.make_async_copy(source, target, local_sems.at[6 + len(stores)])
                )
                stores[-1].start()

            loads = []

            def begin():
                for source, rows_from, count, target in (
                    (x, chip * seg, seg, x_seg),
                    (fv, chip * seg, seg, fv_seg),
                    (og, me * own, own, og2.at[pl.ds(0, own), :]),
                    (og, across * own, own, og2.at[pl.ds(own, own), :]),
                ):
                    load = pltpu.make_async_copy(
                        source.at[rows_at(rows_from, count), :], target, local_sems.at[len(loads)]
                    )
                    load.start()
                    loads.append(load)
                for load in weight_loads:
                    load.start()

            greet([to_sib, to_far], begin)
            cuts = [0, *range(2 * HEAD, cols, 2 * HEAD), cols]
            spans = list(zip(cuts[:-1], cuts[1:]))
            swaps = []
            for low, high in spans:
                for i, w in enumerate((wq, wk)):
                    swaps.append(
                        wire.start(
                            w.at[pl.ds(low, high - low), :],
                            w_far.at[pl.ds(i * cols + low, high - low), :],
                            to_far,
                        )
                    )
            up_swap = wire.start(wu_hbm, wu_sib, to_sib)
            down_swap = wire.start(wd_hbm, wd_sib, to_sib)
            scalars = (chip, core, *[lengths[i] for i in range(docs)])
            fill_bias(scalars, bias, seg, docs)
            for load in loads:
                load.wait()

            hat, _ = normalise(x_seg[...].astype(F32))
            normed = (hat * g1[...][None] + b1[...][None]).astype(BF16)
            n1[...] = normed
            qo[...] = mm(normed, wq[...], NT).astype(BF16)
            ko[...] = mm(normed, wk[...], NT).astype(BF16)
            value_cols = jnp.where(core == 0, wv[:, :cols], wv[:, cols : 2 * cols])
            fresh = mm(normed, value_cols).astype(BF16)
            reused = jnp.where(core == 0, fv_seg[:, :cols], fv_seg[:, cols : 2 * cols])
            vo[...] = jnp.where(chip == 0, fresh, reused)
            vf[...] = jnp.where(chip == 0, reused, fresh)
            for name in ((n1, n1_hbm), (qo, qo_hbm), (ko, ko_hbm), (vo, vo_hbm), (vf, vf_hbm)):
                store(*name)
            heads = list(enumerate(head_parts(cols)))
            attention_forward(bias, qo, ko, vo, mo, lo, seg, heads)
            store(mo, mo_hbm)
            store(lo, lo_hbm)
            out_swap = wire.start(wo, w_far.at[pl.ds(2 * cols, cols), :], to_far)
            for at, (low, high) in enumerate(spans):
                swaps[2 * at].wait_recv()
                swaps[2 * at + 1].wait_recv()
                normed = n1[...]
                qf[:, low:high] = mm(normed, w_far[low:high, :], NT).astype(BF16)
                kf[:, low:high] = mm(normed, w_far[cols + low : cols + high, :], NT).astype(BF16)
                here = [item for item in heads if item[1][0] == low]
                attention_forward(bias, qf, kf, vf, mf, lf, seg, here)
            store(qf, qf_hbm)
            store(kf, kf_hbm)
            store(mf, mf_hbm)
            store(lf, lf_hbm)
            out_swap.wait_recv()
            store(w_far, w_far_hbm)

            chunk = own // 2

            def out_part(start):
                span = rows_at(start, chunk)
                left = mm(mo[span, :], wo[...]).astype(BF16).astype(F32)
                right = mm(mf[span, :], w_far[2 * cols :, :]).astype(BF16).astype(F32)
                return (left + right).astype(BF16)

            att_swaps, n2_swaps = [], []
            for part in range(2):
                span = slice(part * chunk, (part + 1) * chunk)
                att_send[span, :] = out_part((1 - core) * own + part * chunk)
                place = pl.ds(part * chunk, chunk)
                att_swaps.append(
                    wire.start(att_send.at[place, :], att_recv.at[place, :], to_sib)
                )
            for part in range(2):
                span = slice(part * chunk, (part + 1) * chunk)
                kept = out_part(core * own + part * chunk)
                att_swaps[part].wait_recv()
                attention = kept.astype(F32) + att_recv[span, :].astype(F32)
                bo_part[span, :] = attention
                mine = rows_at(core * own + part * chunk, chunk)
                hidden = x_seg[mine, :].astype(F32) + attention
                hat, _ = normalise(hidden)
                n2[span, :] = (hat * g2[...][None] + b2[...][None]).astype(BF16)
                n2_swaps.append(
                    wire.start(
                        n2.at[pl.ds(part * chunk, chunk), :],
                        n2.at[pl.ds(own + part * chunk, chunk), :],
                        to_far,
                    )
                )
                through[span, :] = hidden
            up_swap.wait_recv()
            down_swap.wait_recv()
            for load in weight_loads:
                load.wait()

            def mlp(start, count):
                span = slice(start, start + count)
                step = min(hid, 256)
                for at, (up_w, down_w) in enumerate(((wu, wd), (wu_sib, wd_sib))):
                    for tile in range(hid // step):
                        part = slice(tile * step, (tile + 1) * step)
                        place = slice(at * hid + tile * step, at * hid + (tile + 1) * step)
                        up = mm(n2[span, :], up_w[:, part])
                        back = mm(og2[span, :], down_w[part, :], NT)
                        square = up * up
                        slope = jnp.tanh(GELU_C * up * (1.0 + GELU_A * square))
                        bell = 0.5 * (1.0 + slope)
                        act[span, place] = (up * bell).astype(BF16)
                        inner = GELU_C * (1.0 + 3.0 * GELU_A * square)
                        deriv = bell + 0.5 * up * (1.0 - slope * slope) * inner
                        dup[span, place] = (back * deriv).astype(BF16)
                total = mm(dup[span, :hid], wu[...], NT)
                return total + mm(dup[span, hid:], wu_sib[...], NT)

            def feed(start, count):
                span = slice(start, start + count)
                return mm(act[span, :hid], wd[...]) + mm(act[span, hid:], wd_sib[...])

            dn2_own[...] = mlp(0, own).astype(BF16)
            bo_part[...] += feed(0, own)
            store(bo_part, bo_part_hbm)
            dn2_swaps = []
            for part in range(2):
                n2_swaps[part].wait_recv()
                span = slice(part * chunk, (part + 1) * chunk)
                dn2_send[span, :] = mlp(own + part * chunk, chunk).astype(BF16)
                block = pl.ds(part * chunk, chunk)
                dn2_swaps.append(wire.start(dn2_send.at[block, :], dn2_recv.at[block, :], to_far))
            g_send[:hid, :] = mm(act[:, hid:], og2[...], TN).astype(BF16)
            down_sum = wire.start(
                g_send.at[pl.ds(0, hid), :], g_recv.at[pl.ds(0, hid), :], to_sib
            )
            down_own = mm(act[:, :hid], og2[...], TN)
            down_sum.wait_recv()
            w_grads[:hid, :] = (down_own + g_recv[:hid, :].astype(F32)).astype(BF16)
            g_send[hid:, :] = mm(n2[...], dup[:, hid:], TN).astype(BF16)
            up_sum = wire.start(
                g_send.at[pl.ds(hid, hid), :], g_recv.at[pl.ds(hid, hid), :], to_sib
            )
            feed_far[...] = feed(own, own).astype(BF16)
            store(feed_far, feed_far_hbm)
            up_own = mm(n2[...], dup[:, :hid], TN)
            up_sum.wait_recv()
            w_grads[hid:, :] = (up_own + g_recv[hid:, :].astype(F32)).astype(BF16)
            store(w_grads, w_grads_hbm)

            sums = []
            for part in range(2):
                block = slice(part * chunk, (part + 1) * chunk)
                dn2_swaps[part].wait_recv()
                d_norm = dn2_own[block, :].astype(F32) + dn2_recv[block, :].astype(F32)
                back, d_gain, d_bias = norm_backward(d_norm, through[block, :], g2[...][None])
                sums.append((d_gain, d_bias))
                through[block, :] = back
                da[block, :] = (og2[block, :].astype(F32) + back).astype(BF16)
                place = pl.ds(part * chunk, chunk)
                store(through.at[place, :], through_hbm.at[place, :])
                store(da.at[place, :], da_hbm.at[place, :])
            d_gain, d_bias = (first + second for first, second in zip(*sums))
            vec[...] = jnp.concatenate([d_gain, d_bias, jnp.zeros((6, width), F32)], axis=0)
            for moving in stores:
                moving.wait()
            wire.drain()

        def norm_backward(d_norm, values, gain):
            hat, inverse = normalise(values)
            d_gain = jnp.sum(d_norm * hat, axis=0, keepdims=True)
            d_bias = jnp.sum(d_norm, axis=0, keepdims=True)
            scaled = d_norm * gain
            mean1 = jnp.mean(scaled, axis=-1, keepdims=True)
            mean2 = jnp.mean(scaled * hat, axis=-1, keepdims=True)
            return (scaled - mean1 - hat * mean2) * inverse, d_gain, d_bias

        vm = pl.BlockSpec(memory_space=pltpu.VMEM)
        hbm = pl.BlockSpec(memory_space=pl.ANY)
        smem = pl.BlockSpec(memory_space=pltpu.SMEM)
        attn_flops = 2 * 2 * seg * seg * cols * 4
        query_rows, key_rows = query_weight.T, key_weight.T
        heads_of_shard = [*[sds((seg, cols), BF16)] * 4, sds((seg, 2 * HEAD), F32)]
        shard_scratch = [*[pltpu.VMEM((seg, cols), BF16)] * 4, pltpu.VMEM((seg, 2 * HEAD), F32)]
        n_head_copies = 20
        (
            n1,
            q_own,
            k_own,
            v_own,
            mixed_own,
            lse_own,
            q_far,
            k_far,
            v_far,
            mixed_far,
            lse_far,
            w_far,
            through,
            d_att,
            bo_part,
            feed_far,
            w_grads,
            vec2,
        ) = pl.pallas_call(
            head_kernel,
            name="head",
            out_shape=[
                sds((seg, width), BF16),
                *heads_of_shard,
                *heads_of_shard,
                sds((3 * cols, width), BF16),
                sds((own, width), F32),
                sds((own, width), BF16),
                sds((own, width), F32),
                sds((own, width), BF16),
                sds((2 * hid, width), BF16),
                sds((8, width), F32),
            ],
            in_specs=[smem, hbm, hbm, hbm, *[vm] * 8, hbm, hbm],
            out_specs=[*[hbm] * 17, vm],
            scratch_shapes=[
                pltpu.VMEM((seg, seg), F32),
                pltpu.VMEM((width, hid), BF16),
                pltpu.VMEM((hid, width), BF16),
                pltpu.VMEM((seg, width), BF16),
                *shard_scratch,
                *shard_scratch,
                pltpu.VMEM((3 * cols, width), BF16),
                pltpu.VMEM((own, width), F32),
                pltpu.VMEM((own, width), BF16),
                pltpu.VMEM((own, width), F32),
                pltpu.VMEM((own, width), BF16),
                pltpu.VMEM((2 * hid, width), BF16),
                pltpu.VMEM((seg, width), BF16),
                pltpu.VMEM((seg, half_width), BF16),
                pltpu.VMEM((2 * own, width), BF16),
                pltpu.VMEM((2 * own, width), BF16),
                pltpu.VMEM((2 * own, 2 * hid), BF16),
                pltpu.VMEM((2 * own, 2 * hid), BF16),
                pltpu.VMEM((width, hid), BF16),
                pltpu.VMEM((hid, width), BF16),
                *[pltpu.VMEM((own, width), BF16)] * 5,
                pltpu.VMEM((2 * hid, width), BF16),
                pltpu.VMEM((2 * hid, width), BF16),
                pltpu.SemaphoreType.DMA((n_head_copies,)),
                pltpu.SemaphoreType.DMA((n_head_copies,)),
                pltpu.SemaphoreType.DMA((6 + 19,)),
            ],
            cost_estimate=pl.CostEstimate(
                flops=attn_flops * 8, bytes_accessed=30000000, transcendentals=0
            ),
            compiler_params=pltpu.CompilerParams(
                collective_id=1, has_side_effects=True, vmem_limit_bytes=HEAD_VMEM
            ),
        )(
            doc_lengths[0],
            block_input,
            out_grad,
            first_values,
            norm1_gain,
            norm1_bias,
            norm2_gain,
            norm2_bias,
            query_rows,
            key_rows,
            out_weight,
            value_weight,
            up_weight,
            down_weight,
        )

        def attention_backward(bias, wo, mixed, lse, q, k, v, da, dm, dkt, dvt, dq, dk, dv, tick):
            dm[...] = mm(da[...], wo, NT).astype(BF16)
            dkt[...] = jnp.zeros_like(dkt)
            dvt[...] = jnp.zeros_like(dvt)
            lane = lax.broadcasted_iota(jnp.int32, (QROWS, 2 * HEAD), 1)
            for block in range(seg // QROWS):
                low, keys = block * QROWS, (block + 1) * QROWS
                held = None
                for head, (first, last, half) in enumerate(head_parts(cols)):
                    query = pick(q[low:keys, first:last], half) * jnp.asarray(SCALE, BF16)
                    grad = pick(dm[low:keys, first:last], half)
                    scores = mm(query, k[:keys, first:last], NT) + bias[low:keys, :keys]
                    weights = jnp.exp(scores - lse[low:keys, head : head + 1])
                    d_weights = mm(grad, v[:keys, first:last], NT)
                    inner = jnp.sum(
                        grad.astype(F32) * mixed[low:keys, first:last].astype(F32),
                        axis=-1,
                        keepdims=True,
                    )
                    d_scores = (weights * (d_weights - inner)).astype(BF16)
                    dvt[:keys, first:last] += mm(weights.astype(BF16), grad, TN)
                    dkt[:keys, first:last] += mm(d_scores, query, TN)
                    d_query = mm(d_scores, k[:keys, first:last]) * SCALE
                    tick(0.95)
                    if half == 0:
                        held = d_query
                    elif half == 1:
                        both = jnp.where(lane < HEAD, held, d_query)
                        dq[low:keys, first:last] = both.astype(BF16)
                    else:
                        dq[low:keys, first:last] = d_query.astype(BF16)
            dk[...] = dkt[...].astype(BF16)
            dv[...] = dvt[...].astype(BF16)

        def tail_kernel(
            lengths,
            x,
            og,
            through_hbm,
            da_own,
            bo_part_hbm,
            feed_far,
            vec2,
            g1,
            wq_hbm,
            wk_hbm,
            wo_hbm,
            w_far_hbm,
            wv_hbm,
            n1_hbm,
            w_grads,
            mo_hbm,
            lo_hbm,
            qo_hbm,
            ko_hbm,
            vo_hbm,
            mf_hbm,
            lf_hbm,
            qf_hbm,
            kf_hbm,
            vf_hbm,
            bo_all,
            ig_all,
            fv_out,
            total,
            w_total,
            value_out,
            vec,
            bias,
            through,
            bo_part,
            wq,
            wk,
            wo,
            w_far,
            wv,
            n1,
            mo,
            lo,
            qo,
            ko,
            vo,
            mf,
            lf,
            qf,
            kf,
            vf,
            x_here,
            og_here,
            fv_all,
            v_total,
            da,
            dm,
            dkt,
            dvt,
            dqo,
            dko,
            dvo,
            dqf,
            dkf,
            dvf,
            fresh,
            o_send,
            o_recv,
            g_send,
            g_recv,
            v_recv,
            dn_send,
            dn_recv,
            feed_recv,
            acc,
            landing,
            w_acc,
            w_landing,
            vec_send,
            vec_recv,
            send_sems,
            recv_sems,
            local_sems,
        ):
            me = lax.axis_index("mp")
            row = lax.axis_index("batch")
            sibling, core = flipped(me, 1)
            across, chip = flipped(me, 2)
            to_sib, to_far = {"mp": sibling}, {"mp": across}
            wire = Wire(send_sems, recv_sems)
            here = rows_at(me * own, own)
            there = rows_at(across * own, own)
            mine = rows_at(core * own, own)
            loads = {}

            def load(name, source, target):
                loads[name] = pltpu.make_async_copy(source, target, local_sems.at[len(loads)])
                loads[name].start()

            load("da", da_own, da.at[mine, :])
            load("w", w_grads, w_acc.at[pl.ds(0, 2 * hid), :])
            load("w_far", w_far_hbm, w_far)
            load("qf", qf_hbm, qf)
            load("kf", kf_hbm, kf)
            load("vf", vf_hbm, vf)
            load("mf", mf_hbm, mf)
            load("lf", lf_hbm, lf)
            load("n1", n1_hbm, n1)
            load("wo", wo_hbm, wo)
            load("qo", qo_hbm, qo)
            load("ko", ko_hbm, ko)
            load("vo", vo_hbm, vo)
            load("mo", mo_hbm, mo)
            load("lo", lo_hbm, lo)
            load("wq", wq_hbm, wq)
            load("wk", wk_hbm, wk)
            load("wv", wv_hbm, wv)
            load("through", through_hbm, through)
            load("bo_part", bo_part_hbm, bo_part)
            load("x", x.at[here, :], x_here)
            load("og", og.at[here, :], og_here)

            def loaded(*which):
                for name in which or tuple(loads):
                    loads.pop(name).wait()

            greet([to_sib, to_far, *[{"batch": flipped(row, bit)[0]} for bit in bits]])
            half_rows = [pl.ds(part * (own // 2), own // 2) for part in range(2)]
            feed_swaps = []

            def send_feed(part):
                block = half_rows[part]
                feed_swaps.append(
                    wire.start(feed_far.at[block, :], feed_recv.at[block, :], to_far)
                )

            send_feed(0)
            da_swap = wire.start(da_own, da.at[mine, :], to_sib)
            if w_rows > 2 * hid:
                w_acc[2 * hid :, :] = jnp.zeros((w_rows - 2 * hid, width), BF16)
            loaded("w")
            w_streams = [
                Reduction(
                    wire, row, ([bits[1], bits[0], *bits[2:]] if i == 0 else bits), w_acc, w_total, w_landing, i * w_stream, w_stream
                )
                for i in range(w_count)
            ]
            for one in w_streams:
                one.send_half(0)
            fill_bias((chip, core, *[lengths[i] for i in range(docs)]), bias, seg, docs)
            loaded("da", "w_far", "qf", "kf", "vf", "mf", "lf")
            da_swap.wait_recv()

            agenda = []
            last_step = len(bits) - 1

            def halve(one, step):
                one.add_half()
                if step < last_step:
                    one.send_half(step + 1)
                else:
                    one.turn()
                    one.send_whole()

            def double(one, step):
                one.take_whole()
                if step < last_step:
                    one.send_whole()

            def plan(due, action, *args):
                agenda.append((due, len(agenda), functools.partial(action, *args)))
                agenda.sort(key=lambda item: item[:2])

            for at, one in enumerate(w_streams):
                due = 12 if at == 0 else 6 + 7 * at
                for step in range(len(bits)):
                    plan(due, halve, one, step)
                    due += 16 if at == step == 0 else 6.5
                for step in range(len(bits)):
                    plan(due, double, one, step)
                    due += 7 if step < last_step - 1 else 10
            clock = [2.0]

            def tick(count):
                clock[0] += count
                while agenda and agenda[0][0] <= clock[0]:
                    agenda.pop(0)[2]()

            bo_near, bo_far, bo_diag = [], [], []

            def send_out(part):
                feed_swaps[part].wait_recv()
                block = slice(part * (own // 2), (part + 1) * (own // 2))
                out = bo_part[block, :] + feed_recv[block, :].astype(F32)
                out = out + x_here[block, :].astype(F32)
                place = rows_at(me * own + part * (own // 2), own // 2)
                bo_all[place, :] = out.astype(BF16)
                bo_near.append(wire.start(bo_all.at[place, :], bo_all.at[place, :], to_sib))
                bo_far.append(wire.start(bo_all.at[place, :], bo_all.at[place, :], to_far))

            def pass_out(part):
                bo_far[part].wait_recv()
                block = rows_at(across * own + part * (own // 2), own // 2)
                bo_diag.append(wire.start(bo_all.at[block, :], bo_all.at[block, :], to_sib))

            o_send[...] = mm(mf[...], da[...], TN).astype(BF16)
            o_swap = wire.start(o_send, o_recv, to_far)

            far_out = w_far[2 * cols :, :]
            attention_backward(
                bias, far_out, mf, lf, qf, kf, vf, da, dm, dkt, dvt, dqf, dkf, dvf, tick
            )
            loaded()
            g_send[:cols, :] = mm(dqf[...], n1[...], TN).astype(BF16)
            g_send[cols : 2 * cols, :] = mm(dkf[...], n1[...], TN).astype(BF16)
            g_swap = wire.start(g_send, g_recv, to_far)
            send_feed(1)
            tick(1.5)
            attention_backward(
                bias, wo[...], mo, lo, qo, ko, vo, da, dm, dkt, dvt, dqo, dko, dvo, tick
            )

            low_chip = chip == 0
            fresh[...] = jnp.where(low_chip, dvo[...], dvf[...])
            reused = jnp.where(low_chip, dvf[...], dvo[...])
            fv_all[pl.ds(me, 1)] = jnp.concatenate([reused[:own], reused[own:]], axis=1)[None]
            value_cols = jnp.where(core == 0, wv[:, :cols], wv[:, cols : 2 * cols])

            def dn1_part(start):
                span = rows_at(start, own)
                part = mm(dqo[span, :], wq[...])
                part = part + mm(dko[span, :], wk[...])
                part = part + mm(dqf[span, :], w_far[:cols, :])
                part = part + mm(dkf[span, :], w_far[cols : 2 * cols, :])
                return (part + mm(fresh[span, :], value_cols, NT)).astype(BF16)

            dn_send[...] = dn1_part((1 - core) * own)
            dn_swap = wire.start(dn_send, dn_recv, to_sib)
            tick(1.2)
            acc[3 * cols : 4 * cols, :] = mm(fresh[...], n1[...], TN).astype(BF16)
            kept = dn1_part(core * own).astype(F32)
            tick(1.5)
            dn_swap.wait_recv()
            d_norm = kept + dn_recv[...].astype(F32)
            back, d_gain1, d_bias1 = norm_backward(
                d_norm, x_here[...].astype(F32), g1[...][None]
            )
            ig_all[here, :] = (og_here[...].astype(F32) + back + through[...]).astype(BF16)
            ig_far = wire.start(ig_all.at[here, :], ig_all.at[here, :], to_far)
            ig_near = wire.start(ig_all.at[here, :], ig_all.at[here, :], to_sib)
            fv_mine, fv_there = fv_all.at[pl.ds(me, 1)], fv_all.at[pl.ds(across, 1)]
            fv_near = wire.start(fv_mine, fv_mine, to_sib)
            tick(1.5)

            acc[:cols, :] = mm(dqo[...], n1[...], TN).astype(BF16)
            acc[cols : 2 * cols, :] = mm(dko[...], n1[...], TN).astype(BF16)
            acc[2 * cols : 3 * cols, :] = mm(mo[...], da[...], TN).astype(BF16)
            if a_rows > 4 * cols:
                acc[4 * cols :, :] = jnp.zeros((a_rows - 4 * cols, width), BF16)
            tick(1.5)
            o_swap.wait_recv()
            o_rows = slice(2 * cols, 3 * cols)
            acc[o_rows, :] = (acc[o_rows, :].astype(F32) + o_recv[...].astype(F32)).astype(BF16)
            g_swap.wait_recv()
            shared = acc[: 2 * cols, :].astype(F32) + g_recv[...].astype(F32)
            acc[: 2 * cols, :] = shared.astype(BF16)

            ranks = [to_sib, to_far, *[{"batch": flipped(row, bit)[0]} for bit in bits]]
            vec_send[0] = jnp.concatenate(
                [d_gain1, d_bias1, vec2[:2, :], jnp.zeros((4, width), F32)], axis=0
            )
            streams = [
                Reduction(wire, row, bits, acc, total, landing, i * a_stream, a_stream)
                for i in range(a_count)
            ]

            def vector_step(at):
                if at < len(ranks):
                    return wire.start(vec_send.at[at], vec_recv.at[at], ranks[at])
                return None

            def vector_add(at, moving):
                if moving is not None:
                    moving.wait_recv()
                    vec_send[at + 1] = vec_send[at] + vec_recv[at]

            riding = []

            def start_vector(at):
                riding.append(vector_step(at))

            last = streams[-1]
            v_swaps, diag = [], {}

            def halve_all(step):
                for one in streams:
                    one.add_half()
                    if step < last_step:
                        one.send_half(step + 1)
                vector_add(step, riding[step])
                start_vector(step + 1)
                if step == last_step:
                    span = rows_at(last.start, last.size)
                    v_swaps.append(wire.start(acc.at[span, :], v_recv, to_far))
                    for one in streams[:-1]:
                        one.turn()
                        one.send_whole()
                    send_out(0)
                    send_first()
                    send_out(1)

            def merge_values():
                v_swaps[0].wait_recv()
                span = rows_at(last.start, last.size)
                at_row = last.start + lax.broadcasted_iota(jnp.int32, (last.size, 1), 0)
                is_value = (at_row >= 3 * cols) & (at_row < 4 * cols)
                other = jnp.where(is_value, v_recv[...].astype(F32), 0.0)
                total[span, :] = (acc[span, :].astype(F32) + other).astype(BF16)
                last.send_whole()

            def double_all(step):
                for one in streams:
                    one.take_whole()
                    if step < last_step:
                        one.send_whole()
                vector_add(len(bits) + step, riding[len(bits) + step])
                if step < last_step:
                    start_vector(len(bits) + step + 1)
                else:
                    v_rows = total.at[pl.ds(3 * cols, cols), :]
                    half = rows_at(core * cols, cols)
                    diag["v"] = wire.start(v_rows, v_total.at[half, :], to_sib)
                    v_total[half, :] = total[3 * cols : 4 * cols, :]

            def send_first():
                diag["fv far"] = wire.start(fv_mine, fv_mine, to_far)

            def pass_first():
                diag["fv far"].wait_recv()
                diag["fv"] = wire.start(fv_there, fv_there, to_sib)

            def pass_grad():
                ig_far.wait_recv()
                diag["ig"] = wire.start(ig_all.at[there, :], ig_all.at[there, :], to_sib)

            for one in streams:
                one.send_half(0)
            start_vector(0)
            turn = 46 + 5 * len(bits)
            for step in range(len(bits)):
                plan(46 + 5 * step, halve_all, step)
                plan(turn + 4 + 6 * step, double_all, step)
            plan(turn + 0.5, merge_values)
            plan(turn + 2, pass_grad)
            plan(turn + 17, pass_out, 0)
            plan(turn + 24, pass_first)
            plan(turn + 33, pass_out, 1)
            tick(10000)
            vec[...] = vec_send[len(ranks)]

            diag["v"].wait_recv()
            value_out[...] = v_total[...].astype(F32).T.astype(BF16)
            fv_near.wait_recv()
            diag["fv"].wait_recv()
            for part in range(rows // own):
                first = part // 2 * 2
                lanes = slice(part % 2 * cols, (part % 2 + 1) * cols)
                fv_out[part * own : (part + 1) * own, :] = jnp.concatenate(
                    [fv_all[first][:, lanes], fv_all[first + 1][:, lanes]], axis=1
                )
            for moving in (*bo_near, *bo_diag, ig_near, diag["ig"]):
                moving.wait_recv()
            wire.drain()

        tail_args = (
            doc_lengths[0],
            block_input,
            out_grad,
            through,
            d_att,
            bo_part,
            feed_far,
            vec2,
            norm1_gain,
            query_rows,
            key_rows,
            out_weight,
            w_far,
            value_weight,
            n1,
            w_grads,
            mixed_own,
            lse_own,
            q_own,
            k_own,
            v_own,
            mixed_far,
            lse_far,
            q_far,
            k_far,
            v_far,
        )
        bo_all, ig_all, fv_out, attn_sum, w_total, value_out, vectors = pl.pallas_call(
            tail_kernel,
            name="tail",
            out_shape=[
                pltpu.VMEM((rows, width), BF16),
                pltpu.VMEM((rows, width), BF16),
                pltpu.VMEM((rows, half_width), BF16),
                pltpu.VMEM((a_rows, width), BF16),
                pltpu.VMEM((w_rows, width), BF16),
                pltpu.VMEM((width, half_width), BF16),
                pltpu.VMEM((8, width), F32),
            ],
            in_specs=[smem, *[hbm] * 6, vm, vm, *[hbm] * 17],
            out_specs=[vm] * 7,
            scratch_shapes=[
                pltpu.VMEM((seg, seg), F32),
                pltpu.VMEM((own, width), F32),
                pltpu.VMEM((own, width), F32),
                pltpu.VMEM((cols, width), BF16),
                pltpu.VMEM((cols, width), BF16),
                pltpu.VMEM((cols, width), BF16),
                pltpu.VMEM((3 * cols, width), BF16),
                pltpu.VMEM((width, half_width), BF16),
                pltpu.VMEM((seg, width), BF16),
                pltpu.VMEM((seg, cols), BF16),
                pltpu.VMEM((seg, 2 * HEAD), F32),
                pltpu.VMEM((seg, cols), BF16),
                pltpu.VMEM((seg, cols), BF16),
                pltpu.VMEM((seg, cols), BF16),
                pltpu.VMEM((seg, cols), BF16),
                pltpu.VMEM((seg, 2 * HEAD), F32),
                pltpu.VMEM((seg, cols), BF16),
                pltpu.VMEM((seg, cols), BF16),
                pltpu.VMEM((seg, cols), BF16),
                pltpu.VMEM((own, width), BF16),
                pltpu.VMEM((own, width), BF16),
                pltpu.VMEM((4, own, 2 * cols), BF16),
                pltpu.VMEM((2 * cols, width), BF16),
                pltpu.VMEM((seg, width), BF16),
                pltpu.VMEM((seg, cols), BF16),
                pltpu.VMEM((seg, cols), F32),
                pltpu.VMEM((seg, cols), F32),
                *[pltpu.VMEM((seg, cols), BF16)] * 7,
                pltpu.VMEM((cols, width), BF16),
                pltpu.VMEM((cols, width), BF16),
                pltpu.VMEM((2 * cols, width), BF16),
                pltpu.VMEM((2 * cols, width), BF16),
                pltpu.VMEM((a_stream // batch_size, width), BF16),
                pltpu.VMEM((own, width), BF16),
                pltpu.VMEM((own, width), BF16),
                pltpu.VMEM((own, width), BF16),
                pltpu.VMEM((a_rows, width), BF16),
                pltpu.VMEM((a_rows, width), BF16),
                pltpu.VMEM((w_rows, width), BF16),
                pltpu.VMEM((w_rows, width), BF16),
                pltpu.VMEM((len(bits) + 3, 8, width), F32),
                pltpu.VMEM((len(bits) + 2, 8, width), F32),
                pltpu.SemaphoreType.DMA((n_copies,)),
                pltpu.SemaphoreType.DMA((n_copies,)),
                pltpu.SemaphoreType.DMA((22,)),
            ],
            cost_estimate=pl.CostEstimate(
                flops=attn_flops * 12, bytes_accessed=30000000, transcendentals=0
            ),
            compiler_params=pltpu.CompilerParams(
                collective_id=0, has_side_effects=True, vmem_limit_bytes=TAIL_VMEM
            ),
        )(*tail_args)
        block_out, input_grad = bo_all.astype(F32), ig_all.astype(F32)
        first_values_grad, value_grad = fv_out.astype(F32), value_out.astype(F32)
        query_grad = attn_sum[:cols].astype(F32).T
        key_grad = attn_sum[cols : 2 * cols].astype(F32).T
        out_sum = attn_sum[2 * cols : 3 * cols].astype(F32)
        down_grad, up_grad = w_total[:hid].astype(F32), w_total[hid : 2 * hid].astype(F32)
        return (
            block_out,
            input_grad,
            first_values_grad,
            vectors[0],
            vectors[1],
            query_grad,
            key_grad,
            value_grad,
            out_sum,
            vectors[2],
            vectors[3],
            up_grad,
            down_grad,
        )

    return jax.shard_map(
        shards,
        mesh=mesh,
        in_specs=(
            P("batch", None),
            P("batch", None),
            P(),
            P(),
            P(None, "mp"),
            P(None, "mp"),
            P(),
            P("mp", None),
            P(),
            P(),
            P(None, "mp"),
            P("mp", None),
            P("batch", None),
            P("batch", None),
        ),
        out_specs=(
            P("batch", None),
            P("batch", None),
            P("batch", None),
            P(),
            P(),
            P(None, "mp"),
            P(None, "mp"),
            P(),
            P("mp", None),
            P(),
            P(),
            P(None, "mp"),
            P("mp", None),
        ),
        check_vma=False,
    )
```
